128 devices in a mesh: wide: 32 (over y, x, core), samp: 4 (over z).
Axes of the slice: x: 4, y: 4, z: 4, core: 2. Of those that a mesh axis runs over, the one named last changes fastest.
Arguments:
- features: bfloat16 [4, 128, 96, 128], P('samp', 'wide'), may hold values from -6 to 6
- labels: int32 [4, 128, 96], P('samp', 'wide'), may hold values from 0 to 8
- conv_weight: bfloat16 [3, 3, 128, 128], replicated, may hold values from -0.1875 to 0.1875
- down_weight: bfloat16 [512, 1024], replicated, may hold values from -0.25 to 0.25
- expand_weight: bfloat16 [3, 3, 1024, 2048], P(None, None, None, 'wide'), may hold values from -0.0625 to 0.0625
- reduce_weight: bfloat16 [3, 3, 2048, 1024], P(None, None, 'wide'), may hold values from -0.046875 to 0.046875
- up_weight: bfloat16 [1024, 512], replicated, may hold values from -0.1875 to 0.1875
- class_weight: bfloat16 [128, 9], replicated, may hold values from -3 to 3
Outputs:
- conv_grad: float32 [3, 3, 128, 128], replicated
- down_grad: float32 [512, 1024], replicated
- expand_grad: float32 [3, 3, 1024, 2048], P(None, None, 'samp', 'wide')
- reduce_grad: float32 [3, 3, 2048, 1024], P(None, None, 'wide', 'samp')
- up_grad: float32 [1024, 512], replicated
- class_grad: float32 [128, 9], replicated
The draws below stay inside these ranges and needn't reach their ends.
All inputs are finite; a program needn't handle non-finite values.
Results may differ from the reference program's by a relative error of at most 0.012.
Values may be sent and summed in bfloat16 or wider, within the bound.
A program may use at most 192 MiB of HBM per device.

```python
import math
import jax
import jax.numpy as jnp
from jax import lax

C1 = 128
CB = 1024
CF = 2048
NCLS = 9
COLS = 96
H = 128
SAMPLES = 4
PIXELS = 49152


def place_ends(drawn, own_key, smallest, largest):
    longest = drawn.shape.index(max(drawn.shape))
    spots = []
    for shift in (0, 1):
        where = [jax.random.randint(jax.random.fold_in(own_key, axis), (), 0, length) for axis, length in enumerate(drawn.shape)]
        where[longest] = (where[longest] + shift) % drawn.shape[longest]
        spots.append(tuple(where))
    return drawn.at[spots[0]].set(smallest).at[spots[1]].set(largest)


def shard_levels(rng, extent, cuts, low, largest):
    level = 1.0
    for position, shards_of in cuts:
        draws = jax.random.uniform(jax.random.fold_in(jax.random.fold_in(rng, 6), position), (shards_of,), jnp.float32, low / len(cuts), largest / len(cuts))
        level = level * jnp.repeat(jnp.exp(draws), extent[position] // shards_of).reshape((-1,) + (1,) * (len(extent) - 1 - position))
    return level


def gaussian(key, dims, spread, bound, cuts=(), kind=jnp.bfloat16):
    level = shard_levels(key, dims, cuts, -0.22, 0.18) if cuts else 1.0
    drawn = jax.random.normal(key, dims, jnp.float32) * spread * level
    return jnp.minimum(jnp.maximum(drawn, -bound), bound).astype(kind)


def setup_inputs(seed: int = 0) -> dict:
    streams_of = jax.random.split(jax.random.key(seed), 9)
    return {
        "features": gaussian(streams_of[0], (SAMPLES, H, COLS, C1), 1.0, 6.0, ((0, 4), (1, 32))),
        "labels": place_ends(jax.random.randint(streams_of[1], (SAMPLES, H, COLS), 0, NCLS), jax.random.fold_in(streams_of[1], 1), 0, NCLS - 1).astype(jnp.int32),
        "conv_weight": gaussian(streams_of[2], (3, 3, C1, C1), (9 * C1) ** -0.5, 0.1875),
        "down_weight": gaussian(streams_of[3], (4 * C1, CB), (4 * C1) ** -0.5, 0.25),
        "expand_weight": gaussian(streams_of[4], (3, 3, CB, CF), (9 * CB) ** -0.5, 0.0625, ((3, 32),)),
        "reduce_weight": gaussian(streams_of[5], (3, 3, CF, CB), (9 * CF) ** -0.5, 0.046875, ((2, 32),)),
        "up_weight": gaussian(streams_of[6], (CB, 4 * C1), CB ** -0.5, 0.1875),
        "class_weight": gaussian(streams_of[7], (C1, NCLS), (max(C1 // 32, 1)) ** -0.5, 3.0),
    }


def silu_slope(value):
    logistic = jax.nn.sigmoid(value)
    return logistic * (1.0 + value * (1.0 - logistic))

def pad_both(values):
    return jnp.pad(values, ((1, 1), (1, 1), (0, 0)))

def to_depth(grid):
    height, across, channels = grid.shape
    blocks = grid.reshape(height // 2, 2, across // 2, 2, channels)
    return jnp.transpose(blocks, (0, 2, 1, 3, 4)).reshape(height // 2, across // 2, 4 * channels)

def from_depth(grid):
    height, across, channels = grid.shape
    blocks = grid.reshape(height, across, 2, 2, channels // 4)
    return jnp.transpose(blocks, (0, 2, 1, 3, 4)).reshape(2 * height, 2 * across, channels // 4)

def taps_in(padded, height, across):
    return jnp.concatenate([padded[p:p + height, q:q + across] for p in range(3) for q in range(3)], axis=-1)

def taps_out(values):
    return jnp.concatenate([jnp.pad(values, ((p, 2 - p), (q, 2 - q), (0, 0))) for p in range(3) for q in range(3)], axis=-1)

def conv_padded(padded, weight):
    height = padded.shape[0] - 2
    across = padded.shape[1] - 2
    inward = weight.shape[2]
    outward = weight.shape[3]
    if inward <= outward:
        window = taps_in(padded, height, across).reshape(height * across, 9 * inward)
        result = jnp.dot(window, weight.reshape(9 * inward, outward), preferred_element_type=jnp.float32)
        return result.reshape(height, across, outward)
    flattened = padded.reshape((height + 2) * (across + 2), inward)
    stacked = jnp.transpose(weight, (2, 0, 1, 3)).reshape(inward, 9 * outward)
    spread_out = jnp.dot(flattened, stacked, preferred_element_type=jnp.float32).reshape(height + 2, across + 2, 9, outward)
    summed = spread_out[0:height, 0:across, 0]
    for offset in range(1, 9):
        p = offset // 3
        q = offset % 3
        summed = summed + spread_out[p:p + height, q:q + across, offset]
    return summed

def correlate(padded, values):
    height, across, outward = values.shape
    inward = padded.shape[-1]
    if inward <= outward:
        window = taps_in(padded, height, across).reshape(height * across, 9 * inward)
        result = lax.dot_general(window, values.reshape(height * across, outward), (((0,), (0,)), ((), ())), preferred_element_type=jnp.float32)
        return result.reshape(3, 3, inward, outward)
    shifted = taps_out(values).reshape((height + 2) * (across + 2), 9 * outward)
    result = lax.dot_general(padded.reshape(-1, inward), shifted, (((0,), (0,)), ((), ())), preferred_element_type=jnp.float32)
    return jnp.transpose(result.reshape(inward, 3, 3, outward), (1, 2, 0, 3))

def contract_rows(left, right):
    left_flat = left.reshape(-1, left.shape[-1])
    right_flat = right.reshape(-1, right.shape[-1])
    return lax.dot_general(left_flat, right_flat, (((0,), (0,)), ((), ())), preferred_element_type=jnp.float32)

def flip_kernel(weight):
    return jnp.transpose(weight[::-1, ::-1], (0, 1, 3, 2))

def reference(features, labels, conv_weight, down_weight, expand_weight, reduce_weight, up_weight, class_weight):
    loss_scale = 8.0 / math.sqrt(PIXELS)
    classes = lax.broadcasted_iota(jnp.int32, (1, 1, NCLS), 2)
    back_reduce = flip_kernel(reduce_weight)
    back_expand = flip_kernel(expand_weight)
    conv_grad = jnp.zeros(conv_weight.shape, jnp.float32)
    down_grad = jnp.zeros(down_weight.shape, jnp.float32)
    expand_grad = jnp.zeros(expand_weight.shape, jnp.float32)
    reduce_grad = jnp.zeros(reduce_weight.shape, jnp.float32)
    up_grad = jnp.zeros(up_weight.shape, jnp.float32)
    class_grad = jnp.zeros(class_weight.shape, jnp.float32)
    for sample in range(SAMPLES):
        crop_rows = features[sample]
        label_map = labels[sample]
        padded_in = pad_both(crop_rows)
        hidden_pre = conv_padded(padded_in, conv_weight)
        hidden = jax.nn.silu(hidden_pre).astype(jnp.bfloat16)
        stacked = to_depth(hidden)
        coarse = jnp.dot(stacked, down_weight, preferred_element_type=jnp.float32).astype(jnp.bfloat16)
        coarse_pad = pad_both(coarse)
        expand_pre = conv_padded(coarse_pad, expand_weight)
        expanded = jax.nn.silu(expand_pre).astype(jnp.bfloat16)
        expand_pad = pad_both(expanded)
        bottom = (coarse.astype(jnp.float32) + conv_padded(expand_pad, reduce_weight)).astype(jnp.bfloat16)
        upward = from_depth(jnp.dot(bottom, up_weight, preferred_element_type=jnp.float32))
        joined_pre = upward + hidden.astype(jnp.float32)
        joined = jax.nn.silu(joined_pre).astype(jnp.bfloat16)
        logits = jnp.dot(joined, class_weight, preferred_element_type=jnp.float32)
        exp_logits = jnp.exp(logits)
        probability = exp_logits / lax.optimization_barrier(jnp.sum(exp_logits, axis=-1, keepdims=True))
        onehot = (label_map[:, :, None] == classes).astype(jnp.float32)
        logit_grad = ((probability - onehot) * loss_scale).astype(jnp.bfloat16)
        class_grad = class_grad + contract_rows(joined, logit_grad)
        joined_grad = lax.dot_general(logit_grad, class_weight, (((2,), (1,)), ((), ())), preferred_element_type=jnp.float32)
        upward_grad = (joined_grad * silu_slope(joined_pre)).astype(jnp.bfloat16)
        stacked_grad = to_depth(upward_grad)
        up_grad = up_grad + contract_rows(bottom, stacked_grad)
        bottom_grad = lax.dot_general(stacked_grad, up_weight, (((2,), (1,)), ((), ())), preferred_element_type=jnp.float32).astype(jnp.bfloat16)
        reduce_grad = reduce_grad + correlate(expand_pad, bottom_grad)
        expanded_back = conv_padded(pad_both(bottom_grad), back_reduce)
        expanded_grad = (expanded_back * silu_slope(expand_pre)).astype(jnp.bfloat16)
        expand_grad = expand_grad + correlate(coarse_pad, expanded_grad)
        coarse_back = conv_padded(pad_both(expanded_grad), back_expand)
        coarse_grad = (bottom_grad.astype(jnp.float32) + coarse_back).astype(jnp.bfloat16)
        down_grad = down_grad + contract_rows(stacked, coarse_grad)
        down_back = lax.dot_general(coarse_grad, down_weight, (((2,), (1,)), ((), ())), preferred_element_type=jnp.float32)
        hidden_sum = from_depth(down_back) + upward_grad.astype(jnp.float32)
        hidden_grad = (hidden_sum * silu_slope(hidden_pre)).astype(jnp.bfloat16)
        conv_grad = conv_grad + correlate(padded_in, hidden_grad)
    return (conv_grad, down_grad, expand_grad, reduce_grad, up_grad, class_grad)
```

```python
import functools
import math

import jax
import jax.numpy as jnp
from jax import lax
from jax.experimental import pallas as pl
from jax.experimental.pallas import tpu as pltpu
from jax.sharding import PartitionSpec as P


def split_up(x, dim, length):
    before, after = (x.shape[:dim], x.shape[dim + 1 :])
    return jnp.moveaxis(x.reshape(*before, length, -1, *after), dim, 0)


def sum_at_owner(x, axis, dim):
    length = lax.axis_size(axis)
    pieces = lax.all_to_all(split_up(x, dim, length), axis, 0, 0, tiled=True)
    return jnp.sum(pieces.astype(jnp.float32), axis=0)


def extended(block, sides, width):
    for axis, dim in sides:
        count = lax.axis_size(axis)
        forward = [(i, i + 1) for i in range(count - 1)]
        backward = [(target, source) for source, target in forward]
        low = lax.ppermute(
            lax.slice_in_dim(block, block.shape[dim] - width, None, axis=dim), axis, forward
        )
        high = lax.ppermute(lax.slice_in_dim(block, 0, width, axis=dim), axis, backward)
        block = jnp.concatenate([low, block, high], axis=dim)
    return block


def silu_slope(value):
    logistic = jax.nn.sigmoid(value)
    return logistic * (1.0 + value * (1.0 - logistic))


def pad_both(values):
    return jnp.pad(values, ((1, 1), (1, 1), (0, 0)))


def to_depth(grid):
    height, across, channels = grid.shape
    blocks = grid.reshape(height // 2, 2, across // 2, 2, channels)
    return jnp.transpose(blocks, (0, 2, 1, 3, 4)).reshape(height // 2, across // 2, 4 * channels)


def from_depth(grid):
    height, across, channels = grid.shape
    blocks = grid.reshape(height, across, 2, 2, channels // 4)
    return jnp.transpose(blocks, (0, 2, 1, 3, 4)).reshape(2 * height, 2 * across, channels // 4)


def taps_in(padded, height, across):
    return jnp.concatenate(
        [padded[p : p + height, q : q + across] for p in range(3) for q in range(3)], axis=-1
    )


def taps_out(values):
    return jnp.concatenate(
        [jnp.pad(values, ((p, 2 - p), (q, 2 - q), (0, 0))) for p in range(3) for q in range(3)],
        axis=-1,
    )


def conv_padded(padded, weight):
    height = padded.shape[0] - 2
    across = padded.shape[1] - 2
    inward = weight.shape[2]
    outward = weight.shape[3]
    if inward <= outward:
        window = taps_in(padded, height, across).reshape(height * across, 9 * inward)
        result = jnp.dot(
            window, weight.reshape(9 * inward, outward), preferred_element_type=jnp.float32
        )
        return result.reshape(height, across, outward)
    flattened = padded.reshape((height + 2) * (across + 2), inward)
    stacked = jnp.transpose(weight, (2, 0, 1, 3)).reshape(inward, 9 * outward)
    spread_out = jnp.dot(flattened, stacked, preferred_element_type=jnp.float32).reshape(
        height + 2, across + 2, 9, outward
    )
    summed = spread_out[0:height, 0:across, 0]
    for offset in range(1, 9):
        p = offset // 3
        q = offset % 3
        summed = summed + spread_out[p : p + height, q : q + across, offset]
    return summed


def correlate(padded, values):
    height, across, outward = values.shape
    inward = padded.shape[-1]
    if inward <= outward:
        window = taps_in(padded, height, across).reshape(height * across, 9 * inward)
        result = lax.dot_general(
            window,
            values.reshape(height * across, outward),
            (((0,), (0,)), ((), ())),
            preferred_element_type=jnp.float32,
        )
        return result.reshape(3, 3, inward, outward)
    shifted = taps_out(values).reshape((height + 2) * (across + 2), 9 * outward)
    result = lax.dot_general(
        padded.reshape(-1, inward),
        shifted,
        (((0,), (0,)), ((), ())),
        preferred_element_type=jnp.float32,
    )
    return jnp.transpose(result.reshape(inward, 3, 3, outward), (1, 2, 0, 3))


def contract_rows(left, right):
    left_flat = left.reshape(-1, left.shape[-1])
    right_flat = right.reshape(-1, right.shape[-1])
    return lax.dot_general(
        left_flat, right_flat, (((0,), (0,)), ((), ())), preferred_element_type=jnp.float32
    )


def flip_kernel(weight):
    return jnp.transpose(weight[::-1, ::-1], (0, 1, 3, 2))


def keep_rows(block_rows, first_row):
    return block_rows


def project_rows(values, weight):
    return jnp.dot(values, weight, preferred_element_type=jnp.float32).astype(jnp.bfloat16)


def widen_rows(values, weight):
    return lax.dot_general(
        values, weight, (((2,), (1,)), ((), ())), preferred_element_type=jnp.float32
    ).astype(jnp.bfloat16)


def collect(values, transform):
    return transform(lax.all_gather(values, "wide", axis=0, tiled=True), jnp.int32(0))


def spread_sum(term_rows, row_total):
    return sum_at_owner(
        term_rows(jnp.int32(0), row_total * lax.axis_size("wide")).astype(jnp.bfloat16), "wide", 0
    )


ROWS = 64
ACROSS = 48
SPOTS = ROWS * ACROSS
PIECE = 192
HALF = 96
PART = 512
INNER = 128
WIDE_ROWS = 3 * INNER


def place():
    wide = lax.axis_index("wide")
    core = wide % 2
    x = (wide // 2) % 4
    y = wide // 8
    first = x + core * (y - x)
    second = y + core * (x - y)
    return core, first % 4, second % 4


def block_of(core, first, second):
    x = first + core * (second - first)
    y = second + core * (first - second)
    return y * 4 + x


def rows_of(block, length=PIECE):
    return pl.ds(pl.multiple_of(block * PIECE, 64), length)


def edge_masks(length):
    column = lax.broadcasted_iota(jnp.int32, (length, INNER), 0) % ACROSS
    return column == 0, column == ACROSS - 1


def from_left(values, at_left):
    return jnp.where(at_left, 0.0, pltpu.roll(values, 1, axis=0))


def from_right(values, at_right):
    return jnp.where(at_right, 0.0, pltpu.roll(values, values.shape[0] - 1, axis=0))


class Copies:
    def __init__(self, send_sems, recv_sems):
        self.send_sems = send_sems
        self.recv_sems = recv_sems
        self.sent = []

    def remote(self, index, source, target, device):
        copy = pltpu.make_async_remote_copy(
            src_ref=source,
            dst_ref=target,
            send_sem=self.send_sems.at[index],
            recv_sem=self.recv_sems.at[index],
            device_id={"wide": device},
            device_id_type=pl.DeviceIdType.MESH,
        )
        return copy

    def start(self, index, source, target, device):
        copy = self.remote(index, source, target, device)
        copy.start()
        self.sent.append(copy)

    def arrived(self, index, target, device):
        self.remote(index, target, target, device).wait_recv()

    def finish(self):
        for copy in self.sent:
            copy.wait_send()


def phase_kernel(backward, *refs):
    if backward:
        (x_ref, wa_hbm, wb_hbm, pre_hbm, ef_hbm, xf_hbm, out_ref, ge_ref, gf_ref) = refs[:9]
        scratch = refs[9:]
    else:
        (x_ref, wa_hbm, wb_hbm, out_ref, pre_hbm, ef_hbm, xf_hbm) = refs[:7]
        scratch = refs[7:]
    (
        xall, wa, wb, total, pre, other, padded, chunk, window,
        far_out, up_out, down_out, far_in, up_in, down_in, reduced,
        far2_out, up2_out, down2_out, far2_in, up2_in, down2_in, swap_out, swap_in,
        send_sems, recv_sems, local_sems,
    ) = scratch[:27]
    core, first, second = place()
    me = block_of(core, first, second)
    partner = me * 2 + 1 - core
    f_up = block_of(core, (first + 1) % 4, second) * 2 + core
    f_down = block_of(core, (first + 3) % 4, second) * 2 + core
    s_up = block_of(core, first, (second + 1) % 4) * 2 + core
    s_down = block_of(core, first, (second + 3) % 4) * 2 + core
    copies = Copies(send_sems, recv_sems)

    loads = [
        pltpu.make_async_copy(wa_hbm, wa, local_sems.at[0]),
        pltpu.make_async_copy(wb_hbm, wb, local_sems.at[1]),
    ]
    if backward:
        pre_f, ef, xf, grad = scratch[27:]
        loads += [
            pltpu.make_async_copy(pre_hbm, pre_f, local_sems.at[2]),
            pltpu.make_async_copy(ef_hbm, ef, local_sems.at[3]),
            pltpu.make_async_copy(xf_hbm, xf, local_sems.at[4]),
        ]
    for load in loads:
        load.start()

    barrier = pltpu.get_barrier_semaphore()
    for device in (partner, f_up, f_down, s_up, s_down):
        pl.semaphore_signal(
            barrier, inc=1, device_id={"wide": device}, device_id_type=pl.DeviceIdType.MESH
        )
    pl.semaphore_wait(barrier, 5)

    mine = pl.ds(pl.multiple_of(me * PIECE + core * HALF, 32), HALF)
    theirs = pl.ds(pl.multiple_of(me * PIECE + (1 - core) * HALF, 32), HALF)
    copies.start(0, x_ref.at[1 - core], xall.at[mine, :], partner)
    xall[mine, :] = x_ref[core]
    copies.arrived(0, xall.at[theirs, :], partner)

    def piece(first_at, second_at, low=0, length=PIECE):
        block = block_of(core, first_at % 4, second_at % 4)
        return xall.at[pl.ds(pl.multiple_of(block * PIECE + low, 32), length), :]

    def send_second(order, first_at):
        copies.start(5 + order, piece(first_at, second), piece(first_at, second), s_up)
        copies.start(9 + order, piece(first_at, second), piece(first_at, second), s_down)

    own = piece(first, second)
    copies.start(1, own, own, f_up)
    copies.start(2, own, own, f_down)
    send_second(0, first)

    def clear(step, carry):
        total[pl.ds(pl.multiple_of(step * 96, 32), 96), :] = jnp.zeros((96, WIDE_ROWS), jnp.float32)
        return carry

    lax.fori_loop(0, 33, clear, 0)
    padded[0:ACROSS, :] = jnp.zeros((ACROSS, WIDE_ROWS), jnp.bfloat16)
    padded[SPOTS + ACROSS :, :] = jnp.zeros((ACROSS, WIDE_ROWS), jnp.bfloat16)

    left = piece(first + 3, second)
    right = piece(first + 1, second)
    copies.arrived(1, left, f_up)
    low = piece(first + 3, second, 0, HALF)
    copies.start(3, low, low, f_up)
    copies.arrived(2, right, f_down)
    high = piece(first + 1, second, HALF, HALF)
    copies.start(4, high, high, f_down)
    send_second(1, first + 3)
    send_second(2, first + 1)
    copies.arrived(3, piece(first + 2, second, 0, HALF), f_up)
    copies.arrived(4, piece(first + 2, second, HALF, HALF), f_down)
    send_second(3, first + 2)
    for load in loads:
        load.wait()

    offsets = (0, 3, 1, 2)

    def product(step, carry):
        @pl.when(step == 1)
        def _():
            for order in range(4):
                here = piece(first + offsets[order], second + 3)
                copies.arrived(5 + order, here, s_up)
                if order < 2:
                    copies.remote(13 + order, here, here, s_up).start()

        @pl.when(step == 2)
        def _():
            for order in range(4):
                here = piece(first + offsets[order], second + 1)
                copies.arrived(9 + order, here, s_down)
                if order >= 2:
                    copies.remote(13 + order, here, here, s_down).start()

        @pl.when(step == 3)
        def _():
            for order in range(4):
                here = piece(first + offsets[order], second + 2)
                copies.arrived(13 + order, here, s_up)

        turn = (3 * step + (step // 2) * (7 - 2 * step)) % 4
        row = (second + turn) % 4
        for position in range(4):
            block = block_of(core, position, row)
            chunk[position * PIECE : (position + 1) * PIECE, :] = xall[rows_of(block), :]
        result = jnp.dot(chunk[...], wa[...], preferred_element_type=jnp.float32)
        for position in range(4):
            block = block_of(core, position, row)
            for p in range(3):
                where = pl.ds(pl.multiple_of(block * PIECE + (2 - p) * ACROSS, 16), PIECE)
                total[where, :] += result[
                    position * PIECE : (position + 1) * PIECE, p * WIDE_ROWS : (p + 1) * WIDE_ROWS
                ]
        return carry

    lax.fori_loop(0, 4, product, 0)
    for order in range(4):
        here = piece(first + offsets[order], second + (3 if order < 2 else 1))
        copies.sent.append(copies.remote(13 + order, here, here, s_up))

    at_left, at_right = edge_masks(PIECE)

    def fold(step, carry):
        rows = rows_of(step)
        padded_rows = pl.ds(pl.multiple_of(step * PIECE + ACROSS, 16), PIECE)
        pre[rows, :] = (
            total[padded_rows, INNER : 2 * INNER]
            + from_left(total[padded_rows, 0:INNER], at_left)
            + from_right(total[padded_rows, 2 * INNER :], at_right)
        )
        return carry

    for quarter in range(4):
        lax.fori_loop(quarter * 4, quarter * 4 + 4, fold, 0)
        rows = pl.ds(quarter * 768, 768)
        copies.start(17 + quarter, pre.at[rows, :], other.at[rows, :], partner)

    def shape(step, carry):
        rows = rows_of(step)
        padded_rows = pl.ds(pl.multiple_of(step * PIECE + ACROSS, 16), PIECE)
        value = pre[rows, :] + other[rows, :]
        if backward:
            value = value * silu_slope(pre_f[rows, :])
        else:
            other[rows, :] = value
            value = jax.nn.silu(value)
        value = value.astype(jnp.bfloat16).astype(jnp.float32)
        padded[padded_rows, 0:INNER] = from_left(value, at_left).astype(jnp.bfloat16)
        padded[padded_rows, INNER : 2 * INNER] = value.astype(jnp.bfloat16)
        padded[padded_rows, 2 * INNER :] = from_right(value, at_right).astype(jnp.bfloat16)
        return carry

    for quarter in range(4):
        copies.arrived(17 + quarter, other.at[pl.ds(quarter * 768, 768), :], partner)
        lax.fori_loop(quarter * 4, quarter * 4 + 4, shape, 0)

    stores = []
    if not backward:
        stores = [
            pltpu.make_async_copy(other, pre_hbm, local_sems.at[2]),
            pltpu.make_async_copy(padded, ef_hbm, local_sems.at[3]),
            pltpu.make_async_copy(xall, xf_hbm, local_sems.at[4]),
        ]
        for store in stores:
            store.start()

    def gradients(left_ref, right_ref, out):
        def clear_grad(step, carry):
            grad[pl.ds(pl.multiple_of(step * 128, 128), 128), :] = jnp.zeros((128, PART), jnp.float32)
            return carry

        lax.fori_loop(0, 9, clear_grad, 0)

        def step_of(step, carry):
            p = step // 4
            part = step % 4
            window_rows = pl.ds(pl.multiple_of(part * 768 + p * ACROSS, 16), 768)
            value_rows = pl.ds(pl.multiple_of(part * 768, 256), 768)
            to = pl.ds(pl.multiple_of(p * WIDE_ROWS, 128), WIDE_ROWS)
            grad[to, :] += lax.dot_general(
                left_ref[window_rows, :],
                right_ref[value_rows, :],
                (((0,), (0,)), ((), ())),
                preferred_element_type=jnp.float32,
            )
            return carry

        lax.fori_loop(0, 12, step_of, 0)

        def cast(step, carry):
            rows = pl.ds(pl.multiple_of(step * 128, 128), 128)
            out[rows, :] = grad[rows, :].astype(jnp.bfloat16)
            return carry

        lax.fori_loop(0, 9, cast, 0)

    def narrow(values):
        return values.astype(jnp.bfloat16)

    def spread(step, carry):
        turn = (2 - step + (step // 2) * (7 - 2 * step)) % 4
        row = (second + turn) % 4
        for position in range(4):
            block = block_of(core, position, row)
            for p in range(3):
                window[
                    position * PIECE : (position + 1) * PIECE, p * WIDE_ROWS : (p + 1) * WIDE_ROWS
                ] = padded[pl.ds(pl.multiple_of(block * PIECE + p * ACROSS, 16), PIECE), :]
        result = jnp.dot(window[...], wb[...], preferred_element_type=jnp.float32)
        for position in range(4):
            reduced[position] = result[position * PIECE : (position + 1) * PIECE, :]

        @pl.when(step == 0)
        def _():
            for position in range(4):
                far_out[position] = narrow(reduced[position])
                copies.remote(
                    21 + position,
                    far_out.at[position],
                    far_in.at[position],
                    s_up if position < 2 else s_down,
                ).start()

        @pl.when(step == 1)
        def _():
            for position in (2, 3, 0, 1):
                value = reduced[position]
                if position < 2:
                    copies.arrived(21 + position, far_in.at[position], s_up)
                    value = value + far_in[position].astype(jnp.float32)
                up_out[position] = narrow(value)
                copies.remote(25 + position, up_out.at[position], up_in.at[position], s_up).start()

        @pl.when(step == 2)
        def _():
            for position in (0, 1, 2, 3):
                value = reduced[position]
                if position >= 2:
                    copies.arrived(21 + position, far_in.at[position], s_down)
                    value = value + far_in[position].astype(jnp.float32)
                down_out[position] = narrow(value)
                copies.remote(
                    29 + position, down_out.at[position], down_in.at[position], s_down
                ).start()
            if backward:
                gradients(ef, xall, ge_ref)
                gradients(padded, xf, gf_ref)

        return carry

    lax.fori_loop(0, 4, spread, 0)
    for position in range(4):
        copies.sent.append(
            copies.remote(21 + position, far_out.at[position], far_in.at[position], s_up)
        )
        copies.sent.append(
            copies.remote(25 + position, up_out.at[position], up_in.at[position], s_up)
        )
        copies.sent.append(
            copies.remote(29 + position, down_out.at[position], down_in.at[position], s_down)
        )
    for position in range(4):
        copies.arrived(25 + position, up_in.at[position], s_up)
        copies.arrived(29 + position, down_in.at[position], s_down)

    def gathered(at, low, length):
        rows = pl.ds(low, length)
        return (
            reduced[at, rows, :]
            + up_in[at, rows, :].astype(jnp.float32)
            + down_in[at, rows, :].astype(jnp.float32)
        )

    opposite = (first + 2) % 4
    far2_out[0] = narrow(gathered(opposite, 0, HALF))
    copies.start(33, far2_out.at[0], far2_in.at[0], f_up)
    far2_out[1] = narrow(gathered(opposite, HALF, HALF))
    copies.start(34, far2_out.at[1], far2_in.at[1], f_down)
    above = (first + 1) % 4
    below = (first + 3) % 4
    up2_out[HALF:, :] = narrow(gathered(above, HALF, HALF))
    down2_out[:HALF, :] = narrow(gathered(below, 0, HALF))
    copies.arrived(33, far2_in.at[0], f_up)
    up2_out[:HALF, :] = narrow(gathered(above, 0, HALF) + far2_in[0].astype(jnp.float32))
    copies.start(35, up2_out, up2_in, f_up)
    copies.arrived(34, far2_in.at[1], f_down)
    down2_out[HALF:, :] = narrow(gathered(below, HALF, HALF) + far2_in[1].astype(jnp.float32))
    copies.start(36, down2_out, down2_in, f_down)
    copies.arrived(35, up2_in, f_up)
    copies.arrived(36, down2_in, f_down)

    def settled(which):
        rows = pl.ds(pl.multiple_of(which * HALF, 32), HALF)
        return (
            reduced[first, rows, :]
            + up_in[first, rows, :].astype(jnp.float32)
            + down_in[first, rows, :].astype(jnp.float32)
            + up2_in[rows, :].astype(jnp.float32)
            + down2_in[rows, :].astype(jnp.float32)
        )

    swap_out[...] = narrow(settled(1 - core))
    copies.start(37, swap_out, swap_in, partner)
    out_ref[core] = narrow(x_ref[core].astype(jnp.float32) + settled(core))
    copies.arrived(37, swap_in, partner)
    out_ref[1 - core] = narrow(x_ref[1 - core].astype(jnp.float32) + swap_in[...].astype(jnp.float32))
    copies.finish()
    for store in stores:
        store.wait()


def bottleneck(values, wa, wb, saved=None):
    backward = saved is not None
    b16, f32 = jnp.bfloat16, jnp.float32
    vmem = pl.BlockSpec(memory_space=pltpu.VMEM)
    anywhere = pl.BlockSpec(memory_space=pl.ANY)
    padded_rows = SPOTS + 2 * ACROSS
    keep = [
        jax.ShapeDtypeStruct((SPOTS, INNER), f32),
        jax.ShapeDtypeStruct((padded_rows, WIDE_ROWS), b16),
        jax.ShapeDtypeStruct((SPOTS, PART), b16),
    ]
    out = jax.ShapeDtypeStruct((2, HALF, PART), b16)
    grad = jax.ShapeDtypeStruct((9 * INNER, PART), b16)
    scratch = [
        pltpu.VMEM((SPOTS, PART), b16),
        pltpu.VMEM((PART, 9 * INNER), b16),
        pltpu.VMEM((9 * INNER, PART), b16),
        pltpu.VMEM((padded_rows, WIDE_ROWS), f32),
        pltpu.VMEM((SPOTS, INNER), f32),
        pltpu.VMEM((SPOTS, INNER), f32),
        pltpu.VMEM((padded_rows, WIDE_ROWS), b16),
        pltpu.VMEM((4 * PIECE, PART), b16),
        pltpu.VMEM((4 * PIECE, 9 * INNER), b16),
        *[pltpu.VMEM((4, PIECE, PART), b16) for _ in range(6)],
        pltpu.VMEM((4, PIECE, PART), f32),
        pltpu.VMEM((2, HALF, PART), b16),
        pltpu.VMEM((PIECE, PART), b16),
        pltpu.VMEM((PIECE, PART), b16),
        pltpu.VMEM((2, HALF, PART), b16),
        pltpu.VMEM((PIECE, PART), b16),
        pltpu.VMEM((PIECE, PART), b16),
        pltpu.VMEM((HALF, PART), b16),
        pltpu.VMEM((HALF, PART), b16),
        pltpu.SemaphoreType.DMA((38,)),
        pltpu.SemaphoreType.DMA((38,)),
        pltpu.SemaphoreType.DMA((5,)),
    ]
    if backward:
        scratch += [
            pltpu.VMEM((SPOTS, INNER), f32),
            pltpu.VMEM((padded_rows, WIDE_ROWS), b16),
            pltpu.VMEM((SPOTS, PART), b16),
            pltpu.VMEM((9 * INNER, PART), f32),
        ]
    blocks = jnp.transpose(values.reshape(HALF, 2, PART), (1, 0, 2))
    results = pl.pallas_call(
        functools.partial(phase_kernel, backward),
        out_shape=[out, grad, grad] if backward else [out, *keep],
        in_specs=[vmem] + [anywhere] * (5 if backward else 2),
        out_specs=[vmem] * 3 if backward else [vmem] + [anywhere] * 3,
        scratch_shapes=scratch,
        compiler_params=pltpu.CompilerParams(
            collective_id=2 if backward else 1,
            has_side_effects=True,
            vmem_limit_bytes=60 * 1024 * 1024,
        ),
        name="backward_phase" if backward else "forward_phase",
    )(blocks, wa, wb, *(saved or ()))
    total = jnp.transpose(results[0], (1, 0, 2)).reshape(HALF, 2 * PART)
    return total, results[1:]


def swap_cores(values):
    count = lax.axis_size("wide")
    return lax.ppermute(values, "wide", [(i, i ^ 1) for i in range(count)])


def pair_part(values, dim, core):
    own = lax.dynamic_slice_in_dim(values, core * PART, PART, axis=dim)
    theirs = swap_cores(lax.dynamic_slice_in_dim(values, (1 - core) * PART, PART, axis=dim))
    return jnp.where(core == 0, own, theirs), jnp.where(core == 0, theirs, own)


def own_inner(grad, core):
    grad = grad.reshape(9, 2, INNER // 2, PART)
    own = lax.dynamic_index_in_dim(grad, core, axis=1, keepdims=False)
    theirs = swap_cores(lax.dynamic_index_in_dim(grad, 1 - core, axis=1, keepdims=False))
    low, high = jnp.where(core == 0, own, theirs), jnp.where(core == 0, theirs, own)
    return jnp.concatenate([low, high], axis=-1)


def local(
    features,
    labels,
    conv_weight,
    down_weight,
    expand_weight,
    reduce_weight,
    up_weight,
    class_weight,
):
    crop_rows = features[0]
    label_map = labels[0]
    height, across, channels = crop_rows.shape
    half_rows = height // 2
    half_across = across // 2
    core = lax.axis_index("wide") % 2
    pixel_count = lax.axis_size("wide") * lax.axis_size("samp") * height * across
    loss_scale = 8.0 / math.sqrt(pixel_count)
    classes = lax.broadcasted_iota(jnp.int32, (1, 1, class_weight.shape[1]), 2)

    expand_both = jnp.concatenate(
        pair_part(expand_weight.reshape(9, 2 * PART, INNER // 2), 1, core), axis=2
    )
    reduce_both = jnp.concatenate(
        pair_part(reduce_weight.reshape(9, INNER // 2, 2 * PART), 2, core), axis=1
    )
    wa_forward = jnp.transpose(expand_both, (1, 0, 2)).reshape(PART, 9 * INNER)
    wb_forward = reduce_both.reshape(9 * INNER, PART)
    wa_backward = jnp.transpose(reduce_both[::-1], (2, 0, 1)).reshape(PART, 9 * INNER)
    wb_backward = jnp.transpose(expand_both[::-1], (0, 2, 1)).reshape(9 * INNER, PART)

    near_rows = extended(crop_rows, (("wide", 0),), 1)
    padded_in = jnp.pad(near_rows, ((0, 0), (1, 1), (0, 0)))
    hidden_pre = conv_padded(padded_in, conv_weight)
    hidden = jax.nn.silu(hidden_pre).astype(jnp.bfloat16)
    stacked = to_depth(hidden)
    coarse = project_rows(stacked, down_weight)
    bottom, saved = bottleneck(coarse.reshape(-1, 2 * PART), wa_forward, wb_forward)
    bottom = bottom.reshape(half_rows, half_across, 2 * PART)
    upward = from_depth(jnp.dot(bottom, up_weight, preferred_element_type=jnp.float32))
    joined_pre = upward + hidden.astype(jnp.float32)
    joined = jax.nn.silu(joined_pre).astype(jnp.bfloat16)
    logits = jnp.dot(joined, class_weight, preferred_element_type=jnp.float32)
    exp_logits = jnp.exp(logits)
    probability = exp_logits / jnp.sum(exp_logits, axis=-1, keepdims=True)
    onehot = (label_map[:, :, None] == classes).astype(jnp.float32)
    logit_grad = ((probability - onehot) * loss_scale).astype(jnp.bfloat16)
    class_grad = contract_rows(joined, logit_grad)
    joined_grad = lax.dot_general(
        logit_grad, class_weight, (((2,), (1,)), ((), ())), preferred_element_type=jnp.float32
    )
    upward_grad = (joined_grad * silu_slope(joined_pre)).astype(jnp.bfloat16)
    stacked_grad = to_depth(upward_grad)
    up_grad = contract_rows(bottom, stacked_grad)
    bottom_grad = widen_rows(stacked_grad, up_weight)
    coarse_grad, (reduce_grad, expand_grad) = bottleneck(
        bottom_grad.reshape(-1, 2 * PART), wa_backward, wb_backward, saved
    )
    coarse_grad = coarse_grad.reshape(half_rows, half_across, 2 * PART)
    down_grad = contract_rows(stacked, coarse_grad)
    down_back = lax.dot_general(
        coarse_grad, down_weight, (((2,), (1,)), ((), ())), preferred_element_type=jnp.float32
    )
    hidden_sum = from_depth(down_back) + upward_grad.astype(jnp.float32)
    hidden_grad = (hidden_sum * silu_slope(hidden_pre)).astype(jnp.bfloat16)
    conv_grad = correlate(padded_in, hidden_grad)
    conv_grad, down_grad, up_grad, class_grad = lax.psum(
        (conv_grad, down_grad, up_grad, class_grad), ("wide", "samp")
    )
    reduce_grad = sum_at_owner(own_inner(reduce_grad, core), "samp", 2)
    expand_grad = sum_at_owner(own_inner(expand_grad, core)[::-1], "samp", 2)
    reduce_grad = reduce_grad.reshape(3, 3, INNER // 2, -1)
    expand_grad = jnp.transpose(expand_grad, (0, 2, 1)).reshape(3, 3, -1, INNER // 2)
    return (conv_grad, down_grad, expand_grad, reduce_grad, up_grad, class_grad)


def solution(mesh):
    return jax.shard_map(
        local,
        mesh=mesh,
        in_specs=(
            P("samp", "wide", None, None),
            P("samp", "wide", None),
            P(),
            P(),
            P(None, None, None, "wide"),
            P(None, None, "wide", None),
            P(),
            P(),
        ),
        out_specs=(
            P(),
            P(),
            P(None, None, "samp", "wide"),
            P(None, None, "wide", "samp"),
            P(),
            P(),
        ),
        check_vma=False,
    )
```

```python
import functools
import math

import jax
import jax.numpy as jnp
from jax import lax
from jax.experimental import pallas as pl
from jax.experimental.pallas import tpu as pltpu
from jax.sharding import PartitionSpec as P


def split_up(x, dim, length):
    before, after = (x.shape[:dim], x.shape[dim + 1 :])
    return jnp.moveaxis(x.reshape(*before, length, -1, *after), dim, 0)


def sum_at_owner(x, axis, dim):
    length = lax.axis_size(axis)
    pieces = lax.all_to_all(split_up(x, dim, length), axis, 0, 0, tiled=True)
    return jnp.sum(pieces.astype(jnp.float32), axis=0)


def extended(block, sides, width):
    for axis, dim in sides:
        count = lax.axis_size(axis)
        forward = [(i, i + 1) for i in range(count - 1)]
        backward = [(target, source) for source, target in forward]
        low = lax.ppermute(
            lax.slice_in_dim(block, block.shape[dim] - width, None, axis=dim), axis, forward
        )
        high = lax.ppermute(lax.slice_in_dim(block, 0, width, axis=dim), axis, backward)
        block = jnp.concatenate([low, block, high], axis=dim)
    return block


def silu_slope(value):
    logistic = jax.nn.sigmoid(value)
    return logistic * (1.0 + value * (1.0 - logistic))


def pad_both(values):
    return jnp.pad(values, ((1, 1), (1, 1), (0, 0)))


def to_depth(grid):
    height, across, channels = grid.shape
    blocks = grid.reshape(height // 2, 2, across // 2, 2, channels)
    return jnp.transpose(blocks, (0, 2, 1, 3, 4)).reshape(height // 2, across // 2, 4 * channels)


def from_depth(grid):
    height, across, channels = grid.shape
    blocks = grid.reshape(height, across, 2, 2, channels // 4)
    return jnp.transpose(blocks, (0, 2, 1, 3, 4)).reshape(2 * height, 2 * across, channels // 4)


def taps_in(padded, height, across):
    return jnp.concatenate(
        [padded[p : p + height, q : q + across] for p in range(3) for q in range(3)], axis=-1
    )


def taps_out(values):
    return jnp.concatenate(
        [jnp.pad(values, ((p, 2 - p), (q, 2 - q), (0, 0))) for p in range(3) for q in range(3)],
        axis=-1,
    )


def conv_padded(padded, weight):
    height = padded.shape[0] - 2
    across = padded.shape[1] - 2
    inward = weight.shape[2]
    outward = weight.shape[3]
    if inward <= outward:
        window = taps_in(padded, height, across).reshape(height * across, 9 * inward)
        result = jnp.dot(
            window, weight.reshape(9 * inward, outward), preferred_element_type=jnp.float32
        )
        return result.reshape(height, across, outward)
    flattened = padded.reshape((height + 2) * (across + 2), inward)
    stacked = jnp.transpose(weight, (2, 0, 1, 3)).reshape(inward, 9 * outward)
    spread_out = jnp.dot(flattened, stacked, preferred_element_type=jnp.float32).reshape(
        height + 2, across + 2, 9, outward
    )
    summed = spread_out[0:height, 0:across, 0]
    for offset in range(1, 9):
        p = offset // 3
        q = offset % 3
        summed = summed + spread_out[p : p + height, q : q + across, offset]
    return summed


def correlate(padded, values):
    height, across, outward = values.shape
    inward = padded.shape[-1]
    if inward <= outward:
        window = taps_in(padded, height, across).reshape(height * across, 9 * inward)
        result = lax.dot_general(
            window,
            values.reshape(height * across, outward),
            (((0,), (0,)), ((), ())),
            preferred_element_type=jnp.float32,
        )
        return result.reshape(3, 3, inward, outward)
    shifted = taps_out(values).reshape((height + 2) * (across + 2), 9 * outward)
    result = lax.dot_general(
        padded.reshape(-1, inward),
        shifted,
        (((0,), (0,)), ((), ())),
        preferred_element_type=jnp.float32,
    )
    return jnp.transpose(result.reshape(inward, 3, 3, outward), (1, 2, 0, 3))


def contract_rows(left, right):
    left_flat = left.reshape(-1, left.shape[-1])
    right_flat = right.reshape(-1, right.shape[-1])
    return lax.dot_general(
        left_flat, right_flat, (((0,), (0,)), ((), ())), preferred_element_type=jnp.float32
    )


def flip_kernel(weight):
    return jnp.transpose(weight[::-1, ::-1], (0, 1, 3, 2))


def keep_rows(block_rows, first_row):
    return block_rows


def project_rows(values, weight):
    return jnp.dot(values, weight, preferred_element_type=jnp.float32).astype(jnp.bfloat16)


def widen_rows(values, weight):
    return lax.dot_general(
        values, weight, (((2,), (1,)), ((), ())), preferred_element_type=jnp.float32
    ).astype(jnp.bfloat16)


def collect(values, transform):
    return transform(lax.all_gather(values, "wide", axis=0, tiled=True), jnp.int32(0))


def spread_sum(term_rows, row_total):
    return sum_at_owner(
        term_rows(jnp.int32(0), row_total * lax.axis_size("wide")).astype(jnp.bfloat16), "wide", 0
    )


ROWS = 64
ACROSS = 48
SPOTS = ROWS * ACROSS
PIECE = 192
HALF = 96
PART = 512
INNER = 128
WIDE_ROWS = 3 * INNER


def place():
    wide = lax.axis_index("wide")
    core = wide % 2
    x = (wide // 2) % 4
    y = wide // 8
    first = x + core * (y - x)
    second = y + core * (x - y)
    return core, first % 4, second % 4


def block_of(core, first, second):
    x = first + core * (second - first)
    y = second + core * (first - second)
    return y * 4 + x


def rows_of(block, length=PIECE):
    return pl.ds(pl.multiple_of(block * PIECE, 64), length)


def edge_masks(length):
    column = lax.broadcasted_iota(jnp.int32, (length, INNER), 0) % ACROSS
    return column == 0, column == ACROSS - 1


def from_left(values, at_left):
    return jnp.where(at_left, 0.0, pltpu.roll(values, 1, axis=0))


def from_right(values, at_right):
    return jnp.where(at_right, 0.0, pltpu.roll(values, values.shape[0] - 1, axis=0))


class Copies:
    def __init__(self, send_sems, recv_sems):
        self.send_sems = send_sems
        self.recv_sems = recv_sems
        self.sent = []

    def remote(self, index, source, target, device):
        copy = pltpu.make_async_remote_copy(
            src_ref=source,
            dst_ref=target,
            send_sem=self.send_sems.at[index],
            recv_sem=self.recv_sems.at[index],
            device_id=device if isinstance(device, dict) else {"wide": device},
            device_id_type=pl.DeviceIdType.MESH,
        )
        return copy

    def start(self, index, source, target, device):
        copy = self.remote(index, source, target, device)
        copy.start()
        self.sent.append(copy)

    def arrived(self, index, target, device):
        self.remote(index, target, target, device).wait_recv()

    def finish(self):
        for copy in self.sent:
            copy.wait_send()


def phase_kernel(backward, *refs):
    if backward:
        (x_ref, wa_hbm, wb_hbm, pre_hbm, ef_hbm, xf_hbm, out_ref, ge_ref, gf_ref) = refs[:9]
        scratch = refs[9:]
    else:
        (x_ref, wa_hbm, wb_hbm, out_ref, pre_hbm, ef_hbm, xf_hbm) = refs[:7]
        scratch = refs[7:]
    (
        xall, wa, wb, total, pre, other, padded, chunk, window,
        far_out, up_out, down_out, far_in, up_in, down_in, reduced,
        far2_out, up2_out, down2_out, far2_in, up2_in, down2_in, swap_out, swap_in,
        send_sems, recv_sems, local_sems,
    ) = scratch[:27]
    core, first, second = place()
    me = block_of(core, first, second)
    partner = me * 2 + 1 - core
    f_up = block_of(core, (first + 1) % 4, second) * 2 + core
    f_down = block_of(core, (first + 3) % 4, second) * 2 + core
    s_up = block_of(core, first, (second + 1) % 4) * 2 + core
    s_down = block_of(core, first, (second + 3) % 4) * 2 + core
    copies = Copies(send_sems, recv_sems)

    loads = [
        pltpu.make_async_copy(wa_hbm, wa, local_sems.at[0]),
        pltpu.make_async_copy(wb_hbm, wb, local_sems.at[1]),
    ]
    if backward:
        pre_f, ef, xf, grad, full, give, zfar_in, zup_out, zdown_out, zup_in, zdown_in = scratch[27:]
        loads += [
            pltpu.make_async_copy(pre_hbm, pre_f, local_sems.at[2]),
            pltpu.make_async_copy(ef_hbm, ef, local_sems.at[3]),
            pltpu.make_async_copy(xf_hbm, xf, local_sems.at[4]),
        ]
    for load in loads:
        load.start()

    peers = [{"wide": device} for device in (partner, f_up, f_down, s_up, s_down)]
    if backward:
        depth = lax.axis_index("samp")
        z_up = {"samp": (depth + 1) % 4}
        z_down = {"samp": (depth + 3) % 4}
        peers += [z_up, z_down]
    barrier = pltpu.get_barrier_semaphore()
    for device in peers:
        pl.semaphore_signal(
            barrier, inc=1, device_id=device, device_id_type=pl.DeviceIdType.MESH
        )
    pl.semaphore_wait(barrier, len(peers))

    mine = pl.ds(pl.multiple_of(me * PIECE + core * HALF, 32), HALF)
    theirs = pl.ds(pl.multiple_of(me * PIECE + (1 - core) * HALF, 32), HALF)
    copies.start(0, x_ref.at[1 - core], xall.at[mine, :], partner)
    xall[mine, :] = x_ref[core]
    copies.arrived(0, xall.at[theirs, :], partner)

    def piece(first_at, second_at, low=0, length=PIECE):
        block = block_of(core, first_at % 4, second_at % 4)
        return xall.at[pl.ds(pl.multiple_of(block * PIECE + low, 32), length), :]

    def send_second(order, first_at):
        copies.start(5 + order, piece(first_at, second), piece(first_at, second), s_up)
        copies.start(9 + order, piece(first_at, second), piece(first_at, second), s_down)

    own = piece(first, second)
    copies.start(1, own, own, f_up)
    copies.start(2, own, own, f_down)
    send_second(0, first)

    def clear(step, carry):
        total[pl.ds(pl.multiple_of(step * 96, 32), 96), :] = jnp.zeros((96, WIDE_ROWS), jnp.float32)
        return carry

    def clear_grad(step, carry):
        grad[pl.ds(pl.multiple_of(step * INNER, 128), INNER), :] = jnp.zeros((INNER, PART), jnp.float32)
        return carry

    def add_gradient():
        grad[...] += lax.dot_general(
            window[...], chunk[...], (((0,), (0,)), ((), ())), preferred_element_type=jnp.float32
        )

    def fill_window(source, row):
        for position in range(4):
            block = block_of(core, position, row)
            for p in range(3):
                window[
                    position * PIECE : (position + 1) * PIECE, p * WIDE_ROWS : (p + 1) * WIDE_ROWS
                ] = source[pl.ds(pl.multiple_of(block * PIECE + p * ACROSS, 16), PIECE), :]

    def fill_chunk(source, row):
        for position in range(4):
            block = block_of(core, position, row)
            chunk[position * PIECE : (position + 1) * PIECE, :] = source[rows_of(block), :]

    def hand_over(which):
        def pack(tap, carry):
            to = pl.ds(pl.multiple_of(tap * 64, 64), 64)
            own_rows = pl.ds(pl.multiple_of(tap * INNER + core * 64, 64), 64)
            other_rows = pl.ds(pl.multiple_of(tap * INNER + (1 - core) * 64, 64), 64)
            full[which, core, to, :] = grad[own_rows, :].astype(jnp.bfloat16)
            give[which, to, :] = grad[other_rows, :].astype(jnp.bfloat16)
            return carry

        lax.fori_loop(0, 9, pack, 0)
        copies.start(38 + which, give.at[which], full.at[which, core], partner)

    def share(which, at, low, length):
        at = at % 4
        lanes = pl.ds(pl.multiple_of((at % 2) * 256, 256), 256)
        return full.at[which, at // 2, pl.ds(low, length), lanes]

    def depth_far(which):
        copies.arrived(38 + which, full.at[which, 1 - core], partner)
        copies.start(40 + which, share(which, depth + 2, 0, 288), zfar_in.at[which, 0], z_up)
        copies.start(42 + which, share(which, depth + 2, 288, 288), zfar_in.at[which, 1], z_down)

    def depth_near(which):
        near = share(which, depth + 1, 288, 288)[...]
        zup_out[which, 288:576, :] = near
        near = share(which, depth + 3, 0, 288)[...]
        zdown_out[which, 0:288, :] = near
        copies.arrived(40 + which, zfar_in.at[which, 0], z_up)
        near = share(which, depth + 1, 0, 288)[...].astype(jnp.float32)
        zup_out[which, 0:288, :] = narrow(near + zfar_in[which, 0].astype(jnp.float32))
        copies.start(44 + which, zup_out.at[which], zup_in.at[which], z_up)
        copies.arrived(42 + which, zfar_in.at[which, 1], z_down)
        near = share(which, depth + 3, 288, 288)[...].astype(jnp.float32)
        zdown_out[which, 288:576, :] = narrow(near + zfar_in[which, 1].astype(jnp.float32))
        copies.start(46 + which, zdown_out.at[which], zdown_in.at[which], z_down)

    def depth_own(which, out):
        copies.arrived(44 + which, zup_in.at[which], z_up)
        copies.arrived(46 + which, zdown_in.at[which], z_down)
        out[...] = (
            share(which, depth, 0, 576)[...].astype(jnp.float32)
            + zup_in[which].astype(jnp.float32)
            + zdown_in[which].astype(jnp.float32)
        )

    def narrow(values):
        return values.astype(jnp.bfloat16)

    lax.fori_loop(0, 33, clear, 0)
    if backward:
        lax.fori_loop(0, 9, clear_grad, 0)
    padded[0:ACROSS, :] = jnp.zeros((ACROSS, WIDE_ROWS), jnp.bfloat16)
    padded[SPOTS + ACROSS :, :] = jnp.zeros((ACROSS, WIDE_ROWS), jnp.bfloat16)

    left = piece(first + 3, second)
    right = piece(first + 1, second)
    copies.arrived(1, left, f_up)
    low = piece(first + 3, second, 0, HALF)
    copies.start(3, low, low, f_up)
    copies.arrived(2, right, f_down)
    high = piece(first + 1, second, HALF, HALF)
    copies.start(4, high, high, f_down)
    send_second(1, first + 3)
    send_second(2, first + 1)
    copies.arrived(3, piece(first + 2, second, 0, HALF), f_up)
    copies.arrived(4, piece(first + 2, second, HALF, HALF), f_down)
    send_second(3, first + 2)
    for load in loads:
        load.wait()

    offsets = (0, 3, 1, 2)

    def product(step, carry):
        @pl.when(step == 1)
        def _():
            for order in range(4):
                here = piece(first + offsets[order], second + 3)
                copies.arrived(5 + order, here, s_up)
                if order < 2:
                    copies.remote(13 + order, here, here, s_up).start()

        @pl.when(step == 2)
        def _():
            for order in range(4):
                here = piece(first + offsets[order], second + 1)
                copies.arrived(9 + order, here, s_down)
                if order >= 2:
                    copies.remote(13 + order, here, here, s_down).start()

        @pl.when(step == 3)
        def _():
            for order in range(4):
                here = piece(first + offsets[order], second + 2)
                copies.arrived(13 + order, here, s_up)

        turn = (3 * step + (step // 2) * (7 - 2 * step)) % 4
        row = (second + turn) % 4
        fill_chunk(xall, row)
        result = jnp.dot(chunk[...], wa[...], preferred_element_type=jnp.float32)
        for position in range(4):
            block = block_of(core, position, row)
            for p in range(3):
                where = pl.ds(pl.multiple_of(block * PIECE + (2 - p) * ACROSS, 16), PIECE)
                total[where, :] += result[
                    position * PIECE : (position + 1) * PIECE, p * WIDE_ROWS : (p + 1) * WIDE_ROWS
                ]
        if backward:
            fill_window(ef, row)
            add_gradient()
        return carry

    lax.fori_loop(0, 4, product, 0)
    for order in range(4):
        here = piece(first + offsets[order], second + (3 if order < 2 else 1))
        copies.sent.append(copies.remote(13 + order, here, here, s_up))

    at_left, at_right = edge_masks(PIECE)

    def fold(step, carry):
        rows = rows_of(step)
        padded_rows = pl.ds(pl.multiple_of(step * PIECE + ACROSS, 16), PIECE)
        pre[rows, :] = (
            total[padded_rows, INNER : 2 * INNER]
            + from_left(total[padded_rows, 0:INNER], at_left)
            + from_right(total[padded_rows, 2 * INNER :], at_right)
        )
        return carry

    for quarter in range(4):
        lax.fori_loop(quarter * 4, quarter * 4 + 4, fold, 0)
        rows = pl.ds(quarter * 768, 768)
        copies.start(17 + quarter, pre.at[rows, :], other.at[rows, :], partner)

    if backward:
        hand_over(0)
        lax.fori_loop(0, 9, clear_grad, 0)

    def shape(step, carry):
        rows = rows_of(step)
        padded_rows = pl.ds(pl.multiple_of(step * PIECE + ACROSS, 16), PIECE)
        value = pre[rows, :] + other[rows, :]
        if backward:
            value = value * silu_slope(pre_f[rows, :])
        else:
            other[rows, :] = value
            value = jax.nn.silu(value)
        value = value.astype(jnp.bfloat16).astype(jnp.float32)
        padded[padded_rows, 0:INNER] = from_left(value, at_left).astype(jnp.bfloat16)
        padded[padded_rows, INNER : 2 * INNER] = value.astype(jnp.bfloat16)
        padded[padded_rows, 2 * INNER :] = from_right(value, at_right).astype(jnp.bfloat16)
        return carry

    for quarter in range(4):
        copies.arrived(17 + quarter, other.at[pl.ds(quarter * 768, 768), :], partner)
        lax.fori_loop(quarter * 4, quarter * 4 + 4, shape, 0)

    stores = []
    if not backward:
        stores = [
            pltpu.make_async_copy(other, pre_hbm, local_sems.at[2]),
            pltpu.make_async_copy(padded, ef_hbm, local_sems.at[3]),
            pltpu.make_async_copy(xall, xf_hbm, local_sems.at[4]),
        ]
        for store in stores:
            store.start()

    if backward:
        depth_far(0)

    def spread(step, carry):
        turn = (2 - step + (step // 2) * (7 - 2 * step)) % 4
        row = (second + turn) % 4
        fill_window(padded, row)
        result = jnp.dot(window[...], wb[...], preferred_element_type=jnp.float32)
        for position in range(4):
            reduced[position] = result[position * PIECE : (position + 1) * PIECE, :]

        @pl.when(step == 0)
        def _():
            for position in range(4):
                far_out[position] = narrow(reduced[position])
                copies.remote(
                    21 + position,
                    far_out.at[position],
                    far_in.at[position],
                    s_up if position < 2 else s_down,
                ).start()

        @pl.when(step == 1)
        def _():
            for position in (2, 3, 0, 1):
                value = reduced[position]
                if position < 2:
                    copies.arrived(21 + position, far_in.at[position], s_up)
                    value = value + far_in[position].astype(jnp.float32)
                up_out[position] = narrow(value)
                copies.remote(25 + position, up_out.at[position], up_in.at[position], s_up).start()

        @pl.when(step == 2)
        def _():
            for position in (0, 1, 2, 3):
                value = reduced[position]
                if position >= 2:
                    copies.arrived(21 + position, far_in.at[position], s_down)
                    value = value + far_in[position].astype(jnp.float32)
                down_out[position] = narrow(value)
                copies.remote(
                    29 + position, down_out.at[position], down_in.at[position], s_down
                ).start()

        if backward:
            fill_chunk(xf, row)
            add_gradient()
        return carry

    lax.fori_loop(0, 4, spread, 0)
    if backward:
        hand_over(1)
        depth_near(0)
        depth_far(1)
    for position in range(4):
        copies.sent.append(
            copies.remote(21 + position, far_out.at[position], far_in.at[position], s_up)
        )
        copies.sent.append(
            copies.remote(25 + position, up_out.at[position], up_in.at[position], s_up)
        )
        copies.sent.append(
            copies.remote(29 + position, down_out.at[position], down_in.at[position], s_down)
        )
    for position in range(4):
        copies.arrived(25 + position, up_in.at[position], s_up)
        copies.arrived(29 + position, down_in.at[position], s_down)

    def gathered(at, low, length):
        rows = pl.ds(low, length)
        return (
            reduced[at, rows, :]
            + up_in[at, rows, :].astype(jnp.float32)
            + down_in[at, rows, :].astype(jnp.float32)
        )

    opposite = (first + 2) % 4
    far2_out[0] = narrow(gathered(opposite, 0, HALF))
    copies.start(33, far2_out.at[0], far2_in.at[0], f_up)
    far2_out[1] = narrow(gathered(opposite, HALF, HALF))
    copies.start(34, far2_out.at[1], far2_in.at[1], f_down)
    above = (first + 1) % 4
    below = (first + 3) % 4
    up2_out[HALF:, :] = narrow(gathered(above, HALF, HALF))
    down2_out[:HALF, :] = narrow(gathered(below, 0, HALF))
    copies.arrived(33, far2_in.at[0], f_up)
    up2_out[:HALF, :] = narrow(gathered(above, 0, HALF) + far2_in[0].astype(jnp.float32))
    copies.start(35, up2_out, up2_in, f_up)
    copies.arrived(34, far2_in.at[1], f_down)
    down2_out[HALF:, :] = narrow(gathered(below, HALF, HALF) + far2_in[1].astype(jnp.float32))
    copies.start(36, down2_out, down2_in, f_down)
    copies.arrived(35, up2_in, f_up)
    copies.arrived(36, down2_in, f_down)

    def settled(which):
        rows = pl.ds(pl.multiple_of(which * HALF, 32), HALF)
        return (
            reduced[first, rows, :]
            + up_in[first, rows, :].astype(jnp.float32)
            + down_in[first, rows, :].astype(jnp.float32)
            + up2_in[rows, :].astype(jnp.float32)
            + down2_in[rows, :].astype(jnp.float32)
        )

    if backward:
        depth_near(1)
    swap_out[...] = narrow(settled(1 - core))
    copies.start(37, swap_out, swap_in, partner)
    out_ref[core] = narrow(x_ref[core].astype(jnp.float32) + settled(core))
    copies.arrived(37, swap_in, partner)
    out_ref[1 - core] = narrow(x_ref[1 - core].astype(jnp.float32) + swap_in[...].astype(jnp.float32))
    if backward:
        depth_own(0, ge_ref)
        depth_own(1, gf_ref)
    copies.finish()
    for store in stores:
        store.wait()


def bottleneck(values, wa, wb, saved=None):
    backward = saved is not None
    b16, f32 = jnp.bfloat16, jnp.float32
    vmem = pl.BlockSpec(memory_space=pltpu.VMEM)
    anywhere = pl.BlockSpec(memory_space=pl.ANY)
    padded_rows = SPOTS + 2 * ACROSS
    keep = [
        jax.ShapeDtypeStruct((SPOTS, INNER), f32),
        jax.ShapeDtypeStruct((padded_rows, WIDE_ROWS), b16),
        jax.ShapeDtypeStruct((SPOTS, PART), b16),
    ]
    out = jax.ShapeDtypeStruct((2, HALF, PART), b16)
    grad = jax.ShapeDtypeStruct((9 * INNER // 2, PART // 2), f32)
    scratch = [
        pltpu.VMEM((SPOTS, PART), b16),
        pltpu.VMEM((PART, 9 * INNER), b16),
        pltpu.VMEM((9 * INNER, PART), b16),
        pltpu.VMEM((padded_rows, WIDE_ROWS), f32),
        pltpu.VMEM((SPOTS, INNER), f32),
        pltpu.VMEM((SPOTS, INNER), f32),
        pltpu.VMEM((padded_rows, WIDE_ROWS), b16),
        pltpu.VMEM((4 * PIECE, PART), b16),
        pltpu.VMEM((4 * PIECE, 9 * INNER), b16),
        *[pltpu.VMEM((4, PIECE, PART), b16) for _ in range(6)],
        pltpu.VMEM((4, PIECE, PART), f32),
        pltpu.VMEM((2, HALF, PART), b16),
        pltpu.VMEM((PIECE, PART), b16),
        pltpu.VMEM((PIECE, PART), b16),
        pltpu.VMEM((2, HALF, PART), b16),
        pltpu.VMEM((PIECE, PART), b16),
        pltpu.VMEM((PIECE, PART), b16),
        pltpu.VMEM((HALF, PART), b16),
        pltpu.VMEM((HALF, PART), b16),
        pltpu.SemaphoreType.DMA((48,)),
        pltpu.SemaphoreType.DMA((48,)),
        pltpu.SemaphoreType.DMA((5,)),
    ]
    if backward:
        scratch += [
            pltpu.VMEM((SPOTS, INNER), f32),
            pltpu.VMEM((padded_rows, WIDE_ROWS), b16),
            pltpu.VMEM((SPOTS, PART), b16),
            pltpu.VMEM((9 * INNER, PART), f32),
            pltpu.VMEM((2, 2, 576, PART), b16),
            pltpu.VMEM((2, 576, PART), b16),
            pltpu.VMEM((2, 2, 288, 256), b16),
            *[pltpu.VMEM((2, 576, 256), b16) for _ in range(4)],
        ]
    blocks = jnp.transpose(values.reshape(HALF, 2, PART), (1, 0, 2))
    results = pl.pallas_call(
        functools.partial(phase_kernel, backward),
        out_shape=[out, grad, grad] if backward else [out, *keep],
        in_specs=[vmem] + [anywhere] * (5 if backward else 2),
        out_specs=[vmem] * 3 if backward else [vmem] + [anywhere] * 3,
        scratch_shapes=scratch,
        compiler_params=pltpu.CompilerParams(
            collective_id=2 if backward else 1,
            has_side_effects=True,
            vmem_limit_bytes=60 * 1024 * 1024,
        ),
        name="backward_phase" if backward else "forward_phase",
    )(blocks, wa, wb, *(saved or ()))
    total = jnp.transpose(results[0], (1, 0, 2)).reshape(HALF, 2 * PART)
    return total, results[1:]


def swap_cores(values):
    count = lax.axis_size("wide")
    return lax.ppermute(values, "wide", [(i, i ^ 1) for i in range(count)])


def pair_part(values, dim, core):
    own = lax.dynamic_slice_in_dim(values, core * PART, PART, axis=dim)
    theirs = swap_cores(lax.dynamic_slice_in_dim(values, (1 - core) * PART, PART, axis=dim))
    return jnp.where(core == 0, own, theirs), jnp.where(core == 0, theirs, own)


SUM_ROWS = 1280


def sum_kernel(down_ref, up_ref, conv_ref, class_ref, out_ref, total, give, pair_in, a_out, a_in,
               b_out, b_in, z_out, z_in, result, send_sems, recv_sems):
    core, first, second = place()
    depth = lax.axis_index("samp")
    me = block_of(core, first, second)
    partner = {"wide": me * 2 + 1 - core}
    first_peers = [
        {"wide": block_of(core, (first + d) % 4, second) * 2 + core} for d in range(4)
    ]
    second_peers = [
        {"wide": block_of(core, first, (second + d) % 4) * 2 + core} for d in range(4)
    ]
    depth_peers = [{"samp": (depth + d) % 4} for d in range(4)]
    copies = Copies(send_sems, recv_sems)
    barrier = pltpu.get_barrier_semaphore()
    for device in [partner, *first_peers[1:], *second_peers[1:], *depth_peers[1:]]:
        pl.semaphore_signal(
            barrier, inc=1, device_id=device, device_id_type=pl.DeviceIdType.MESH
        )
    pl.semaphore_wait(barrier, 10)

    def own_lanes(half, width):
        return pl.ds(pl.multiple_of(half * width, 128), width)

    def pack(half, to, kind):
        to[0:512, :] = down_ref[:, own_lanes(half, 512)].astype(kind)
        to[512:1024, :] = up_ref[pl.ds(pl.multiple_of(half * 512, 512), 512), :].astype(kind)
        for piece in range(4):
            rows = pl.ds(pl.multiple_of((half * 4 + piece) * 144, 16), 144)
            to[1024:1168, piece * 128 : (piece + 1) * 128] = conv_ref[rows, :].astype(kind)
        to[1168:1184, :] = class_ref[:, own_lanes(half, 512)].astype(kind)
        to[1184:, :] = jnp.zeros((SUM_ROWS - 1184, PART), kind)

    def rows320(at):
        return pl.ds(pl.multiple_of((at % 4) * 320, 64), 320)

    pack(1 - core, give, jnp.bfloat16)
    for d in range(4):
        part = rows320(second + (d + 1))
        copies.start(d, give.at[part, :], pair_in.at[part, :], partner)
    pack(core, total, jnp.float32)
    for d in range(1, 4):
        part = rows320(first + d)
        copies.arrived(d - 1, pair_in.at[rows320(first + d), :], partner)
        a_out[d] = (total[part, :] + pair_in[part, :].astype(jnp.float32)).astype(jnp.bfloat16)
        copies.start(3 + d, a_out.at[d], a_in.at[d], first_peers[d])
    copies.arrived(3, pair_in.at[rows320(first), :], partner)
    for d in range(1, 4):
        copies.arrived(3 + d, a_in.at[d], first_peers[d])

    def after_first(at):
        base = first * 320 + at * 80
        rows = pl.ds(pl.multiple_of(base, 16), 80)
        inner = pl.ds(pl.multiple_of(at * 80, 16), 80)
        value = total[rows, :] + pair_in[rows, :].astype(jnp.float32)
        for d in range(1, 4):
            value = value + a_in[d, inner, :].astype(jnp.float32)
        return value

    for d in range(1, 4):
        b_out[d] = after_first((second + d) % 4).astype(jnp.bfloat16)
        copies.start(6 + d, b_out.at[d], b_in.at[d], second_peers[d])
    total[0:80, :] = after_first(second)
    for d in range(1, 4):
        copies.arrived(6 + d, b_in.at[d], second_peers[d])
        total[0:80, :] += b_in[d].astype(jnp.float32)
    for d in range(1, 4):
        z_out[d] = total[0:80, own_lanes((depth + d) % 4, 128)].astype(jnp.bfloat16)
        copies.start(9 + d, z_out.at[d], z_in.at[d], depth_peers[d])
    value = total[0:80, own_lanes(depth, 128)]
    for d in range(1, 4):
        copies.arrived(9 + d, z_in.at[d], depth_peers[d])
        value = value + z_in[d].astype(jnp.float32)

    def at_depth(d):
        base = first * 320 + second * 80
        return result.at[
            core, pl.ds(pl.multiple_of(base, 16), 80), own_lanes((depth + d) % 4, 128)
        ]

    def at_second(d):
        base = first * 320 + ((second + d) % 4) * 80
        return result.at[core, pl.ds(pl.multiple_of(base, 16), 80), :]

    def at_first(d, half):
        return result.at[half, rows320(first + d), :]

    at_depth(0)[...] = value.astype(jnp.bfloat16)
    for d in range(1, 4):
        copies.start(12 + d, at_depth(0), at_depth(0), depth_peers[d])
    for d in range(1, 4):
        copies.arrived(12 + d, at_depth(4 - d), depth_peers[d])
    for d in range(1, 4):
        copies.start(15 + d, at_second(0), at_second(0), second_peers[d])
    for d in range(1, 4):
        copies.arrived(15 + d, at_second(4 - d), second_peers[d])
    for d in range(1, 4):
        copies.start(18 + d, at_first(0, core), at_first(0, core), first_peers[d])
    copies.start(22, at_first(0, core), at_first(0, core), partner)
    for d in range(1, 4):
        copies.arrived(18 + d, at_first(4 - d, core), first_peers[d])
        copies.start(22 + d, at_first(4 - d, core), at_first(4 - d, core), partner)
    out_ref[core] = result[core]
    copies.arrived(22, at_first(0, 1 - core), partner)
    for d in range(1, 4):
        copies.arrived(22 + d, at_first(4 - d, 1 - core), partner)
    out_ref[1 - core] = result[1 - core]
    copies.finish()


def sum_everywhere(conv_grad, down_grad, up_grad, class_grad):
    b16, f32 = jnp.bfloat16, jnp.float32
    vmem = pl.BlockSpec(memory_space=pltpu.VMEM)
    classes = class_grad.shape[1]
    small = jnp.pad(class_grad.T, ((0, 16 - classes), (0, 2 * PART - INNER)))
    out = pl.pallas_call(
        sum_kernel,
        out_shape=jax.ShapeDtypeStruct((2, SUM_ROWS, PART), b16),
        in_specs=[vmem] * 4,
        out_specs=vmem,
        scratch_shapes=[
            pltpu.VMEM((SUM_ROWS, PART), f32),
            pltpu.VMEM((SUM_ROWS, PART), b16),
            pltpu.VMEM((SUM_ROWS, PART), b16),
            pltpu.VMEM((4, 320, PART), b16),
            pltpu.VMEM((4, 320, PART), b16),
            pltpu.VMEM((4, 80, PART), b16),
            pltpu.VMEM((4, 80, PART), b16),
            pltpu.VMEM((4, 80, 128), b16),
            pltpu.VMEM((4, 80, 128), b16),
            pltpu.VMEM((2, SUM_ROWS, PART), b16),
            pltpu.SemaphoreType.DMA((26,)),
            pltpu.SemaphoreType.DMA((26,)),
        ],
        compiler_params=pltpu.CompilerParams(
            collective_id=3, has_side_effects=True, vmem_limit_bytes=60 * 1024 * 1024
        ),
        name="sum_everywhere",
    )(down_grad, up_grad, conv_grad.reshape(9 * INNER, INNER), small)
    down = jnp.concatenate([out[0, 0:512], out[1, 0:512]], axis=1).astype(f32)
    up = out[:, 512:1024].astype(f32).reshape(2 * PART, PART)
    conv = jnp.concatenate(
        [out[h, 1024:1168, i * 128 : (i + 1) * 128] for h in range(2) for i in range(4)], axis=0
    )
    conv = conv.astype(f32).reshape(conv_grad.shape)
    return conv, down, up, out[0, 1168 : 1168 + classes, 0:INNER].astype(f32).T


def local(
    features,
    labels,
    conv_weight,
    down_weight,
    expand_weight,
    reduce_weight,
    up_weight,
    class_weight,
):
    crop_rows = features[0]
    label_map = labels[0]
    height, across, channels = crop_rows.shape
    half_rows = height // 2
    half_across = across // 2
    core = lax.axis_index("wide") % 2
    pixel_count = lax.axis_size("wide") * lax.axis_size("samp") * height * across
    loss_scale = 8.0 / math.sqrt(pixel_count)
    classes = lax.broadcasted_iota(jnp.int32, (1, 1, class_weight.shape[1]), 2)

    expand_both = jnp.concatenate(
        pair_part(expand_weight.reshape(9, 2 * PART, INNER // 2), 1, core), axis=2
    )
    reduce_both = jnp.concatenate(
        pair_part(reduce_weight.reshape(9, INNER // 2, 2 * PART), 2, core), axis=1
    )
    wa_forward = jnp.transpose(expand_both, (1, 0, 2)).reshape(PART, 9 * INNER)
    wb_forward = reduce_both.reshape(9 * INNER, PART)
    wa_backward = jnp.transpose(reduce_both[::-1], (2, 0, 1)).reshape(PART, 9 * INNER)
    wb_backward = jnp.transpose(expand_both[::-1], (0, 2, 1)).reshape(9 * INNER, PART)

    near_rows = extended(crop_rows, (("wide", 0),), 1)
    padded_in = jnp.pad(near_rows, ((0, 0), (1, 1), (0, 0)))
    hidden_pre = conv_padded(padded_in, conv_weight)
    hidden = jax.nn.silu(hidden_pre).astype(jnp.bfloat16)
    stacked = to_depth(hidden)
    coarse = project_rows(stacked, down_weight)
    bottom, saved = bottleneck(coarse.reshape(-1, 2 * PART), wa_forward, wb_forward)
    bottom = bottom.reshape(half_rows, half_across, 2 * PART)
    upward = from_depth(jnp.dot(bottom, up_weight, preferred_element_type=jnp.float32))
    joined_pre = upward + hidden.astype(jnp.float32)
    joined = jax.nn.silu(joined_pre).astype(jnp.bfloat16)
    logits = jnp.dot(joined, class_weight, preferred_element_type=jnp.float32)
    exp_logits = jnp.exp(logits)
    probability = exp_logits / jnp.sum(exp_logits, axis=-1, keepdims=True)
    onehot = (label_map[:, :, None] == classes).astype(jnp.float32)
    logit_grad = ((probability - onehot) * loss_scale).astype(jnp.bfloat16)
    class_grad = contract_rows(joined, logit_grad)
    joined_grad = lax.dot_general(
        logit_grad, class_weight, (((2,), (1,)), ((), ())), preferred_element_type=jnp.float32
    )
    upward_grad = (joined_grad * silu_slope(joined_pre)).astype(jnp.bfloat16)
    stacked_grad = to_depth(upward_grad)
    up_grad = contract_rows(bottom, stacked_grad)
    bottom_grad = widen_rows(stacked_grad, up_weight)
    coarse_grad, (reduce_grad, expand_grad) = bottleneck(
        bottom_grad.reshape(-1, 2 * PART), wa_backward, wb_backward, saved
    )
    coarse_grad = coarse_grad.reshape(half_rows, half_across, 2 * PART)
    down_grad = contract_rows(stacked, coarse_grad)
    down_back = lax.dot_general(
        coarse_grad, down_weight, (((2,), (1,)), ((), ())), preferred_element_type=jnp.float32
    )
    hidden_sum = from_depth(down_back) + upward_grad.astype(jnp.float32)
    hidden_grad = (hidden_sum * silu_slope(hidden_pre)).astype(jnp.bfloat16)
    conv_grad = correlate(padded_in, hidden_grad)
    conv_grad, down_grad, up_grad, class_grad = sum_everywhere(
        conv_grad, down_grad, up_grad, class_grad
    )
    reduce_grad = reduce_grad.reshape(3, 3, INNER // 2, -1)
    expand_grad = jnp.transpose(expand_grad.reshape(9, INNER // 2, -1)[::-1], (0, 2, 1))
    expand_grad = expand_grad.reshape(3, 3, -1, INNER // 2)
    return (conv_grad, down_grad, expand_grad, reduce_grad, up_grad, class_grad)


def solution(mesh):
    return jax.shard_map(
        local,
        mesh=mesh,
        in_specs=(
            P("samp", "wide", None, None),
            P("samp", "wide", None),
            P(),
            P(),
            P(None, None, None, "wide"),
            P(None, None, "wide", None),
            P(),
            P(),
        ),
        out_specs=(
            P(),
            P(),
            P(None, None, "samp", "wide"),
            P(None, None, "wide", "samp"),
            P(),
            P(),
        ),
        check_vma=False,
    )
```

```python
import functools
import math

import jax
import jax.numpy as jnp
from jax import lax
from jax.experimental import pallas as pl
from jax.experimental.pallas import tpu as pltpu
from jax.sharding import PartitionSpec as P


def split_up(x, dim, length):
    before, after = (x.shape[:dim], x.shape[dim + 1 :])
    return jnp.moveaxis(x.reshape(*before, length, -1, *after), dim, 0)


def sum_at_owner(x, axis, dim):
    length = lax.axis_size(axis)
    pieces = lax.all_to_all(split_up(x, dim, length), axis, 0, 0, tiled=True)
    return jnp.sum(pieces.astype(jnp.float32), axis=0)


def extended(block, sides, width):
    for axis, dim in sides:
        count = lax.axis_size(axis)
        forward = [(i, i + 1) for i in range(count - 1)]
        backward = [(target, source) for source, target in forward]
        low = lax.ppermute(
            lax.slice_in_dim(block, block.shape[dim] - width, None, axis=dim), axis, forward
        )
        high = lax.ppermute(lax.slice_in_dim(block, 0, width, axis=dim), axis, backward)
        block = jnp.concatenate([low, block, high], axis=dim)
    return block


def silu_slope(value):
    logistic = jax.nn.sigmoid(value)
    return logistic * (1.0 + value * (1.0 - logistic))


def pad_both(values):
    return jnp.pad(values, ((1, 1), (1, 1), (0, 0)))


def to_depth(grid):
    height, across, channels = grid.shape
    blocks = grid.reshape(height // 2, 2, across // 2, 2, channels)
    return jnp.transpose(blocks, (0, 2, 1, 3, 4)).reshape(height // 2, across // 2, 4 * channels)


def from_depth(grid):
    height, across, channels = grid.shape
    blocks = grid.reshape(height, across, 2, 2, channels // 4)
    return jnp.transpose(blocks, (0, 2, 1, 3, 4)).reshape(2 * height, 2 * across, channels // 4)


def taps_in(padded, height, across):
    return jnp.concatenate(
        [padded[p : p + height, q : q + across] for p in range(3) for q in range(3)], axis=-1
    )


def taps_out(values):
    return jnp.concatenate(
        [jnp.pad(values, ((p, 2 - p), (q, 2 - q), (0, 0))) for p in range(3) for q in range(3)],
        axis=-1,
    )


def conv_padded(padded, weight):
    height = padded.shape[0] - 2
    across = padded.shape[1] - 2
    inward = weight.shape[2]
    outward = weight.shape[3]
    if inward <= outward:
        window = taps_in(padded, height, across).reshape(height * across, 9 * inward)
        result = jnp.dot(
            window, weight.reshape(9 * inward, outward), preferred_element_type=jnp.float32
        )
        return result.reshape(height, across, outward)
    flattened = padded.reshape((height + 2) * (across + 2), inward)
    stacked = jnp.transpose(weight, (2, 0, 1, 3)).reshape(inward, 9 * outward)
    spread_out = jnp.dot(flattened, stacked, preferred_element_type=jnp.float32).reshape(
        height + 2, across + 2, 9, outward
    )
    summed = spread_out[0:height, 0:across, 0]
    for offset in range(1, 9):
        p = offset // 3
        q = offset % 3
        summed = summed + spread_out[p : p + height, q : q + across, offset]
    return summed


def correlate(padded, values):
    height, across, outward = values.shape
    inward = padded.shape[-1]
    if inward <= outward:
        window = taps_in(padded, height, across).reshape(height * across, 9 * inward)
        result = lax.dot_general(
            window,
            values.reshape(height * across, outward),
            (((0,), (0,)), ((), ())),
            preferred_element_type=jnp.float32,
        )
        return result.reshape(3, 3, inward, outward)
    shifted = taps_out(values).reshape((height + 2) * (across + 2), 9 * outward)
    result = lax.dot_general(
        padded.reshape(-1, inward),
        shifted,
        (((0,), (0,)), ((), ())),
        preferred_element_type=jnp.float32,
    )
    return jnp.transpose(result.reshape(inward, 3, 3, outward), (1, 2, 0, 3))


def contract_rows(left, right):
    left_flat = left.reshape(-1, left.shape[-1])
    right_flat = right.reshape(-1, right.shape[-1])
    return lax.dot_general(
        left_flat, right_flat, (((0,), (0,)), ((), ())), preferred_element_type=jnp.float32
    )


def flip_kernel(weight):
    return jnp.transpose(weight[::-1, ::-1], (0, 1, 3, 2))


def keep_rows(block_rows, first_row):
    return block_rows


def project_rows(values, weight):
    return jnp.dot(values, weight, preferred_element_type=jnp.float32).astype(jnp.bfloat16)


def widen_rows(values, weight):
    return lax.dot_general(
        values, weight, (((2,), (1,)), ((), ())), preferred_element_type=jnp.float32
    ).astype(jnp.bfloat16)


def collect(values, transform):
    return transform(lax.all_gather(values, "wide", axis=0, tiled=True), jnp.int32(0))


def spread_sum(term_rows, row_total):
    return sum_at_owner(
        term_rows(jnp.int32(0), row_total * lax.axis_size("wide")).astype(jnp.bfloat16), "wide", 0
    )


ROWS = 64
ACROSS = 48
SPOTS = ROWS * ACROSS
PIECE = 192
HALF = 96
PART = 512
INNER = 128
WIDE_ROWS = 3 * INNER


def place():
    wide = lax.axis_index("wide")
    core = wide % 2
    x = (wide // 2) % 4
    y = wide // 8
    first = x + core * (y - x)
    second = y + core * (x - y)
    return core, first % 4, second % 4


def block_of(core, first, second):
    x = first + core * (second - first)
    y = second + core * (first - second)
    return y * 4 + x


def rows_of(block, length=PIECE):
    return pl.ds(pl.multiple_of(block * PIECE, 64), length)


def edge_masks(length):
    column = lax.broadcasted_iota(jnp.int32, (length, INNER), 0) % ACROSS
    return column == 0, column == ACROSS - 1


def from_left(values, at_left):
    return jnp.where(at_left, 0.0, pltpu.roll(values, 1, axis=0))


def from_right(values, at_right):
    return jnp.where(at_right, 0.0, pltpu.roll(values, values.shape[0] - 1, axis=0))


class Copies:
    def __init__(self, send_sems, recv_sems):
        self.send_sems = send_sems
        self.recv_sems = recv_sems
        self.sent = []

    def remote(self, index, source, target, device):
        copy = pltpu.make_async_remote_copy(
            src_ref=source,
            dst_ref=target,
            send_sem=self.send_sems.at[index],
            recv_sem=self.recv_sems.at[index],
            device_id=device if isinstance(device, dict) else {"wide": device},
            device_id_type=pl.DeviceIdType.MESH,
        )
        return copy

    def start(self, index, source, target, device):
        copy = self.remote(index, source, target, device)
        copy.start()
        self.sent.append(copy)

    def arrived(self, index, target, device):
        self.remote(index, target, target, device).wait_recv()

    def finish(self):
        for copy in self.sent:
            copy.wait_send()


def phase_kernel(backward, *refs):
    if backward:
        (x_ref, wa_hbm, wb_hbm, pre_hbm, ef_hbm, xf_hbm, out_ref, ge_ref, gf_ref) = refs[:9]
        scratch = refs[9:]
    else:
        (x_ref, wa_hbm, wb_hbm, out_ref, pre_hbm, ef_hbm, xf_hbm) = refs[:7]
        scratch = refs[7:]
    (
        xall, wa, wb, total, pre, other, padded, chunk, window,
        far_out, up_out, down_out, far_in, up_in, down_in, reduced,
        far2_out, up2_out, down2_out, far2_in, up2_in, down2_in, swap_out, swap_in,
        send_sems, recv_sems, local_sems,
    ) = scratch[:27]
    core, first, second = place()
    me = block_of(core, first, second)
    partner = me * 2 + 1 - core
    f_up = block_of(core, (first + 1) % 4, second) * 2 + core
    f_down = block_of(core, (first + 3) % 4, second) * 2 + core
    s_up = block_of(core, first, (second + 1) % 4) * 2 + core
    s_down = block_of(core, first, (second + 3) % 4) * 2 + core
    copies = Copies(send_sems, recv_sems)

    loads = [
        pltpu.make_async_copy(wa_hbm, wa, local_sems.at[0]),
        pltpu.make_async_copy(wb_hbm, wb, local_sems.at[1]),
    ]
    if backward:
        pre_f, ef, xf, grad, full, give, zfar_in, zup_out, zdown_out, zup_in, zdown_in = scratch[27:]
        loads += [
            pltpu.make_async_copy(pre_hbm, pre_f, local_sems.at[2]),
            pltpu.make_async_copy(ef_hbm, ef, local_sems.at[3]),
            pltpu.make_async_copy(xf_hbm, xf, local_sems.at[4]),
        ]
    for load in loads:
        load.start()

    peers = [{"wide": device} for device in (partner, f_up, f_down, s_up, s_down)]
    if backward:
        depth = lax.axis_index("samp")
        z_up = {"samp": (depth + 1) % 4}
        z_down = {"samp": (depth + 3) % 4}
        peers += [z_up, z_down]
    barrier = pltpu.get_barrier_semaphore()
    for device in peers:
        pl.semaphore_signal(
            barrier, inc=1, device_id=device, device_id_type=pl.DeviceIdType.MESH
        )
    pl.semaphore_wait(barrier, len(peers))

    mine = pl.ds(pl.multiple_of(me * PIECE + core * HALF, 32), HALF)
    theirs = pl.ds(pl.multiple_of(me * PIECE + (1 - core) * HALF, 32), HALF)
    copies.start(0, x_ref.at[1 - core], xall.at[mine, :], partner)
    xall[mine, :] = x_ref[core]
    copies.arrived(0, xall.at[theirs, :], partner)

    def piece(first_at, second_at, low=0, length=PIECE):
        block = block_of(core, first_at % 4, second_at % 4)
        return xall.at[pl.ds(pl.multiple_of(block * PIECE + low, 32), length), :]

    def send_second(order, first_at):
        copies.start(5 + order, piece(first_at, second), piece(first_at, second), s_up)
        copies.start(9 + order, piece(first_at, second), piece(first_at, second), s_down)

    own = piece(first, second)
    copies.start(1, own, own, f_up)
    copies.start(2, own, own, f_down)
    send_second(0, first)

    def clear(step, carry):
        total[pl.ds(pl.multiple_of(step * 96, 32), 96), :] = jnp.zeros((96, WIDE_ROWS), jnp.float32)
        return carry

    def clear_grad(step, carry):
        grad[pl.ds(pl.multiple_of(step * INNER, 128), INNER), :] = jnp.zeros((INNER, PART), jnp.float32)
        return carry

    def add_gradient():
        grad[...] += lax.dot_general(
            window[...], chunk[...], (((0,), (0,)), ((), ())), preferred_element_type=jnp.float32
        )

    def fill_window(source, row):
        for position in range(4):
            block = block_of(core, position, row)
            for p in range(3):
                window[
                    position * PIECE : (position + 1) * PIECE, p * WIDE_ROWS : (p + 1) * WIDE_ROWS
                ] = source[pl.ds(pl.multiple_of(block * PIECE + p * ACROSS, 16), PIECE), :]

    def fill_chunk(source, row):
        for position in range(4):
            block = block_of(core, position, row)
            chunk[position * PIECE : (position + 1) * PIECE, :] = source[rows_of(block), :]

    def hand_over(which):
        def pack(tap, carry):
            to = pl.ds(pl.multiple_of(tap * 64, 64), 64)
            own_rows = pl.ds(pl.multiple_of(tap * INNER + core * 64, 64), 64)
            other_rows = pl.ds(pl.multiple_of(tap * INNER + (1 - core) * 64, 64), 64)
            full[which, core, to, :] = grad[own_rows, :].astype(jnp.bfloat16)
            give[which, to, :] = grad[other_rows, :].astype(jnp.bfloat16)
            return carry

        lax.fori_loop(0, 9, pack, 0)
        copies.start(38 + which, give.at[which], full.at[which, core], partner)

    def share(which, at, low, length):
        at = at % 4
        lanes = pl.ds(pl.multiple_of((at % 2) * 256, 256), 256)
        return full.at[which, at // 2, pl.ds(low, length), lanes]

    def depth_far(which):
        copies.arrived(38 + which, full.at[which, 1 - core], partner)
        copies.start(40 + which, share(which, depth + 2, 0, 288), zfar_in.at[which, 0], z_up)
        copies.start(42 + which, share(which, depth + 2, 288, 288), zfar_in.at[which, 1], z_down)

    def depth_near(which):
        near = share(which, depth + 1, 288, 288)[...]
        zup_out[which, 288:576, :] = near
        near = share(which, depth + 3, 0, 288)[...]
        zdown_out[which, 0:288, :] = near
        copies.arrived(40 + which, zfar_in.at[which, 0], z_up)
        near = share(which, depth + 1, 0, 288)[...].astype(jnp.float32)
        zup_out[which, 0:288, :] = narrow(near + zfar_in[which, 0].astype(jnp.float32))
        copies.start(44 + which, zup_out.at[which], zup_in.at[which], z_up)
        copies.arrived(42 + which, zfar_in.at[which, 1], z_down)
        near = share(which, depth + 3, 288, 288)[...].astype(jnp.float32)
        zdown_out[which, 288:576, :] = narrow(near + zfar_in[which, 1].astype(jnp.float32))
        copies.start(46 + which, zdown_out.at[which], zdown_in.at[which], z_down)

    def depth_own(which, out):
        copies.arrived(44 + which, zup_in.at[which], z_up)
        copies.arrived(46 + which, zdown_in.at[which], z_down)
        out[...] = (
            share(which, depth, 0, 576)[...].astype(jnp.float32)
            + zup_in[which].astype(jnp.float32)
            + zdown_in[which].astype(jnp.float32)
        )

    def narrow(values):
        return values.astype(jnp.bfloat16)

    lax.fori_loop(0, 33, clear, 0)
    if backward:
        lax.fori_loop(0, 9, clear_grad, 0)
    padded[0:ACROSS, :] = jnp.zeros((ACROSS, WIDE_ROWS), jnp.bfloat16)
    padded[SPOTS + ACROSS :, :] = jnp.zeros((ACROSS, WIDE_ROWS), jnp.bfloat16)

    offsets = (0, 3, 1, 2)

    def relay(order):
        first_at = first + offsets[order]
        here = piece(first_at, second + 3)
        copies.arrived(5 + order, here, s_up)
        low = piece(first_at, second + 3, 0, HALF)
        copies.start(13 + order, low, low, s_up)
        here = piece(first_at, second + 1)
        copies.arrived(9 + order, here, s_down)
        high = piece(first_at, second + 1, HALF, HALF)
        copies.start(48 + order, high, high, s_down)

    left = piece(first + 3, second)
    right = piece(first + 1, second)
    copies.arrived(1, left, f_up)
    low = piece(first + 3, second, 0, HALF)
    copies.start(3, low, low, f_up)
    send_second(1, first + 3)
    copies.arrived(2, right, f_down)
    high = piece(first + 1, second, HALF, HALF)
    copies.start(4, high, high, f_down)
    send_second(2, first + 1)
    relay(0)
    copies.arrived(3, piece(first + 2, second, 0, HALF), f_up)
    copies.arrived(4, piece(first + 2, second, HALF, HALF), f_down)
    send_second(3, first + 2)
    for load in loads:
        load.wait()

    def product(step, carry):
        turn = (3 * step + (step // 2) * (7 - 2 * step)) % 4

        @pl.when(step == 1)
        def _():
            for order in (1, 2, 3):
                first_at = first + offsets[order]
                copies.arrived(5 + order, piece(first_at, second + 3), s_up)
                low = piece(first_at, second + 3, 0, HALF)
                copies.remote(13 + order, low, low, s_up).start()
                copies.arrived(9 + order, piece(first_at, second + 1), s_down)
                high = piece(first_at, second + 1, HALF, HALF)
                copies.remote(48 + order, high, high, s_down).start()

        @pl.when(step == 3)
        def _():
            for order in range(4):
                first_at = first + offsets[order]
                copies.arrived(13 + order, piece(first_at, second + 2, 0, HALF), s_up)
                copies.arrived(48 + order, piece(first_at, second + 2, HALF, HALF), s_down)

        row = (second + turn) % 4
        fill_chunk(xall, row)
        result = jnp.dot(chunk[...], wa[...], preferred_element_type=jnp.float32)
        for position in range(4):
            block = block_of(core, position, row)
            for p in range(3):
                where = pl.ds(pl.multiple_of(block * PIECE + (2 - p) * ACROSS, 16), PIECE)
                total[where, :] += result[
                    position * PIECE : (position + 1) * PIECE, p * WIDE_ROWS : (p + 1) * WIDE_ROWS
                ]

        if backward:

            @pl.when(step < 3)
            def _():
                fill_window(ef, row)
                add_gradient()

        return carry

    lax.fori_loop(0, 4, product, 0)
    for order in (1, 2, 3):
        here = piece(first, second, 0, HALF)
        copies.sent.append(copies.remote(13 + order, here, here, s_up))
        copies.sent.append(copies.remote(48 + order, here, here, s_down))

    at_left, at_right = edge_masks(PIECE)

    def fold(step, carry):
        rows = rows_of(step)
        padded_rows = pl.ds(pl.multiple_of(step * PIECE + ACROSS, 16), PIECE)
        pre[rows, :] = (
            total[padded_rows, INNER : 2 * INNER]
            + from_left(total[padded_rows, 0:INNER], at_left)
            + from_right(total[padded_rows, 2 * INNER :], at_right)
        )
        return carry

    for quarter in range(4):
        lax.fori_loop(quarter * 4, quarter * 4 + 4, fold, 0)
        rows = pl.ds(quarter * 768, 768)
        copies.start(17 + quarter, pre.at[rows, :], other.at[rows, :], partner)

    if backward:
        fill_window(ef, (second + 2) % 4)
        add_gradient()
        hand_over(0)
        lax.fori_loop(0, 9, clear_grad, 0)

    def shape(step, carry):
        rows = rows_of(step)
        padded_rows = pl.ds(pl.multiple_of(step * PIECE + ACROSS, 16), PIECE)
        value = pre[rows, :] + other[rows, :]
        if backward:
            value = value * silu_slope(pre_f[rows, :])
        else:
            other[rows, :] = value
            value = jax.nn.silu(value)
        value = value.astype(jnp.bfloat16).astype(jnp.float32)
        padded[padded_rows, 0:INNER] = from_left(value, at_left).astype(jnp.bfloat16)
        padded[padded_rows, INNER : 2 * INNER] = value.astype(jnp.bfloat16)
        padded[padded_rows, 2 * INNER :] = from_right(value, at_right).astype(jnp.bfloat16)
        return carry

    for quarter in range(4):
        copies.arrived(17 + quarter, other.at[pl.ds(quarter * 768, 768), :], partner)
        lax.fori_loop(quarter * 4, quarter * 4 + 4, shape, 0)

    stores = []
    if not backward:
        stores = [
            pltpu.make_async_copy(other, pre_hbm, local_sems.at[2]),
            pltpu.make_async_copy(padded, ef_hbm, local_sems.at[3]),
            pltpu.make_async_copy(xall, xf_hbm, local_sems.at[4]),
        ]
        for store in stores:
            store.start()

    if backward:
        depth_far(0)

    def place_of(order):
        return (first + (2, 1, 3, 0)[order]) % 4

    def spread(step, carry):
        turn = (2 - step + (step // 2) * (7 - 2 * step)) % 4
        row = (second + turn) % 4
        fill_window(padded, row)
        result = jnp.dot(window[...], wb[...], preferred_element_type=jnp.float32)
        for position in range(4):
            reduced[step, position] = result[position * PIECE : (position + 1) * PIECE, :]

        @pl.when(step == 0)
        def _():
            for order in range(4):
                far_out[order] = narrow(reduced[0, place_of(order)])
                low = pl.ds(0, HALF)
                copies.remote(
                    21 + order, far_out.at[order, low, :], far_in.at[order, low, :], s_up
                ).start()
                high = pl.ds(HALF, HALF)
                copies.remote(
                    33 + order, far_out.at[order, high, :], far_in.at[order, high, :], s_down
                ).start()

        @pl.when(step == 2)
        def _():
            for order in range(4):
                at = place_of(order)
                low = pl.ds(0, HALF)
                high = pl.ds(HALF, HALF)
                up_out[order, high, :] = narrow(reduced[1, at, high, :])
                down_out[order, low, :] = narrow(reduced[2, at, low, :])
                copies.arrived(21 + order, far_in.at[order, low, :], s_up)
                up_out[order, low, :] = narrow(
                    reduced[1, at, low, :] + far_in[order, low, :].astype(jnp.float32)
                )
                copies.remote(25 + order, up_out.at[order], up_in.at[order], s_up).start()
                copies.arrived(33 + order, far_in.at[order, high, :], s_down)
                down_out[order, high, :] = narrow(
                    reduced[2, at, high, :] + far_in[order, high, :].astype(jnp.float32)
                )
                copies.remote(29 + order, down_out.at[order], down_in.at[order], s_down).start()

        if backward:

            @pl.when(step >= 2)
            def _():
                fill_chunk(xf, row)
                add_gradient()

            @pl.when(step == 3)
            def _():
                for turn in (2, 1):
                    fill_window(padded, (second + turn) % 4)
                    fill_chunk(xf, (second + turn) % 4)
                    add_gradient()

        return carry

    lax.fori_loop(0, 4, spread, 0)
    for order in range(4):
        low = pl.ds(0, HALF)
        half = far_out.at[order, low, :]
        copies.sent.append(copies.remote(21 + order, half, half, s_up))
        copies.sent.append(copies.remote(33 + order, half, half, s_down))
        copies.sent.append(copies.remote(25 + order, up_out.at[order], up_in.at[order], s_up))
        copies.sent.append(copies.remote(29 + order, down_out.at[order], down_in.at[order], s_down))
    if backward:
        hand_over(1)
        depth_near(0)

    def arrive_second(order):
        copies.arrived(25 + order, up_in.at[order], s_up)
        copies.arrived(29 + order, down_in.at[order], s_down)

    def gathered(order, low, length):
        rows = pl.ds(low, length)
        return (
            reduced[3, place_of(order), rows, :]
            + up_in[order, rows, :].astype(jnp.float32)
            + down_in[order, rows, :].astype(jnp.float32)
        )

    arrive_second(0)
    far2_out[0] = narrow(gathered(0, 0, HALF))
    copies.start(52, far2_out.at[0], far2_in.at[0], f_up)
    far2_out[1] = narrow(gathered(0, HALF, HALF))
    copies.start(53, far2_out.at[1], far2_in.at[1], f_down)
    if backward:
        depth_far(1)
    arrive_second(1)
    up2_out[HALF:, :] = narrow(gathered(1, HALF, HALF))
    copies.arrived(52, far2_in.at[0], f_up)
    up2_out[:HALF, :] = narrow(gathered(1, 0, HALF) + far2_in[0].astype(jnp.float32))
    copies.start(54, up2_out, up2_in, f_up)
    arrive_second(2)
    down2_out[:HALF, :] = narrow(gathered(2, 0, HALF))
    copies.arrived(53, far2_in.at[1], f_down)
    down2_out[HALF:, :] = narrow(gathered(2, HALF, HALF) + far2_in[1].astype(jnp.float32))
    copies.start(55, down2_out, down2_in, f_down)
    if backward:
        depth_near(1)
    arrive_second(3)
    copies.arrived(54, up2_in, f_up)
    copies.arrived(55, down2_in, f_down)

    def settled(which):
        rows = pl.ds(pl.multiple_of(which * HALF, 32), HALF)
        return (
            reduced[3, first, rows, :]
            + up_in[3, rows, :].astype(jnp.float32)
            + down_in[3, rows, :].astype(jnp.float32)
            + up2_in[rows, :].astype(jnp.float32)
            + down2_in[rows, :].astype(jnp.float32)
        )

    swap_out[...] = narrow(settled(1 - core))
    copies.start(37, swap_out, swap_in, partner)
    out_ref[core] = narrow(x_ref[core].astype(jnp.float32) + settled(core))
    copies.arrived(37, swap_in, partner)
    out_ref[1 - core] = narrow(x_ref[1 - core].astype(jnp.float32) + swap_in[...].astype(jnp.float32))
    if backward:
        depth_own(0, ge_ref)
        depth_own(1, gf_ref)
    copies.finish()
    for store in stores:
        store.wait()


def bottleneck(values, wa, wb, saved=None):
    backward = saved is not None
    b16, f32 = jnp.bfloat16, jnp.float32
    vmem = pl.BlockSpec(memory_space=pltpu.VMEM)
    anywhere = pl.BlockSpec(memory_space=pl.ANY)
    padded_rows = SPOTS + 2 * ACROSS
    keep = [
        jax.ShapeDtypeStruct((SPOTS, INNER), f32),
        jax.ShapeDtypeStruct((padded_rows, WIDE_ROWS), b16),
        jax.ShapeDtypeStruct((SPOTS, PART), b16),
    ]
    out = jax.ShapeDtypeStruct((2, HALF, PART), b16)
    grad = jax.ShapeDtypeStruct((9 * INNER // 2, PART // 2), f32)
    scratch = [
        pltpu.VMEM((SPOTS, PART), b16),
        pltpu.VMEM((PART, 9 * INNER), b16),
        pltpu.VMEM((9 * INNER, PART), b16),
        pltpu.VMEM((padded_rows, WIDE_ROWS), f32),
        pltpu.VMEM((SPOTS, INNER), f32),
        pltpu.VMEM((SPOTS, INNER), f32),
        pltpu.VMEM((padded_rows, WIDE_ROWS), b16),
        pltpu.VMEM((4 * PIECE, PART), b16),
        pltpu.VMEM((4 * PIECE, 9 * INNER), b16),
        *[pltpu.VMEM((4, PIECE, PART), b16) for _ in range(6)],
        pltpu.VMEM((4, 4, PIECE, PART), f32),
        pltpu.VMEM((2, HALF, PART), b16),
        pltpu.VMEM((PIECE, PART), b16),
        pltpu.VMEM((PIECE, PART), b16),
        pltpu.VMEM((2, HALF, PART), b16),
        pltpu.VMEM((PIECE, PART), b16),
        pltpu.VMEM((PIECE, PART), b16),
        pltpu.VMEM((HALF, PART), b16),
        pltpu.VMEM((HALF, PART), b16),
        pltpu.SemaphoreType.DMA((56,)),
        pltpu.SemaphoreType.DMA((56,)),
        pltpu.SemaphoreType.DMA((5,)),
    ]
    if backward:
        scratch += [
            pltpu.VMEM((SPOTS, INNER), f32),
            pltpu.VMEM((padded_rows, WIDE_ROWS), b16),
            pltpu.VMEM((SPOTS, PART), b16),
            pltpu.VMEM((9 * INNER, PART), f32),
            pltpu.VMEM((2, 2, 576, PART), b16),
            pltpu.VMEM((2, 576, PART), b16),
            pltpu.VMEM((2, 2, 288, 256), b16),
            *[pltpu.VMEM((2, 576, 256), b16) for _ in range(4)],
        ]
    blocks = jnp.transpose(values.reshape(HALF, 2, PART), (1, 0, 2))
    results = pl.pallas_call(
        functools.partial(phase_kernel, backward),
        out_shape=[out, grad, grad] if backward else [out, *keep],
        in_specs=[vmem] + [anywhere] * (5 if backward else 2),
        out_specs=[vmem] * 3 if backward else [vmem] + [anywhere] * 3,
        scratch_shapes=scratch,
        compiler_params=pltpu.CompilerParams(
            collective_id=2 if backward else 1,
            has_side_effects=True,
            vmem_limit_bytes=60 * 1024 * 1024,
        ),
        name="backward_phase" if backward else "forward_phase",
    )(blocks, wa, wb, *(saved or ()))
    total = jnp.transpose(results[0], (1, 0, 2)).reshape(HALF, 2 * PART)
    return total, results[1:]


def swap_cores(values):
    count = lax.axis_size("wide")
    return lax.ppermute(values, "wide", [(i, i ^ 1) for i in range(count)])


def pair_part(values, dim, core):
    own = lax.dynamic_slice_in_dim(values, core * PART, PART, axis=dim)
    theirs = swap_cores(lax.dynamic_slice_in_dim(values, (1 - core) * PART, PART, axis=dim))
    return jnp.where(core == 0, own, theirs), jnp.where(core == 0, theirs, own)


SUM_ROWS = 1280


def sum_kernel(down_ref, up_ref, conv_ref, class_ref, out_ref, total, give, pair_in, a_out, a_in,
               b_out, b_in, z_out, z_in, result, send_sems, recv_sems):
    core, first, second = place()
    depth = lax.axis_index("samp")
    me = block_of(core, first, second)
    partner = {"wide": me * 2 + 1 - core}
    first_peers = [
        {"wide": block_of(core, (first + d) % 4, second) * 2 + core} for d in range(4)
    ]
    second_peers = [
        {"wide": block_of(core, first, (second + d) % 4) * 2 + core} for d in range(4)
    ]
    depth_peers = [{"samp": (depth + d) % 4} for d in range(4)]
    copies = Copies(send_sems, recv_sems)
    barrier = pltpu.get_barrier_semaphore()
    for device in [partner, *first_peers[1:], *second_peers[1:], *depth_peers[1:]]:
        pl.semaphore_signal(
            barrier, inc=1, device_id=device, device_id_type=pl.DeviceIdType.MESH
        )
    pl.semaphore_wait(barrier, 10)

    def own_lanes(half, width):
        return pl.ds(pl.multiple_of(half * width, 128), width)

    def pack(half, to, kind):
        to[0:512, :] = down_ref[:, own_lanes(half, 512)].astype(kind)
        to[512:1024, :] = up_ref[pl.ds(pl.multiple_of(half * 512, 512), 512), :].astype(kind)
        for piece in range(4):
            rows = pl.ds(pl.multiple_of((half * 4 + piece) * 144, 16), 144)
            to[1024:1168, piece * 128 : (piece + 1) * 128] = conv_ref[rows, :].astype(kind)
        to[1168:1184, :] = class_ref[:, own_lanes(half, 512)].astype(kind)
        to[1184:, :] = jnp.zeros((SUM_ROWS - 1184, PART), kind)

    def spot(at_first, at_second):
        base = (at_first % 4) * 320 + (at_second % 4) * 80
        return pl.ds(pl.multiple_of(base, 16), 80)

    order = (2, 1, 3, 0)
    pack(1 - core, give, jnp.bfloat16)
    for i, ds in enumerate(order):
        for df in range(4):
            part = spot(second + df, first + ds)
            copies.start(i * 4 + df, give.at[part, :], pair_in.at[part, :], partner)
    pack(core, total, jnp.float32)
    for i, ds in enumerate(order):
        for df in range(1, 4):
            part = spot(first + df, second + ds)
            copies.arrived(i * 4 + df, pair_in.at[part, :], partner)
            a_out[df, i] = (total[part, :] + pair_in[part, :].astype(jnp.float32)).astype(
                jnp.bfloat16
            )
            copies.start(16 + i * 3 + df - 1, a_out.at[df, i], a_in.at[df, i], first_peers[df])

    def after_first(i):
        part = spot(first, second + order[i])
        copies.arrived(i * 4, pair_in.at[part, :], partner)
        value = total[part, :] + pair_in[part, :].astype(jnp.float32)
        for df in range(1, 4):
            copies.arrived(16 + i * 3 + df - 1, a_in.at[df, i], first_peers[df])
            value = value + a_in[df, i].astype(jnp.float32)
        return value

    for i in range(3):
        b_out[i] = after_first(i).astype(jnp.bfloat16)
        copies.start(28 + i, b_out.at[i], b_in.at[i], second_peers[order[i]])
    total[0:80, :] = after_first(3)
    for i in range(3):
        copies.arrived(28 + i, b_in.at[i], second_peers[order[i]])
        total[0:80, :] += b_in[i].astype(jnp.float32)
    for d in range(1, 4):
        z_out[d] = total[0:80, own_lanes((depth + d) % 4, 128)].astype(jnp.bfloat16)
        copies.start(30 + d, z_out.at[d], z_in.at[d], depth_peers[d])
    value = total[0:80, own_lanes(depth, 128)]
    for d in range(1, 4):
        copies.arrived(30 + d, z_in.at[d], depth_peers[d])
        value = value + z_in[d].astype(jnp.float32)

    def at_depth(d):
        return result.at[core, spot(first, second), own_lanes((depth + d) % 4, 128)]

    def at(df, ds, half):
        return result.at[half, spot(first + df, second + ds), :]

    def pass_on(df, ds):
        copies.start(52 + df * 4 + ds, at(df, ds, core), at(df, ds, core), partner)

    def along_first(ds):
        for df in range(1, 4):
            copies.start(40 + ds * 3 + df - 1, at(0, ds, core), at(0, ds, core), first_peers[df])

    at_depth(0)[...] = value.astype(jnp.bfloat16)
    for d in range(1, 4):
        copies.start(33 + d, at_depth(0), at_depth(0), depth_peers[d])
    for d in range(1, 4):
        copies.arrived(33 + d, at_depth(4 - d), depth_peers[d])
    for ds in range(1, 4):
        copies.start(36 + ds, at(0, 0, core), at(0, 0, core), second_peers[ds])
    along_first(0)
    pass_on(0, 0)
    for ds in (1, 3, 2):
        copies.arrived(36 + ds, at(0, 4 - ds, core), second_peers[ds])
        along_first(4 - ds)
        pass_on(0, 4 - ds)
    for ds in (0, 3, 1, 2):
        for df in (1, 3, 2):
            copies.arrived(40 + ds * 3 + df - 1, at(4 - df, ds, core), first_peers[df])
            pass_on(4 - df, ds)
    out_ref[core] = result[core]
    for df in range(4):
        for ds in range(4):
            copies.arrived(52 + df * 4 + ds, at(df, ds, 1 - core), partner)
    out_ref[1 - core] = result[1 - core]
    copies.finish()


def sum_everywhere(conv_grad, down_grad, up_grad, class_grad):
    b16, f32 = jnp.bfloat16, jnp.float32
    vmem = pl.BlockSpec(memory_space=pltpu.VMEM)
    classes = class_grad.shape[1]
    small = jnp.pad(class_grad.T, ((0, 16 - classes), (0, 2 * PART - INNER)))
    out = pl.pallas_call(
        sum_kernel,
        out_shape=jax.ShapeDtypeStruct((2, SUM_ROWS, PART), b16),
        in_specs=[vmem] * 4,
        out_specs=vmem,
        scratch_shapes=[
            pltpu.VMEM((SUM_ROWS, PART), f32),
            pltpu.VMEM((SUM_ROWS, PART), b16),
            pltpu.VMEM((SUM_ROWS, PART), b16),
            pltpu.VMEM((4, 4, 80, PART), b16),
            pltpu.VMEM((4, 4, 80, PART), b16),
            pltpu.VMEM((3, 80, PART), b16),
            pltpu.VMEM((3, 80, PART), b16),
            pltpu.VMEM((4, 80, 128), b16),
            pltpu.VMEM((4, 80, 128), b16),
            pltpu.VMEM((2, SUM_ROWS, PART), b16),
            pltpu.SemaphoreType.DMA((68,)),
            pltpu.SemaphoreType.DMA((68,)),
        ],
        compiler_params=pltpu.CompilerParams(
            collective_id=3, has_side_effects=True, vmem_limit_bytes=60 * 1024 * 1024
        ),
        name="sum_everywhere",
    )(down_grad, up_grad, conv_grad.reshape(9 * INNER, INNER), small)
    down = jnp.concatenate([out[0, 0:512], out[1, 0:512]], axis=1).astype(f32)
    up = out[:, 512:1024].astype(f32).reshape(2 * PART, PART)
    conv = jnp.concatenate(
        [out[h, 1024:1168, i * 128 : (i + 1) * 128] for h in range(2) for i in range(4)], axis=0
    )
    conv = conv.astype(f32).reshape(conv_grad.shape)
    return conv, down, up, out[0, 1168 : 1168 + classes, 0:INNER].astype(f32).T


def local(
    features,
    labels,
    conv_weight,
    down_weight,
    expand_weight,
    reduce_weight,
    up_weight,
    class_weight,
):
    crop_rows = features[0]
    label_map = labels[0]
    height, across, channels = crop_rows.shape
    half_rows = height // 2
    half_across = across // 2
    core = lax.axis_index("wide") % 2
    pixel_count = lax.axis_size("wide") * lax.axis_size("samp") * height * across
    loss_scale = 8.0 / math.sqrt(pixel_count)
    classes = lax.broadcasted_iota(jnp.int32, (1, 1, class_weight.shape[1]), 2)

    expand_both = jnp.concatenate(
        pair_part(expand_weight.reshape(9, 2 * PART, INNER // 2), 1, core), axis=2
    )
    reduce_both = jnp.concatenate(
        pair_part(reduce_weight.reshape(9, INNER // 2, 2 * PART), 2, core), axis=1
    )
    wa_forward = jnp.transpose(expand_both, (1, 0, 2)).reshape(PART, 9 * INNER)
    wb_forward = reduce_both.reshape(9 * INNER, PART)
    wa_backward = jnp.transpose(reduce_both[::-1], (2, 0, 1)).reshape(PART, 9 * INNER)
    wb_backward = jnp.transpose(expand_both[::-1], (0, 2, 1)).reshape(9 * INNER, PART)

    near_rows = extended(crop_rows, (("wide", 0),), 1)
    padded_in = jnp.pad(near_rows, ((0, 0), (1, 1), (0, 0)))
    hidden_pre = conv_padded(padded_in, conv_weight)
    hidden = jax.nn.silu(hidden_pre).astype(jnp.bfloat16)
    stacked = to_depth(hidden)
    coarse = project_rows(stacked, down_weight)
    bottom, saved = bottleneck(coarse.reshape(-1, 2 * PART), wa_forward, wb_forward)
    bottom = bottom.reshape(half_rows, half_across, 2 * PART)
    upward = from_depth(jnp.dot(bottom, up_weight, preferred_element_type=jnp.float32))
    joined_pre = upward + hidden.astype(jnp.float32)
    joined = jax.nn.silu(joined_pre).astype(jnp.bfloat16)
    logits = jnp.dot(joined, class_weight, preferred_element_type=jnp.float32)
    exp_logits = jnp.exp(logits)
    probability = exp_logits / jnp.sum(exp_logits, axis=-1, keepdims=True)
    onehot = (label_map[:, :, None] == classes).astype(jnp.float32)
    logit_grad = ((probability - onehot) * loss_scale).astype(jnp.bfloat16)
    class_grad = contract_rows(joined, logit_grad)
    joined_grad = lax.dot_general(
        logit_grad, class_weight, (((2,), (1,)), ((), ())), preferred_element_type=jnp.float32
    )
    upward_grad = (joined_grad * silu_slope(joined_pre)).astype(jnp.bfloat16)
    stacked_grad = to_depth(upward_grad)
    up_grad = contract_rows(bottom, stacked_grad)
    bottom_grad = widen_rows(stacked_grad, up_weight)
    coarse_grad, (reduce_grad, expand_grad) = bottleneck(
        bottom_grad.reshape(-1, 2 * PART), wa_backward, wb_backward, saved
    )
    coarse_grad = coarse_grad.reshape(half_rows, half_across, 2 * PART)
    down_grad = contract_rows(stacked, coarse_grad)
    down_back = lax.dot_general(
        coarse_grad, down_weight, (((2,), (1,)), ((), ())), preferred_element_type=jnp.float32
    )
    hidden_sum = from_depth(down_back) + upward_grad.astype(jnp.float32)
    hidden_grad = (hidden_sum * silu_slope(hidden_pre)).astype(jnp.bfloat16)
    conv_grad = correlate(padded_in, hidden_grad)
    conv_grad, down_grad, up_grad, class_grad = sum_everywhere(
        conv_grad, down_grad, up_grad, class_grad
    )
    reduce_grad = reduce_grad.reshape(3, 3, INNER // 2, -1)
    expand_grad = jnp.transpose(expand_grad.reshape(9, INNER // 2, -1)[::-1], (0, 2, 1))
    expand_grad = expand_grad.reshape(3, 3, -1, INNER // 2)
    return (conv_grad, down_grad, expand_grad, reduce_grad, up_grad, class_grad)


def solution(mesh):
    return jax.shard_map(
        local,
        mesh=mesh,
        in_specs=(
            P("samp", "wide", None, None),
            P("samp", "wide", None),
            P(),
            P(),
            P(None, None, None, "wide"),
            P(None, None, "wide", None),
            P(),
            P(),
        ),
        out_specs=(
            P(),
            P(),
            P(None, None, "samp", "wide"),
            P(None, None, "wide", "samp"),
            P(),
            P(),
        ),
        check_vma=False,
    )
```

```python
import functools
import math

import jax
import jax.numpy as jnp
from jax import lax
from jax.experimental import pallas as pl
from jax.experimental.pallas import tpu as pltpu
from jax.sharding import PartitionSpec as P


def silu_slope(value):
    logistic = jax.nn.sigmoid(value)
    return logistic * (1.0 + value * (1.0 - logistic))


ROWS = 64
ACROSS = 48
SPOTS = ROWS * ACROSS
PIECE = 192
HALF = 96
PART = 512
INNER = 128
WIDE_ROWS = 3 * INNER


def place():
    wide = lax.axis_index("wide")
    core = wide % 2
    x = (wide // 2) % 4
    y = wide // 8
    first = x + core * (y - x)
    second = y + core * (x - y)
    return core, first % 4, second % 4


def block_of(core, first, second):
    x = first + core * (second - first)
    y = second + core * (first - second)
    return y * 4 + x


def rows_of(block, length=PIECE):
    return pl.ds(pl.multiple_of(block * PIECE, 64), length)


def edge_masks(length):
    column = lax.broadcasted_iota(jnp.int32, (length, INNER), 0) % ACROSS
    return column == 0, column == ACROSS - 1


def from_left(values, at_left):
    return jnp.where(at_left, 0.0, pltpu.roll(values, 1, axis=0))


def from_right(values, at_right):
    return jnp.where(at_right, 0.0, pltpu.roll(values, values.shape[0] - 1, axis=0))


class Copies:
    def __init__(self, send_sems, recv_sems):
        self.send_sems = send_sems
        self.recv_sems = recv_sems
        self.sent = []

    def remote(self, index, source, target, device):
        copy = pltpu.make_async_remote_copy(
            src_ref=source,
            dst_ref=target,
            send_sem=self.send_sems.at[index],
            recv_sem=self.recv_sems.at[index],
            device_id=device if isinstance(device, dict) else {"wide": device},
            device_id_type=pl.DeviceIdType.MESH,
        )
        return copy

    def start(self, index, source, target, device):
        copy = self.remote(index, source, target, device)
        copy.start()
        self.sent.append(copy)

    def arrived(self, index, target, device):
        self.remote(index, target, target, device).wait_recv()

    def finish(self):
        for copy in self.sent:
            copy.wait_send()


def contract_first(left, right):
    return lax.dot_general(left, right, (((0,), (0,)), ((), ())), preferred_element_type=jnp.float32)


def contract_last(left, right):
    return lax.dot_general(left, right, (((1,), (1,)), ((), ())), preferred_element_type=jnp.float32)


def multiply(left, right):
    return jnp.dot(left, right, preferred_element_type=jnp.float32)


def side_by_side(tall):
    return jnp.concatenate([tall[i * HALF : (i + 1) * HALF] for i in range(4)], axis=1)


def stacked_up(flat):
    return jnp.concatenate([flat[:, i * INNER : (i + 1) * INNER] for i in range(4)], axis=0)


def first_layers(wide, copies, after, before, feature_ref, halo, columns, conv_weight_ref,
                 down_weight_ref, taps_ref, hidden_pre_ref, stacked_ref, x_ref):
    at_left, at_right = edge_masks(ACROSS)

    def row_columns(row, even, odd):
        to = pl.ds(row * ACROSS, ACROSS)
        even = even.astype(jnp.float32)
        odd = odd.astype(jnp.float32)
        columns[0, to, :] = from_left(odd, at_left).astype(jnp.bfloat16)
        columns[1, to, :] = even.astype(jnp.bfloat16)
        columns[2, to, :] = odd.astype(jnp.bfloat16)
        columns[3, to, :] = from_right(even, at_right).astype(jnp.bfloat16)

    for row in range(4):
        row_columns(row + 1, feature_ref[0, row], feature_ref[1, row])
    copies.arrived(56, halo.at[0], after)
    copies.arrived(57, halo.at[1], before)
    inside = jnp.where(wide > 0, 1.0, 0.0)
    row_columns(0, halo[0, 0].astype(jnp.float32) * inside, halo[0, 1].astype(jnp.float32) * inside)
    inside = jnp.where(wide < 31, 1.0, 0.0)
    row_columns(5, halo[1, 0].astype(jnp.float32) * inside, halo[1, 1].astype(jnp.float32) * inside)
    for a in range(2):
        for b in range(2):
            for i in range(2):
                for p in range(3):
                    for q in range(3):
                        low = (a * 2 + b) * HALF + i * ACROSS
                        source = (a + p + 2 * i) * ACROSS
                        tap = (p * 3 + q) * INNER
                        taps_ref[low : low + ACROSS, tap : tap + INNER] = columns[
                            b + q, source : source + ACROSS, :
                        ]
    hidden_pre = multiply(taps_ref[...], conv_weight_ref[...])
    hidden_pre = side_by_side(hidden_pre)
    hidden_pre_ref[...] = hidden_pre
    stacked = jax.nn.silu(hidden_pre).astype(jnp.bfloat16)
    stacked_ref[...] = stacked
    for half in range(2):
        x_ref[half] = multiply(
            stacked, down_weight_ref[:, half * PART : (half + 1) * PART]
        ).astype(jnp.bfloat16)


def middle(bottom_ref, stacked_ref, label_ref, up_weight_ref, class_ref, class_back_ref,
           x_ref, upward_grad_ref, class_grad_ref):
    loss_scale = 8.0 / math.sqrt(49152)
    upward = multiply(bottom_ref[0], up_weight_ref[0:PART, :]) + multiply(
        bottom_ref[1], up_weight_ref[PART:, :]
    )
    joined_pre = stacked_up(upward + stacked_ref[...].astype(jnp.float32))
    joined = jax.nn.silu(joined_pre).astype(jnp.bfloat16)
    logits = multiply(joined, class_ref[...])
    classes = lax.broadcasted_iota(jnp.int32, logits.shape, 1)
    exp_logits = jnp.where(classes < 9, jnp.exp(logits), 0.0)
    probability = exp_logits / jnp.sum(exp_logits, axis=1, keepdims=True)
    onehot = (label_ref[...] == classes).astype(jnp.float32)
    logit_grad = ((probability - onehot) * loss_scale).astype(jnp.bfloat16)
    joined_grad = multiply(logit_grad, class_back_ref[...])
    upward_grad = side_by_side((joined_grad * silu_slope(joined_pre)).astype(jnp.bfloat16))
    upward_grad_ref[...] = upward_grad
    for half in range(2):
        x_ref[half] = contract_last(
            upward_grad, up_weight_ref[half * PART : (half + 1) * PART, :]
        ).astype(jnp.bfloat16)
    class_grad_ref[...] = contract_first(joined, logit_grad)


def phase_kernel(backward, *refs):
    if backward:
        (
            wa_hbm, wb_hbm, pre_hbm, ef_hbm, xf_hbm, bottom_ref, stacked_ref, label_ref,
            up_weight_ref, class_ref, class_back_ref,
            out_ref, ge_ref, gf_ref, upward_grad_ref, class_grad_ref,
        ) = refs[:16]
        scratch = refs[16:]
    else:
        (
            feature_ref, conv_weight_ref, down_weight_ref, expand_hbm, reduce_hbm,
            out_ref, pre_hbm, ef_hbm, xf_hbm, wa_hbm, wb_hbm, stacked_ref, hidden_pre_ref,
            taps_ref,
        ) = refs[:14]
        scratch = refs[14:]
    (
        xall, wa, wb, total, pre, other, padded, chunk, window,
        far_out, up_out, down_out, far_in, up_in, down_in, reduced,
        far2_out, up2_out, down2_out, far2_in, up2_in, down2_in, swap_out, swap_in,
        x_ref, send_sems, recv_sems, local_sems,
    ) = scratch[:28]
    core, first, second = place()
    me = block_of(core, first, second)
    partner = me * 2 + 1 - core
    f_up = block_of(core, (first + 1) % 4, second) * 2 + core
    f_down = block_of(core, (first + 3) % 4, second) * 2 + core
    s_up = block_of(core, first, (second + 1) % 4) * 2 + core
    s_down = block_of(core, first, (second + 3) % 4) * 2 + core
    copies = Copies(send_sems, recv_sems)

    if backward:
        loads = [
            pltpu.make_async_copy(wa_hbm, wa, local_sems.at[0]),
            pltpu.make_async_copy(wb_hbm, wb, local_sems.at[1]),
        ]
        pre_f, ef, xf, grad, full, give, zfar_in, zup_out, zdown_out, zup_in, zdown_in = scratch[28:]
        loads += [
            pltpu.make_async_copy(pre_hbm, pre_f, local_sems.at[2]),
            pltpu.make_async_copy(ef_hbm, ef, local_sems.at[3]),
            pltpu.make_async_copy(xf_hbm, xf, local_sems.at[4]),
        ]
    else:
        expand_both, reduce_both, wa_back, wb_back, halo, columns = scratch[28:]
        lanes = pl.ds(pl.multiple_of(core * PART, PART), PART)
        other_lanes = pl.ds(pl.multiple_of((1 - core) * PART, PART), PART)
        own_rows = pl.ds(pl.multiple_of(core * 64, 64), 64)
        loads = [
            pltpu.make_async_copy(
                expand_hbm.at[:, lanes, :], expand_both.at[core], local_sems.at[0]
            ),
            pltpu.make_async_copy(
                reduce_hbm.at[:, :, lanes], reduce_both.at[:, own_rows, :], local_sems.at[1]
            ),
        ]
    for load in loads:
        load.start()

    peers = [{"wide": device} for device in (partner, f_up, f_down, s_up, s_down)]
    if backward:
        depth = lax.axis_index("samp")
        z_up = {"samp": (depth + 1) % 4}
        z_down = {"samp": (depth + 3) % 4}
        peers += [z_up, z_down]
    else:
        wide = lax.axis_index("wide")
        after = {"wide": (wide + 1) % 32}
        before = {"wide": (wide + 31) % 32}
        peers += [after, before]
    barrier = pltpu.get_barrier_semaphore()
    for device in peers:
        pl.semaphore_signal(
            barrier, inc=1, device_id=device, device_id_type=pl.DeviceIdType.MESH
        )
    if backward:
        middle(
            bottom_ref, stacked_ref, label_ref, up_weight_ref, class_ref, class_back_ref,
            x_ref, upward_grad_ref, class_grad_ref,
        )
    pl.semaphore_wait(barrier, len(peers))
    if not backward:
        copies.start(56, feature_ref.at[:, 3], halo.at[0], after)
        copies.start(57, feature_ref.at[:, 0], halo.at[1], before)
        copies.start(58, expand_hbm.at[:, other_lanes, :], expand_both.at[core], partner)
        copies.start(
            59, reduce_hbm.at[:, :, other_lanes], reduce_both.at[:, own_rows, :], partner
        )
        first_layers(
            wide, copies, after, before, feature_ref, halo, columns, conv_weight_ref,
            down_weight_ref, taps_ref, hidden_pre_ref, stacked_ref, x_ref,
        )

    mine = pl.ds(pl.multiple_of(me * PIECE + core * HALF, 32), HALF)
    theirs = pl.ds(pl.multiple_of(me * PIECE + (1 - core) * HALF, 32), HALF)
    copies.start(0, x_ref.at[1 - core], xall.at[mine, :], partner)
    xall[mine, :] = x_ref[core]
    copies.arrived(0, xall.at[theirs, :], partner)

    def piece(first_at, second_at, low=0, length=PIECE):
        block = block_of(core, first_at % 4, second_at % 4)
        return xall.at[pl.ds(pl.multiple_of(block * PIECE + low, 32), length), :]

    def send_second(order, first_at):
        copies.start(5 + order, piece(first_at, second), piece(first_at, second), s_up)
        copies.start(9 + order, piece(first_at, second), piece(first_at, second), s_down)

    own = piece(first, second)
    copies.start(1, own, own, f_up)
    copies.start(2, own, own, f_down)
    send_second(0, first)

    def clear(step, carry):
        total[pl.ds(pl.multiple_of(step * 96, 32), 96), :] = jnp.zeros((96, WIDE_ROWS), jnp.float32)
        return carry

    def clear_grad(step, carry):
        grad[pl.ds(pl.multiple_of(step * INNER, 128), INNER), :] = jnp.zeros((INNER, PART), jnp.float32)
        return carry

    def add_gradient():
        grad[...] += lax.dot_general(
            window[...], chunk[...], (((0,), (0,)), ((), ())), preferred_element_type=jnp.float32
        )

    def fill_window(source, row):
        for position in range(4):
            block = block_of(core, position, row)
            for p in range(3):
                window[
                    position * PIECE : (position + 1) * PIECE, p * WIDE_ROWS : (p + 1) * WIDE_ROWS
                ] = source[pl.ds(pl.multiple_of(block * PIECE + p * ACROSS, 16), PIECE), :]

    def fill_chunk(source, row):
        for position in range(4):
            block = block_of(core, position, row)
            chunk[position * PIECE : (position + 1) * PIECE, :] = source[rows_of(block), :]

    def hand_over(which):
        def pack(tap, carry):
            to = pl.ds(pl.multiple_of(tap * 64, 64), 64)
            own_rows = pl.ds(pl.multiple_of(tap * INNER + core * 64, 64), 64)
            other_rows = pl.ds(pl.multiple_of(tap * INNER + (1 - core) * 64, 64), 64)
            full[which, core, to, :] = grad[own_rows, :].astype(jnp.bfloat16)
            give[which, to, :] = grad[other_rows, :].astype(jnp.bfloat16)
            return carry

        lax.fori_loop(0, 9, pack, 0)
        copies.start(38 + which, give.at[which], full.at[which, core], partner)

    def share(which, at, low, length):
        at = at % 4
        lanes = pl.ds(pl.multiple_of((at % 2) * 256, 256), 256)
        return full.at[which, at // 2, pl.ds(low, length), lanes]

    def depth_far(which):
        copies.arrived(38 + which, full.at[which, 1 - core], partner)
        copies.start(40 + which, share(which, depth + 2, 0, 288), zfar_in.at[which, 0], z_up)
        copies.start(42 + which, share(which, depth + 2, 288, 288), zfar_in.at[which, 1], z_down)

    def depth_near(which):
        near = share(which, depth + 1, 288, 288)[...]
        zup_out[which, 288:576, :] = near
        near = share(which, depth + 3, 0, 288)[...]
        zdown_out[which, 0:288, :] = near
        copies.arrived(40 + which, zfar_in.at[which, 0], z_up)
        near = share(which, depth + 1, 0, 288)[...].astype(jnp.float32)
        zup_out[which, 0:288, :] = narrow(near + zfar_in[which, 0].astype(jnp.float32))
        copies.start(44 + which, zup_out.at[which], zup_in.at[which], z_up)
        copies.arrived(42 + which, zfar_in.at[which, 1], z_down)
        near = share(which, depth + 3, 288, 288)[...].astype(jnp.float32)
        zdown_out[which, 288:576, :] = narrow(near + zfar_in[which, 1].astype(jnp.float32))
        copies.start(46 + which, zdown_out.at[which], zdown_in.at[which], z_down)

    def depth_own(which, out):
        copies.arrived(44 + which, zup_in.at[which], z_up)
        copies.arrived(46 + which, zdown_in.at[which], z_down)
        out[...] = (
            share(which, depth, 0, 576)[...].astype(jnp.float32)
            + zup_in[which].astype(jnp.float32)
            + zdown_in[which].astype(jnp.float32)
        )

    def narrow(values):
        return values.astype(jnp.bfloat16)

    lax.fori_loop(0, 33, clear, 0)
    if backward:
        lax.fori_loop(0, 9, clear_grad, 0)
    padded[0:ACROSS, :] = jnp.zeros((ACROSS, WIDE_ROWS), jnp.bfloat16)
    padded[SPOTS + ACROSS :, :] = jnp.zeros((ACROSS, WIDE_ROWS), jnp.bfloat16)

    offsets = (0, 3, 1, 2)

    def relay(order):
        first_at = first + offsets[order]
        here = piece(first_at, second + 3)
        copies.arrived(5 + order, here, s_up)
        low = piece(first_at, second + 3, 0, HALF)
        copies.start(13 + order, low, low, s_up)
        here = piece(first_at, second + 1)
        copies.arrived(9 + order, here, s_down)
        high = piece(first_at, second + 1, HALF, HALF)
        copies.start(48 + order, high, high, s_down)

    left = piece(first + 3, second)
    right = piece(first + 1, second)
    copies.arrived(1, left, f_up)
    low = piece(first + 3, second, 0, HALF)
    copies.start(3, low, low, f_up)
    send_second(1, first + 3)
    copies.arrived(2, right, f_down)
    high = piece(first + 1, second, HALF, HALF)
    copies.start(4, high, high, f_down)
    send_second(2, first + 1)
    relay(0)
    copies.arrived(3, piece(first + 2, second, 0, HALF), f_up)
    copies.arrived(4, piece(first + 2, second, HALF, HALF), f_down)
    send_second(3, first + 2)
    for load in loads:
        load.wait()
    if not backward:
        copies.arrived(58, expand_both.at[1 - core], partner)
        partner_rows = pl.ds(pl.multiple_of((1 - core) * 64, 64), 64)
        copies.arrived(59, reduce_both.at[:, partner_rows, :], partner)
        for tap in range(9):
            here = slice(tap * INNER, (tap + 1) * INNER)
            back = slice((8 - tap) * INNER, (9 - tap) * INNER)
            block = jnp.concatenate([expand_both[0, tap], expand_both[1, tap]], axis=1)
            wa[:, here] = block
            wb_back[back, :] = block.T
            block = reduce_both[tap]
            wb[here, :] = block
            wa_back[:, back] = block.T
        stores = [
            pltpu.make_async_copy(wa_back, wa_hbm, local_sems.at[0]),
            pltpu.make_async_copy(wb_back, wb_hbm, local_sems.at[1]),
        ]
        for store in stores:
            store.start()
    else:
        stores = []

    def product(step, carry):
        turn = (3 * step + (step // 2) * (7 - 2 * step)) % 4

        @pl.when(step == 1)
        def _():
            for order in (1, 2, 3):
                first_at = first + offsets[order]
                copies.arrived(5 + order, piece(first_at, second + 3), s_up)
                low = piece(first_at, second + 3, 0, HALF)
                copies.remote(13 + order, low, low, s_up).start()
                copies.arrived(9 + order, piece(first_at, second + 1), s_down)
                high = piece(first_at, second + 1, HALF, HALF)
                copies.remote(48 + order, high, high, s_down).start()

        @pl.when(step == 3)
        def _():
            for order in range(4):
                first_at = first + offsets[order]
                copies.arrived(13 + order, piece(first_at, second + 2, 0, HALF), s_up)
                copies.arrived(48 + order, piece(first_at, second + 2, HALF, HALF), s_down)

        row = (second + turn) % 4
        fill_chunk(xall, row)
        result = jnp.dot(chunk[...], wa[...], preferred_element_type=jnp.float32)
        for position in range(4):
            block = block_of(core, position, row)
            for p in range(3):
                where = pl.ds(pl.multiple_of(block * PIECE + (2 - p) * ACROSS, 16), PIECE)
                total[where, :] += result[
                    position * PIECE : (position + 1) * PIECE, p * WIDE_ROWS : (p + 1) * WIDE_ROWS
                ]

        if backward:

            @pl.when(step < 3)
            def _():
                fill_window(ef, row)
                add_gradient()

        return carry

    lax.fori_loop(0, 4, product, 0)
    for order in (1, 2, 3):
        here = piece(first, second, 0, HALF)
        copies.sent.append(copies.remote(13 + order, here, here, s_up))
        copies.sent.append(copies.remote(48 + order, here, here, s_down))

    at_left, at_right = edge_masks(PIECE)

    def fold(step, carry):
        rows = rows_of(step)
        padded_rows = pl.ds(pl.multiple_of(step * PIECE + ACROSS, 16), PIECE)
        pre[rows, :] = (
            total[padded_rows, INNER : 2 * INNER]
            + from_left(total[padded_rows, 0:INNER], at_left)
            + from_right(total[padded_rows, 2 * INNER :], at_right)
        )
        return carry

    for quarter in range(4):
        lax.fori_loop(quarter * 4, quarter * 4 + 4, fold, 0)
        rows = pl.ds(quarter * 768, 768)
        copies.start(17 + quarter, pre.at[rows, :], other.at[rows, :], partner)

    if backward:
        fill_window(ef, (second + 2) % 4)
        add_gradient()
        hand_over(0)
        lax.fori_loop(0, 9, clear_grad, 0)

    def shape(step, carry):
        rows = rows_of(step)
        padded_rows = pl.ds(pl.multiple_of(step * PIECE + ACROSS, 16), PIECE)
        value = pre[rows, :] + other[rows, :]
        if backward:
            value = value * silu_slope(pre_f[rows, :])
        else:
            other[rows, :] = value
            value = jax.nn.silu(value)
        value = value.astype(jnp.bfloat16).astype(jnp.float32)
        padded[padded_rows, 0:INNER] = from_left(value, at_left).astype(jnp.bfloat16)
        padded[padded_rows, INNER : 2 * INNER] = value.astype(jnp.bfloat16)
        padded[padded_rows, 2 * INNER :] = from_right(value, at_right).astype(jnp.bfloat16)
        return carry

    for quarter in range(4):
        copies.arrived(17 + quarter, other.at[pl.ds(quarter * 768, 768), :], partner)
        lax.fori_loop(quarter * 4, quarter * 4 + 4, shape, 0)

    if not backward:
        more = [
            pltpu.make_async_copy(other, pre_hbm, local_sems.at[2]),
            pltpu.make_async_copy(padded, ef_hbm, local_sems.at[3]),
            pltpu.make_async_copy(xall, xf_hbm, local_sems.at[4]),
        ]
        for store in more:
            store.start()
        stores += more

    if backward:
        depth_far(0)

    def place_of(order):
        return (first + (2, 1, 3, 0)[order]) % 4

    def spread(step, carry):
        turn = (2 - step + (step // 2) * (7 - 2 * step)) % 4
        row = (second + turn) % 4
        fill_window(padded, row)
        result = jnp.dot(window[...], wb[...], preferred_element_type=jnp.float32)
        for position in range(4):
            reduced[step, position] = result[position * PIECE : (position + 1) * PIECE, :]

        @pl.when(step == 0)
        def _():
            for order in range(4):
                far_out[order] = narrow(reduced[0, place_of(order)])
                low = pl.ds(0, HALF)
                copies.remote(
                    21 + order, far_out.at[order, low, :], far_in.at[order, low, :], s_up
                ).start()
                high = pl.ds(HALF, HALF)
                copies.remote(
                    33 + order, far_out.at[order, high, :], far_in.at[order, high, :], s_down
                ).start()

        @pl.when(step == 2)
        def _():
            for order in range(4):
                at = place_of(order)
                low = pl.ds(0, HALF)
                high = pl.ds(HALF, HALF)
                up_out[order, high, :] = narrow(reduced[1, at, high, :])
                down_out[order, low, :] = narrow(reduced[2, at, low, :])
                copies.arrived(21 + order, far_in.at[order, low, :], s_up)
                up_out[order, low, :] = narrow(
                    reduced[1, at, low, :] + far_in[order, low, :].astype(jnp.float32)
                )
                copies.remote(25 + order, up_out.at[order], up_in.at[order], s_up).start()
                copies.arrived(33 + order, far_in.at[order, high, :], s_down)
                down_out[order, high, :] = narrow(
                    reduced[2, at, high, :] + far_in[order, high, :].astype(jnp.float32)
                )
                copies.remote(29 + order, down_out.at[order], down_in.at[order], s_down).start()

        if backward:

            @pl.when(step >= 2)
            def _():
                fill_chunk(xf, row)
                add_gradient()

            @pl.when(step == 3)
            def _():
                for turn in (2, 1):
                    fill_window(padded, (second + turn) % 4)
                    fill_chunk(xf, (second + turn) % 4)
                    add_gradient()

        return carry

    lax.fori_loop(0, 4, spread, 0)
    for order in range(4):
        low = pl.ds(0, HALF)
        half = far_out.at[order, low, :]
        copies.sent.append(copies.remote(21 + order, half, half, s_up))
        copies.sent.append(copies.remote(33 + order, half, half, s_down))
        copies.sent.append(copies.remote(25 + order, up_out.at[order], up_in.at[order], s_up))
        copies.sent.append(copies.remote(29 + order, down_out.at[order], down_in.at[order], s_down))
    if backward:
        hand_over(1)
        depth_near(0)

    def arrive_second(order):
        copies.arrived(25 + order, up_in.at[order], s_up)
        copies.arrived(29 + order, down_in.at[order], s_down)

    def gathered(order, low, length):
        rows = pl.ds(low, length)
        return (
            reduced[3, place_of(order), rows, :]
            + up_in[order, rows, :].astype(jnp.float32)
            + down_in[order, rows, :].astype(jnp.float32)
        )

    arrive_second(0)
    far2_out[0] = narrow(gathered(0, 0, HALF))
    copies.start(52, far2_out.at[0], far2_in.at[0], f_up)
    far2_out[1] = narrow(gathered(0, HALF, HALF))
    copies.start(53, far2_out.at[1], far2_in.at[1], f_down)
    if backward:
        depth_far(1)
    arrive_second(1)
    up2_out[HALF:, :] = narrow(gathered(1, HALF, HALF))
    copies.arrived(52, far2_in.at[0], f_up)
    up2_out[:HALF, :] = narrow(gathered(1, 0, HALF) + far2_in[0].astype(jnp.float32))
    copies.start(54, up2_out, up2_in, f_up)
    arrive_second(2)
    down2_out[:HALF, :] = narrow(gathered(2, 0, HALF))
    copies.arrived(53, far2_in.at[1], f_down)
    down2_out[HALF:, :] = narrow(gathered(2, HALF, HALF) + far2_in[1].astype(jnp.float32))
    copies.start(55, down2_out, down2_in, f_down)
    if backward:
        depth_near(1)
    arrive_second(3)
    copies.arrived(54, up2_in, f_up)
    copies.arrived(55, down2_in, f_down)

    def settled(which):
        rows = pl.ds(pl.multiple_of(which * HALF, 32), HALF)
        return (
            reduced[3, first, rows, :]
            + up_in[3, rows, :].astype(jnp.float32)
            + down_in[3, rows, :].astype(jnp.float32)
            + up2_in[rows, :].astype(jnp.float32)
            + down2_in[rows, :].astype(jnp.float32)
        )

    swap_out[...] = narrow(settled(1 - core))
    copies.start(37, swap_out, swap_in, partner)
    out_ref[core] = narrow(x_ref[core].astype(jnp.float32) + settled(core))
    copies.arrived(37, swap_in, partner)
    out_ref[1 - core] = narrow(x_ref[1 - core].astype(jnp.float32) + swap_in[...].astype(jnp.float32))
    if backward:
        depth_own(0, ge_ref)
        depth_own(1, gf_ref)
    copies.finish()
    for store in stores:
        store.wait()


def bottleneck(backward, *operands):
    b16, f32 = jnp.bfloat16, jnp.float32
    vmem = pl.BlockSpec(memory_space=pltpu.VMEM)
    anywhere = pl.BlockSpec(memory_space=pl.ANY)
    padded_rows = SPOTS + 2 * ACROSS
    shape = jax.ShapeDtypeStruct
    out = shape((2, HALF, PART), b16)
    if backward:
        grad = shape((9 * INNER // 2, PART // 2), f32)
        in_specs = [anywhere] * 5 + [vmem] * 6
        out_shape = [out, grad, grad, shape((HALF, PART), b16), shape((INNER, INNER), f32)]
        out_specs = [vmem] * 5
    else:
        in_specs = [vmem] * 3 + [anywhere] * 2
        out_shape = [
            out,
            shape((SPOTS, INNER), f32),
            shape((padded_rows, WIDE_ROWS), b16),
            shape((SPOTS, PART), b16),
            shape((PART, 9 * INNER), b16),
            shape((9 * INNER, PART), b16),
            shape((HALF, PART), b16),
            shape((HALF, PART), f32),
            shape((4 * HALF, 9 * INNER), b16),
        ]
        out_specs = [vmem] + [anywhere] * 5 + [vmem] * 3
    scratch = [
        pltpu.VMEM((SPOTS, PART), b16),
        pltpu.VMEM((PART, 9 * INNER), b16),
        pltpu.VMEM((9 * INNER, PART), b16),
        pltpu.VMEM((padded_rows, WIDE_ROWS), f32),
        pltpu.VMEM((SPOTS, INNER), f32),
        pltpu.VMEM((SPOTS, INNER), f32),
        pltpu.VMEM((padded_rows, WIDE_ROWS), b16),
        pltpu.VMEM((4 * PIECE, PART), b16),
        pltpu.VMEM((4 * PIECE, 9 * INNER), b16),
        *[pltpu.VMEM((4, PIECE, PART), b16) for _ in range(6)],
        pltpu.VMEM((4, 4, PIECE, PART), f32),
        pltpu.VMEM((2, HALF, PART), b16),
        pltpu.VMEM((PIECE, PART), b16),
        pltpu.VMEM((PIECE, PART), b16),
        pltpu.VMEM((2, HALF, PART), b16),
        pltpu.VMEM((PIECE, PART), b16),
        pltpu.VMEM((PIECE, PART), b16),
        pltpu.VMEM((HALF, PART), b16),
        pltpu.VMEM((HALF, PART), b16),
        pltpu.VMEM((2, HALF, PART), b16),
        pltpu.SemaphoreType.DMA((60,)),
        pltpu.SemaphoreType.DMA((60,)),
        pltpu.SemaphoreType.DMA((5,)),
    ]
    if backward:
        scratch += [
            pltpu.VMEM((SPOTS, INNER), f32),
            pltpu.VMEM((padded_rows, WIDE_ROWS), b16),
            pltpu.VMEM((SPOTS, PART), b16),
            pltpu.VMEM((9 * INNER, PART), f32),
            pltpu.VMEM((2, 2, 576, PART), b16),
            pltpu.VMEM((2, 576, PART), b16),
            pltpu.VMEM((2, 2, 288, 256), b16),
            *[pltpu.VMEM((2, 576, 256), b16) for _ in range(4)],
        ]
    else:
        scratch += [
            pltpu.VMEM((2, 9, PART, INNER // 2), b16),
            pltpu.VMEM((9, INNER, PART), b16),
            pltpu.VMEM((PART, 9 * INNER), b16),
            pltpu.VMEM((9 * INNER, PART), b16),
            pltpu.VMEM((2, 2, ACROSS, INNER), b16),
            pltpu.VMEM((4, 6 * ACROSS, INNER), b16),
        ]
    return pl.pallas_call(
        functools.partial(phase_kernel, backward),
        out_shape=out_shape,
        in_specs=in_specs,
        out_specs=out_specs,
        scratch_shapes=scratch,
        compiler_params=pltpu.CompilerParams(
            collective_id=2 if backward else 1,
            has_side_effects=True,
            vmem_limit_bytes=60 * 1024 * 1024,
        ),
        name="backward_phase" if backward else "forward_phase",
    )(*operands)


SUM_ROWS = 1280


def sum_kernel(stacked_ref, coarse_grad_ref, bottom_ref, upward_grad_ref, down_weight_ref,
               hidden_pre_ref, taps_ref, class_ref, out_ref, total, give, pair_in, a_out, a_in,
               b_out, b_in, z_out, z_in, result, conv_ref, send_sems, recv_sems):
    core, first, second = place()
    depth = lax.axis_index("samp")
    me = block_of(core, first, second)
    partner = {"wide": me * 2 + 1 - core}
    first_peers = [
        {"wide": block_of(core, (first + d) % 4, second) * 2 + core} for d in range(4)
    ]
    second_peers = [
        {"wide": block_of(core, first, (second + d) % 4) * 2 + core} for d in range(4)
    ]
    depth_peers = [{"samp": (depth + d) % 4} for d in range(4)]
    copies = Copies(send_sems, recv_sems)
    barrier = pltpu.get_barrier_semaphore()
    for device in [partner, *first_peers[1:], *second_peers[1:], *depth_peers[1:]]:
        pl.semaphore_signal(
            barrier, inc=1, device_id=device, device_id_type=pl.DeviceIdType.MESH
        )

    def own_lanes(half, width):
        return pl.ds(pl.multiple_of(half * width, 128), width)

    down_back = contract_last(coarse_grad_ref[0], down_weight_ref[:, 0:PART]) + contract_last(
        coarse_grad_ref[1], down_weight_ref[:, PART:]
    )
    hidden_grad = (down_back + upward_grad_ref[...].astype(jnp.float32)) * silu_slope(
        hidden_pre_ref[...]
    )
    conv_ref[...] = contract_first(taps_ref[...], stacked_up(hidden_grad.astype(jnp.bfloat16)))

    def pack(half, to, kind):
        to[0:512, :] = contract_first(stacked_ref[...], coarse_grad_ref[half]).astype(kind)
        to[512:1024, :] = contract_first(bottom_ref[half], upward_grad_ref[...]).astype(kind)
        for piece in range(4):
            rows = pl.ds(pl.multiple_of((half * 4 + piece) * 144, 16), 144)
            to[1024:1168, piece * 128 : (piece + 1) * 128] = conv_ref[rows, :].astype(kind)
            rows = slice(piece * 32, (piece + 1) * 32)
            to[1168:1200, piece * 128 : (piece + 1) * 128] = class_ref[rows, :].astype(kind)
        to[1200:, :] = jnp.zeros((SUM_ROWS - 1200, PART), kind)

    def spot(at_first, at_second):
        base = (at_first % 4) * 320 + (at_second % 4) * 80
        return pl.ds(pl.multiple_of(base, 16), 80)

    order = (2, 1, 3, 0)
    pack(1 - core, give, jnp.bfloat16)
    pl.semaphore_wait(barrier, 10)
    for i, ds in enumerate(order):
        for df in range(4):
            part = spot(second + df, first + ds)
            copies.start(i * 4 + df, give.at[part, :], pair_in.at[part, :], partner)
    pack(core, total, jnp.float32)
    for i, ds in enumerate(order):
        for df in range(1, 4):
            part = spot(first + df, second + ds)
            copies.arrived(i * 4 + df, pair_in.at[part, :], partner)
            a_out[df, i] = (total[part, :] + pair_in[part, :].astype(jnp.float32)).astype(
                jnp.bfloat16
            )
            copies.start(16 + i * 3 + df - 1, a_out.at[df, i], a_in.at[df, i], first_peers[df])

    def after_first(i):
        part = spot(first, second + order[i])
        copies.arrived(i * 4, pair_in.at[part, :], partner)
        value = total[part, :] + pair_in[part, :].astype(jnp.float32)
        for df in range(1, 4):
            copies.arrived(16 + i * 3 + df - 1, a_in.at[df, i], first_peers[df])
            value = value + a_in[df, i].astype(jnp.float32)
        return value

    for i in range(3):
        b_out[i] = after_first(i).astype(jnp.bfloat16)
        copies.start(28 + i, b_out.at[i], b_in.at[i], second_peers[order[i]])
    total[0:80, :] = after_first(3)
    for i in range(3):
        copies.arrived(28 + i, b_in.at[i], second_peers[order[i]])
        total[0:80, :] += b_in[i].astype(jnp.float32)
    for d in range(1, 4):
        z_out[d] = total[0:80, own_lanes((depth + d) % 4, 128)].astype(jnp.bfloat16)
        copies.start(30 + d, z_out.at[d], z_in.at[d], depth_peers[d])
    value = total[0:80, own_lanes(depth, 128)]
    for d in range(1, 4):
        copies.arrived(30 + d, z_in.at[d], depth_peers[d])
        value = value + z_in[d].astype(jnp.float32)

    def at_depth(d):
        return result.at[core, spot(first, second), own_lanes((depth + d) % 4, 128)]

    def at(df, ds, half):
        return result.at[half, spot(first + df, second + ds), :]

    def pass_on(df, ds):
        copies.start(52 + df * 4 + ds, at(df, ds, core), at(df, ds, core), partner)

    def along_first(ds):
        for df in range(1, 4):
            copies.start(40 + ds * 3 + df - 1, at(0, ds, core), at(0, ds, core), first_peers[df])

    at_depth(0)[...] = value.astype(jnp.bfloat16)
    for d in range(1, 4):
        copies.start(33 + d, at_depth(0), at_depth(0), depth_peers[d])
    for d in range(1, 4):
        copies.arrived(33 + d, at_depth(4 - d), depth_peers[d])
    for ds in range(1, 4):
        copies.start(36 + ds, at(0, 0, core), at(0, 0, core), second_peers[ds])
    along_first(0)
    pass_on(0, 0)
    for ds in (1, 3, 2):
        copies.arrived(36 + ds, at(0, 4 - ds, core), second_peers[ds])
        along_first(4 - ds)
        pass_on(0, 4 - ds)
    for ds in (0, 3, 1, 2):
        for df in (1, 3, 2):
            copies.arrived(40 + ds * 3 + df - 1, at(4 - df, ds, core), first_peers[df])
            pass_on(4 - df, ds)
    out_ref[core] = result[core]
    for df in range(4):
        for ds in range(4):
            copies.arrived(52 + df * 4 + ds, at(df, ds, 1 - core), partner)
    out_ref[1 - core] = result[1 - core]
    copies.finish()


def sum_everywhere(*operands):
    b16, f32 = jnp.bfloat16, jnp.float32
    vmem = pl.BlockSpec(memory_space=pltpu.VMEM)
    out = pl.pallas_call(
        sum_kernel,
        out_shape=jax.ShapeDtypeStruct((2, SUM_ROWS, PART), b16),
        in_specs=[vmem] * 8,
        out_specs=vmem,
        scratch_shapes=[
            pltpu.VMEM((SUM_ROWS, PART), f32),
            pltpu.VMEM((SUM_ROWS, PART), b16),
            pltpu.VMEM((SUM_ROWS, PART), b16),
            pltpu.VMEM((4, 4, 80, PART), b16),
            pltpu.VMEM((4, 4, 80, PART), b16),
            pltpu.VMEM((3, 80, PART), b16),
            pltpu.VMEM((3, 80, PART), b16),
            pltpu.VMEM((4, 80, 128), b16),
            pltpu.VMEM((4, 80, 128), b16),
            pltpu.VMEM((2, SUM_ROWS, PART), b16),
            pltpu.VMEM((9 * INNER, INNER), f32),
            pltpu.SemaphoreType.DMA((68,)),
            pltpu.SemaphoreType.DMA((68,)),
        ],
        compiler_params=pltpu.CompilerParams(
            collective_id=3, has_side_effects=True, vmem_limit_bytes=60 * 1024 * 1024
        ),
        name="sum_everywhere",
    )(*operands)
    down = jnp.concatenate([out[0, 0:512], out[1, 0:512]], axis=1).astype(f32)
    up = out[:, 512:1024].astype(f32).reshape(2 * PART, PART)
    conv = jnp.concatenate(
        [out[h, 1024:1168, i * 128 : (i + 1) * 128] for h in range(2) for i in range(4)], axis=0
    )
    conv = conv.astype(f32).reshape(3, 3, INNER, INNER)
    small = jnp.concatenate([out[0, 1168:1200, i * 128 : i * 128 + 9] for i in range(4)], axis=0)
    return conv, down, up, small.astype(f32)


def local(
    features,
    labels,
    conv_weight,
    down_weight,
    expand_weight,
    reduce_weight,
    up_weight,
    class_weight,
):
    height, across, channels = features.shape[1:]
    count = class_weight.shape[1]
    columns = jnp.transpose(features.reshape(height, across // 2, 2, channels), (2, 0, 1, 3))
    places = jnp.transpose(labels.reshape(height // 2, 2, across // 2, 2), (1, 3, 0, 2))
    places = places.reshape(height * across, 1)
    class_wide = jnp.pad(class_weight, ((0, 0), (0, INNER - count)))
    class_tall = jnp.pad(class_weight.T, ((0, INNER - count), (0, 0)))
    bottom, pre, expanded, coarse, wa_back, wb_back, stacked, hidden_pre, taps = bottleneck(
        False,
        columns,
        conv_weight.reshape(9 * INNER, INNER),
        down_weight,
        expand_weight.reshape(9, 2 * PART, INNER // 2),
        reduce_weight.reshape(9, INNER // 2, 2 * PART),
    )
    coarse_grad, reduce_grad, expand_grad, upward_grad, class_grad = bottleneck(
        True, wa_back, wb_back, pre, expanded, coarse, bottom, stacked, places, up_weight,
        class_wide, class_tall,
    )
    conv_grad, down_grad, up_grad, class_grad = sum_everywhere(
        stacked, coarse_grad, bottom, upward_grad, down_weight, hidden_pre, taps, class_grad
    )
    reduce_grad = reduce_grad.reshape(3, 3, INNER // 2, -1)
    expand_grad = jnp.transpose(expand_grad.reshape(9, INNER // 2, -1)[::-1], (0, 2, 1))
    expand_grad = expand_grad.reshape(3, 3, -1, INNER // 2)
    return (conv_grad, down_grad, expand_grad, reduce_grad, up_grad, class_grad)


def solution(mesh):
    return jax.shard_map(
        local,
        mesh=mesh,
        in_specs=(
            P("samp", "wide", None, None),
            P("samp", "wide", None),
            P(),
            P(),
            P(None, None, None, "wide"),
            P(None, None, "wide", None),
            P(),
            P(),
        ),
        out_specs=(
            P(),
            P(),
            P(None, None, "samp", "wide"),
            P(None, None, "wide", "samp"),
            P(),
            P(),
        ),
        check_vma=False,
    )
```

```python
import functools
import math

import jax
import jax.numpy as jnp
from jax import lax
from jax.experimental import pallas as pl
from jax.experimental.pallas import tpu as pltpu
from jax.sharding import PartitionSpec as P


def silu_slope(value):
    logistic = jax.nn.sigmoid(value)
    return logistic * (1.0 + value * (1.0 - logistic))


ROWS = 64
ACROSS = 48
SPOTS = ROWS * ACROSS
PIECE = 192
HALF = 96
PART = 512
LANES = 256
INNER = 128
WIDE_ROWS = 3 * INNER


def place():
    wide = lax.axis_index("wide")
    core = wide % 2
    x = (wide // 2) % 4
    y = wide // 8
    first = x + core * (y - x)
    second = y + core * (x - y)
    return core, first % 4, second % 4


def block_of(core, first, second):
    x = first + core * (second - first)
    y = second + core * (first - second)
    return y * 4 + x


def rows_of(block, length=PIECE):
    return pl.ds(pl.multiple_of(block * PIECE, 64), length)


def edge_masks(length):
    column = lax.broadcasted_iota(jnp.int32, (length, INNER), 0) % ACROSS
    return column == 0, column == ACROSS - 1


def from_left(values, at_left):
    return jnp.where(at_left, 0.0, pltpu.roll(values, 1, axis=0))


def from_right(values, at_right):
    return jnp.where(at_right, 0.0, pltpu.roll(values, values.shape[0] - 1, axis=0))


class Copies:
    def __init__(self, send_sems, recv_sems):
        self.send_sems = send_sems
        self.recv_sems = recv_sems
        self.sent = []

    def remote(self, index, source, target, device):
        copy = pltpu.make_async_remote_copy(
            src_ref=source,
            dst_ref=target,
            send_sem=self.send_sems.at[index],
            recv_sem=self.recv_sems.at[index],
            device_id=device if isinstance(device, dict) else {"wide": device},
            device_id_type=pl.DeviceIdType.MESH,
        )
        return copy

    def start(self, index, source, target, device):
        copy = self.remote(index, source, target, device)
        copy.start()
        self.sent.append(copy)

    def arrived(self, index, target, device):
        self.remote(index, target, target, device).wait_recv()

    def finish(self):
        for copy in self.sent:
            copy.wait_send()


def contract_first(left, right):
    return lax.dot_general(left, right, (((0,), (0,)), ((), ())), preferred_element_type=jnp.float32)


def contract_last(left, right):
    return lax.dot_general(left, right, (((1,), (1,)), ((), ())), preferred_element_type=jnp.float32)


def multiply(left, right):
    return jnp.dot(left, right, preferred_element_type=jnp.float32)


def side_by_side(tall):
    return jnp.concatenate([tall[i * HALF : (i + 1) * HALF] for i in range(4)], axis=1)


def stacked_up(flat):
    return jnp.concatenate([flat[:, i * INNER : (i + 1) * INNER] for i in range(4)], axis=0)


def first_layers(wide, copies, after, before, feature_ref, halo, columns, conv_weight_ref,
                 taps_ref, hidden_pre_ref, stacked_ref, x_ref, spread_rows):
    at_left, at_right = edge_masks(ACROSS)

    def row_columns(row, values):
        spread_rows[pl.ds(row * 2 * ACROSS, 2 * ACROSS), :] = values
        even = spread_rows[pl.ds(row * 2 * ACROSS, ACROSS, stride=2), :]
        odd = spread_rows[pl.ds(row * 2 * ACROSS + 1, ACROSS, stride=2), :]
        to = pl.ds(row * ACROSS, ACROSS)
        columns[0, to, :] = from_left(odd, at_left).astype(jnp.bfloat16)
        columns[1, to, :] = even.astype(jnp.bfloat16)
        columns[2, to, :] = odd.astype(jnp.bfloat16)
        columns[3, to, :] = from_right(even, at_right).astype(jnp.bfloat16)

    for row in range(4):
        row_columns(row + 1, feature_ref[row].astype(jnp.float32))
    copies.arrived(56, halo.at[0], after)
    copies.arrived(57, halo.at[1], before)
    row_columns(0, halo[0].astype(jnp.float32) * jnp.where(wide > 0, 1.0, 0.0))
    row_columns(5, halo[1].astype(jnp.float32) * jnp.where(wide < 31, 1.0, 0.0))
    for a in range(2):
        for b in range(2):
            for i in range(2):
                for p in range(3):
                    for q in range(3):
                        low = (a * 2 + b) * HALF + i * ACROSS
                        source = (a + p + 2 * i) * ACROSS
                        tap = (p * 3 + q) * INNER
                        taps_ref[low : low + ACROSS, tap : tap + INNER] = columns[
                            b + q, source : source + ACROSS, :
                        ]
    hidden_pre = multiply(taps_ref[...], conv_weight_ref[...])
    hidden_pre = side_by_side(hidden_pre)
    hidden_pre_ref[...] = hidden_pre
    stacked = jax.nn.silu(hidden_pre).astype(jnp.bfloat16)
    stacked_ref[...] = stacked
    for half in range(2):
        x_ref[half] = stacked[:, half * LANES : (half + 1) * LANES]


def label_column(labels):
    values = labels.astype(jnp.float32).astype(jnp.bfloat16)
    to = lax.broadcasted_iota(jnp.int32, (ACROSS, HALF), 0)
    source = lax.broadcasted_iota(jnp.int32, (ACROSS, HALF), 1)
    pieces = []
    picked = [
        contract_last((source == 2 * to + b).astype(jnp.float32).astype(jnp.bfloat16), values)
        for b in range(2)
    ]
    for a in range(2):
        for b in range(2):
            for i in range(2):
                row = a + 2 * i
                pieces.append(picked[b][:, row : row + 1])
    return jnp.concatenate(pieces, axis=0)


def middle(coarse_ref, inner_ref, stacked_ref, label_ref, up_weight_ref, class_ref,
           x_ref, upward_grad_ref, class_grad_ref):
    loss_scale = 8.0 / math.sqrt(49152)
    upward = multiply(coarse_ref[0], up_weight_ref[0:PART, :]) + multiply(
        coarse_ref[1], up_weight_ref[PART:, :]
    )
    upward = upward + jnp.concatenate([inner_ref[0], inner_ref[1]], axis=1)
    joined_pre = stacked_up(upward + stacked_ref[...].astype(jnp.float32))
    joined = jax.nn.silu(joined_pre).astype(jnp.bfloat16)
    logits = contract_last(joined, class_ref[...])
    classes = lax.broadcasted_iota(jnp.int32, logits.shape, 1)
    exp_logits = jnp.exp(logits)
    probability = exp_logits / jnp.sum(exp_logits, axis=1, keepdims=True)
    onehot = (label_column(label_ref[...]) == classes.astype(jnp.float32)).astype(jnp.float32)
    logit_grad = ((probability - onehot) * loss_scale).astype(jnp.bfloat16)
    joined_grad = multiply(logit_grad, class_ref[...])
    upward_grad = side_by_side((joined_grad * silu_slope(joined_pre)).astype(jnp.bfloat16))
    upward_grad_ref[...] = upward_grad
    for half in range(2):
        x_ref[half] = upward_grad[:, half * LANES : (half + 1) * LANES]
    class_grad_ref[...] = contract_first(logit_grad, joined)


def phase_kernel(backward, *refs):
    if backward:
        (
            wa_hbm, wb_hbm, pre_hbm, ef_hbm, xf_hbm, coarse_ref, inner_ref, stacked_ref, label_ref,
            up_weight_ref, down_weight_ref, class_ref,
            out_ref, ge_ref, gf_ref, upward_grad_ref, class_grad_ref, bottom_grad_ref, joint_ref,
        ) = refs[:19]
        scratch = refs[19:]
    else:
        (
            feature_ref, conv_weight_ref, down_weight_ref, up_weight_ref, expand_hbm, reduce_hbm,
            out_ref, pre_hbm, ef_hbm, xf_hbm, wa_hbm, wb_hbm, expand_tall_hbm, stacked_ref,
            hidden_pre_ref, taps_ref, coarse_ref,
        ) = refs[:17]
        scratch = refs[17:]
    (
        xall, wa, wb, total, pre, other, padded, chunk, window,
        far_out, up_out, down_out, far_in, up_in, down_in, reduced,
        far2_out, up2_out, down2_out, far2_in, up2_in, down2_in, swap_out, swap_in,
        x_ref, send_sems, recv_sems, local_sems,
    ) = scratch[:28]
    core, first, second = place()
    me = block_of(core, first, second)
    partner = me * 2 + 1 - core
    f_up = block_of(core, (first + 1) % 4, second) * 2 + core
    f_down = block_of(core, (first + 3) % 4, second) * 2 + core
    s_up = block_of(core, first, (second + 1) % 4) * 2 + core
    s_down = block_of(core, first, (second + 3) % 4) * 2 + core
    copies = Copies(send_sems, recv_sems)

    if backward:
        loads = [
            pltpu.make_async_copy(wa_hbm, wa, local_sems.at[0]),
            pltpu.make_async_copy(wb_hbm, wb, local_sems.at[1]),
        ]
        pre_f, ef, xf, grad, full, give, zfar_in, zup_out, zdown_out, zup_in, zdown_in, joint = scratch[28:]
        loads += [
            pltpu.make_async_copy(pre_hbm, pre_f, local_sems.at[2]),
            pltpu.make_async_copy(ef_hbm, ef, local_sems.at[3]),
            pltpu.make_async_copy(xf_hbm, xf, local_sems.at[4]),
        ]
    else:
        expand_both, reduce_both, wa_back, wb_back, halo, columns, expand_tall, spread_rows = scratch[28:]
        lanes = pl.ds(pl.multiple_of(core * LANES, LANES), LANES)
        own_rows = pl.ds(pl.multiple_of(core * 64, 64), 64)
        loads = [
            pltpu.make_async_copy(
                expand_hbm, expand_both.at[:, own_rows, :], local_sems.at[0]
            ),
            pltpu.make_async_copy(
                reduce_hbm, reduce_both.at[:, own_rows, :], local_sems.at[1]
            ),
        ]
    for load in loads:
        load.start()

    peers = [{"wide": device} for device in (partner, f_up, f_down, s_up, s_down)]
    if backward:
        depth = lax.axis_index("samp")
        z_up = {"samp": (depth + 1) % 4}
        z_down = {"samp": (depth + 3) % 4}
        peers += [z_up, z_down]
    else:
        wide = lax.axis_index("wide")
        after = {"wide": (wide + 1) % 32}
        before = {"wide": (wide + 31) % 32}
        peers += [after, before]
    barrier = pltpu.get_barrier_semaphore()
    for device in peers:
        pl.semaphore_signal(
            barrier, inc=1, device_id=device, device_id_type=pl.DeviceIdType.MESH
        )
    if backward:
        middle(
            coarse_ref, inner_ref, stacked_ref, label_ref, up_weight_ref, class_ref,
            x_ref, upward_grad_ref, class_grad_ref,
        )
    pl.semaphore_wait(barrier, len(peers))
    if not backward:
        copies.start(56, feature_ref.at[3], halo.at[0], after)
        copies.start(57, feature_ref.at[0], halo.at[1], before)
        copies.start(58, expand_hbm, expand_both.at[:, own_rows, :], partner)
        copies.start(59, reduce_hbm, reduce_both.at[:, own_rows, :], partner)
        first_layers(
            wide, copies, after, before, feature_ref, halo, columns, conv_weight_ref,
            taps_ref, hidden_pre_ref, stacked_ref, x_ref, spread_rows,
        )

    mine = pl.ds(pl.multiple_of(me * PIECE + core * HALF, 32), HALF)
    theirs = pl.ds(pl.multiple_of(me * PIECE + (1 - core) * HALF, 32), HALF)
    copies.start(0, x_ref.at[1 - core], xall.at[mine, :], partner)
    xall[mine, :] = x_ref[core]
    copies.arrived(0, xall.at[theirs, :], partner)

    def piece(first_at, second_at, low=0, length=PIECE):
        block = block_of(core, first_at % 4, second_at % 4)
        return xall.at[pl.ds(pl.multiple_of(block * PIECE + low, 32), length), :]

    def send_second(order, first_at):
        copies.start(5 + order, piece(first_at, second), piece(first_at, second), s_up)
        copies.start(9 + order, piece(first_at, second), piece(first_at, second), s_down)

    own = piece(first, second)
    copies.start(1, own, own, f_up)
    copies.start(2, own, own, f_down)
    send_second(0, first)

    def clear(step, carry):
        total[pl.ds(pl.multiple_of(step * 96, 32), 96), :] = jnp.zeros((96, WIDE_ROWS), jnp.float32)
        return carry

    def clear_grad(step, carry):
        grad[pl.ds(pl.multiple_of(step * INNER, 128), INNER), :] = jnp.zeros((INNER, LANES), jnp.float32)
        return carry

    def add_gradient():
        grad[...] += lax.dot_general(
            window[...], chunk[...], (((0,), (0,)), ((), ())), preferred_element_type=jnp.float32
        )

    def fill_window(source, row):
        for position in range(4):
            block = block_of(core, position, row)
            for p in range(3):
                window[
                    position * PIECE : (position + 1) * PIECE, p * WIDE_ROWS : (p + 1) * WIDE_ROWS
                ] = source[pl.ds(pl.multiple_of(block * PIECE + p * ACROSS, 16), PIECE), :]

    def fill_chunk(source, row):
        for position in range(4):
            block = block_of(core, position, row)
            chunk[position * PIECE : (position + 1) * PIECE, :] = source[rows_of(block), :]

    def hand_over(which):
        def pack(tap, carry):
            to = pl.ds(pl.multiple_of(tap * 64, 64), 64)
            own_rows = pl.ds(pl.multiple_of(tap * INNER + core * 64, 64), 64)
            other_rows = pl.ds(pl.multiple_of(tap * INNER + (1 - core) * 64, 64), 64)
            joint[which, core, to, :] = grad[own_rows, :].astype(jnp.bfloat16)
            give[which, to, :] = grad[other_rows, :].astype(jnp.bfloat16)
            return carry

        lax.fori_loop(0, 9, pack, 0)
        copies.start(38 + which, give.at[which], joint.at[which, core], partner)

    def share(which, at, low, length):
        at = at % 4
        lanes = pl.ds(pl.multiple_of((at % 2) * 256, 256), 256)
        return full.at[which, at // 2, pl.ds(low, length), lanes]

    def depth_far(which):
        copies.arrived(38 + which, joint.at[which, 1 - core], partner)
        both = jnp.concatenate([joint[which, 0], joint[which, 1]], axis=1)
        joint_ref[which] = both
        for half in range(2):
            part = slice(half * PART, (half + 1) * PART)
            if which == 0:
                full[which, half] = narrow(contract_last(both, up_weight_ref[part, :]))
            else:
                full[which, half] = narrow(multiply(both, down_weight_ref[:, part]))
        copies.start(40 + which, share(which, depth + 2, 0, 288), zfar_in.at[which, 0], z_up)
        copies.start(42 + which, share(which, depth + 2, 288, 288), zfar_in.at[which, 1], z_down)

    def depth_near(which):
        near = share(which, depth + 1, 288, 288)[...]
        zup_out[which, 288:576, :] = near
        near = share(which, depth + 3, 0, 288)[...]
        zdown_out[which, 0:288, :] = near
        copies.arrived(40 + which, zfar_in.at[which, 0], z_up)
        near = share(which, depth + 1, 0, 288)[...].astype(jnp.float32)
        zup_out[which, 0:288, :] = narrow(near + zfar_in[which, 0].astype(jnp.float32))
        copies.start(44 + which, zup_out.at[which], zup_in.at[which], z_up)
        copies.arrived(42 + which, zfar_in.at[which, 1], z_down)
        near = share(which, depth + 3, 288, 288)[...].astype(jnp.float32)
        zdown_out[which, 288:576, :] = narrow(near + zfar_in[which, 1].astype(jnp.float32))
        copies.start(46 + which, zdown_out.at[which], zdown_in.at[which], z_down)

    def depth_own(which, out):
        copies.arrived(44 + which, zup_in.at[which], z_up)
        copies.arrived(46 + which, zdown_in.at[which], z_down)
        out[...] = (
            share(which, depth, 0, 576)[...].astype(jnp.float32)
            + zup_in[which].astype(jnp.float32)
            + zdown_in[which].astype(jnp.float32)
        )

    def narrow(values):
        return values.astype(jnp.bfloat16)

    lax.fori_loop(0, 33, clear, 0)
    if backward:
        lax.fori_loop(0, 9, clear_grad, 0)
    padded[0:ACROSS, :] = jnp.zeros((ACROSS, WIDE_ROWS), jnp.bfloat16)
    padded[SPOTS + ACROSS :, :] = jnp.zeros((ACROSS, WIDE_ROWS), jnp.bfloat16)

    offsets = (0, 3, 1, 2)

    def relay(order):
        first_at = first + offsets[order]
        here = piece(first_at, second + 3)
        copies.arrived(5 + order, here, s_up)
        low = piece(first_at, second + 3, 0, HALF)
        copies.start(13 + order, low, low, s_up)
        here = piece(first_at, second + 1)
        copies.arrived(9 + order, here, s_down)
        high = piece(first_at, second + 1, HALF, HALF)
        copies.start(48 + order, high, high, s_down)

    for load in loads:
        load.wait()
    if not backward:
        partner_rows = pl.ds(pl.multiple_of((1 - core) * 64, 64), 64)
        copies.arrived(58, expand_both.at[:, partner_rows, :], partner)
        copies.arrived(59, reduce_both.at[:, partner_rows, :], partner)
        share_rows = down_weight_ref[pl.ds(pl.multiple_of(core * LANES, LANES), LANES), :]
        joined_weight = narrow(
            contract_last(expand_both[...].reshape(9 * INNER, 2 * PART), share_rows)
        )
        for tap in range(9):
            block = joined_weight[tap * INNER : (tap + 1) * INNER, :]
            wa[:, tap * INNER : (tap + 1) * INNER] = block.T
            wb_back[(8 - tap) * INNER : (9 - tap) * INNER, :] = block
            expand_tall[(8 - tap) * 64 : (9 - tap) * 64, :] = expand_both[tap, own_rows, :]

    left = piece(first + 3, second)
    right = piece(first + 1, second)
    copies.arrived(1, left, f_up)
    low = piece(first + 3, second, 0, HALF)
    copies.start(3, low, low, f_up)
    send_second(1, first + 3)
    copies.arrived(2, right, f_down)
    high = piece(first + 1, second, HALF, HALF)
    copies.start(4, high, high, f_down)
    send_second(2, first + 1)
    relay(0)
    copies.arrived(3, piece(first + 2, second, 0, HALF), f_up)
    copies.arrived(4, piece(first + 2, second, HALF, HALF), f_down)
    send_second(3, first + 2)
    if not backward:
        wb[...] = narrow(
            multiply(
                reduce_both[...].reshape(9 * INNER, 2 * PART), up_weight_ref[:, lanes]
            )
        )
        for tap in range(9):
            here = slice(tap * INNER, (tap + 1) * INNER)
            back = slice((8 - tap) * INNER, (9 - tap) * INNER)
            wa_back[:, back] = wb[here, :].T
        for half in range(2):
            coarse_ref[half] = narrow(
                multiply(stacked_ref[...], down_weight_ref[:, half * PART : (half + 1) * PART])
            )
        stores = [
            pltpu.make_async_copy(wa_back, wa_hbm, local_sems.at[0]),
            pltpu.make_async_copy(wb_back, wb_hbm, local_sems.at[1]),
            pltpu.make_async_copy(expand_tall, expand_tall_hbm, local_sems.at[5]),
        ]
        for store in stores:
            store.start()
    else:
        stores = []
        for half in range(2):
            bottom_grad_ref[half] = narrow(
                contract_last(
                    upward_grad_ref[...], up_weight_ref[half * PART : (half + 1) * PART, :]
                )
            )

    def product(step, carry):
        turn = (3 * step + (step // 2) * (7 - 2 * step)) % 4

        @pl.when(step == 1)
        def _():
            for order in (1, 2, 3):
                first_at = first + offsets[order]
                copies.arrived(5 + order, piece(first_at, second + 3), s_up)
                low = piece(first_at, second + 3, 0, HALF)
                copies.remote(13 + order, low, low, s_up).start()
                copies.arrived(9 + order, piece(first_at, second + 1), s_down)
                high = piece(first_at, second + 1, HALF, HALF)
                copies.remote(48 + order, high, high, s_down).start()

        @pl.when(step == 3)
        def _():
            for order in range(4):
                first_at = first + offsets[order]
                copies.arrived(13 + order, piece(first_at, second + 2, 0, HALF), s_up)
                copies.arrived(48 + order, piece(first_at, second + 2, HALF, HALF), s_down)

        row = (second + turn) % 4
        fill_chunk(xall, row)
        result = jnp.dot(chunk[...], wa[...], preferred_element_type=jnp.float32)
        for position in range(4):
            block = block_of(core, position, row)
            for p in range(3):
                where = pl.ds(pl.multiple_of(block * PIECE + (2 - p) * ACROSS, 16), PIECE)
                total[where, :] += result[
                    position * PIECE : (position + 1) * PIECE, p * WIDE_ROWS : (p + 1) * WIDE_ROWS
                ]

        if backward:

            @pl.when(step < 3)
            def _():
                fill_window(ef, row)
                add_gradient()

        return carry

    lax.fori_loop(0, 4, product, 0)
    for order in (1, 2, 3):
        here = piece(first, second, 0, HALF)
        copies.sent.append(copies.remote(13 + order, here, here, s_up))
        copies.sent.append(copies.remote(48 + order, here, here, s_down))

    at_left, at_right = edge_masks(PIECE)

    def fold(step, carry):
        rows = rows_of(step)
        padded_rows = pl.ds(pl.multiple_of(step * PIECE + ACROSS, 16), PIECE)
        pre[rows, :] = (
            total[padded_rows, INNER : 2 * INNER]
            + from_left(total[padded_rows, 0:INNER], at_left)
            + from_right(total[padded_rows, 2 * INNER :], at_right)
        )
        return carry

    for quarter in range(4):
        lax.fori_loop(quarter * 4, quarter * 4 + 4, fold, 0)
        rows = pl.ds(quarter * 768, 768)
        copies.start(17 + quarter, pre.at[rows, :], other.at[rows, :], partner)

    if backward:
        fill_window(ef, (second + 2) % 4)
        add_gradient()
        hand_over(0)
        lax.fori_loop(0, 9, clear_grad, 0)

    def shape(step, carry):
        rows = rows_of(step)
        padded_rows = pl.ds(pl.multiple_of(step * PIECE + ACROSS, 16), PIECE)
        value = pre[rows, :] + other[rows, :]
        if backward:
            value = value * silu_slope(pre_f[rows, :])
        else:
            other[rows, :] = value
            value = jax.nn.silu(value)
        value = value.astype(jnp.bfloat16).astype(jnp.float32)
        padded[padded_rows, 0:INNER] = from_left(value, at_left).astype(jnp.bfloat16)
        padded[padded_rows, INNER : 2 * INNER] = value.astype(jnp.bfloat16)
        padded[padded_rows, 2 * INNER :] = from_right(value, at_right).astype(jnp.bfloat16)
        return carry

    for quarter in range(4):
        copies.arrived(17 + quarter, other.at[pl.ds(quarter * 768, 768), :], partner)
        lax.fori_loop(quarter * 4, quarter * 4 + 4, shape, 0)

    if not backward:
        more = [
            pltpu.make_async_copy(other, pre_hbm, local_sems.at[2]),
            pltpu.make_async_copy(padded, ef_hbm, local_sems.at[3]),
            pltpu.make_async_copy(xall, xf_hbm, local_sems.at[4]),
        ]
        for store in more:
            store.start()
        stores += more

    if backward:
        depth_far(0)

    def place_of(order):
        return (first + (2, 1, 3, 0)[order]) % 4

    def spread(step, carry):
        turn = (2 - step + (step // 2) * (7 - 2 * step)) % 4
        row = (second + turn) % 4
        fill_window(padded, row)
        result = jnp.dot(window[...], wb[...], preferred_element_type=jnp.float32)
        for position in range(4):
            reduced[step, position] = result[position * PIECE : (position + 1) * PIECE, :]

        @pl.when(step == 0)
        def _():
            for order in range(4):
                far_out[order] = narrow(reduced[0, place_of(order)])
                low = pl.ds(0, HALF)
                copies.remote(
                    21 + order, far_out.at[order, low, :], far_in.at[order, low, :], s_up
                ).start()
                high = pl.ds(HALF, HALF)
                copies.remote(
                    33 + order, far_out.at[order, high, :], far_in.at[order, high, :], s_down
                ).start()

        @pl.when(step == 2)
        def _():
            for order in range(4):
                at = place_of(order)
                low = pl.ds(0, HALF)
                high = pl.ds(HALF, HALF)
                up_out[order, high, :] = narrow(reduced[1, at, high, :])
                down_out[order, low, :] = narrow(reduced[2, at, low, :])
                copies.arrived(21 + order, far_in.at[order, low, :], s_up)
                up_out[order, low, :] = narrow(
                    reduced[1, at, low, :] + far_in[order, low, :].astype(jnp.float32)
                )
                copies.remote(25 + order, up_out.at[order], up_in.at[order], s_up).start()
                copies.arrived(33 + order, far_in.at[order, high, :], s_down)
                down_out[order, high, :] = narrow(
                    reduced[2, at, high, :] + far_in[order, high, :].astype(jnp.float32)
                )
                copies.remote(29 + order, down_out.at[order], down_in.at[order], s_down).start()

        if backward:

            @pl.when(step >= 2)
            def _():
                fill_chunk(xf, row)
                add_gradient()

            @pl.when(step == 3)
            def _():
                for turn in (2, 1):
                    fill_window(padded, (second + turn) % 4)
                    fill_chunk(xf, (second + turn) % 4)
                    add_gradient()

        return carry

    lax.fori_loop(0, 4, spread, 0)
    for order in range(4):
        low = pl.ds(0, HALF)
        half = far_out.at[order, low, :]
        copies.sent.append(copies.remote(21 + order, half, half, s_up))
        copies.sent.append(copies.remote(33 + order, half, half, s_down))
        copies.sent.append(copies.remote(25 + order, up_out.at[order], up_in.at[order], s_up))
        copies.sent.append(copies.remote(29 + order, down_out.at[order], down_in.at[order], s_down))
    if backward:
        hand_over(1)
        depth_near(0)

    def arrive_second(order):
        copies.arrived(25 + order, up_in.at[order], s_up)
        copies.arrived(29 + order, down_in.at[order], s_down)

    def gathered(order, low, length):
        rows = pl.ds(low, length)
        return (
            reduced[3, place_of(order), rows, :]
            + up_in[order, rows, :].astype(jnp.float32)
            + down_in[order, rows, :].astype(jnp.float32)
        )

    arrive_second(0)
    far2_out[0] = narrow(gathered(0, 0, HALF))
    copies.start(52, far2_out.at[0], far2_in.at[0], f_up)
    far2_out[1] = narrow(gathered(0, HALF, HALF))
    copies.start(53, far2_out.at[1], far2_in.at[1], f_down)
    if backward:
        depth_far(1)
    arrive_second(1)
    up2_out[HALF:, :] = narrow(gathered(1, HALF, HALF))
    copies.arrived(52, far2_in.at[0], f_up)
    up2_out[:HALF, :] = narrow(gathered(1, 0, HALF) + far2_in[0].astype(jnp.float32))
    copies.start(54, up2_out, up2_in, f_up)
    arrive_second(2)
    down2_out[:HALF, :] = narrow(gathered(2, 0, HALF))
    copies.arrived(53, far2_in.at[1], f_down)
    down2_out[HALF:, :] = narrow(gathered(2, HALF, HALF) + far2_in[1].astype(jnp.float32))
    copies.start(55, down2_out, down2_in, f_down)
    if backward:
        depth_near(1)
    arrive_second(3)
    copies.arrived(54, up2_in, f_up)
    copies.arrived(55, down2_in, f_down)

    def settled(which):
        rows = pl.ds(pl.multiple_of(which * HALF, 32), HALF)
        return (
            reduced[3, first, rows, :]
            + up_in[3, rows, :].astype(jnp.float32)
            + down_in[3, rows, :].astype(jnp.float32)
            + up2_in[rows, :].astype(jnp.float32)
            + down2_in[rows, :].astype(jnp.float32)
        )

    swap_out[...] = narrow(settled(1 - core))
    copies.start(37, swap_out, swap_in, partner)
    out_ref[core] = settled(core)
    copies.arrived(37, swap_in, partner)
    out_ref[1 - core] = swap_in[...].astype(jnp.float32)
    if backward:
        depth_own(0, ge_ref)
        depth_own(1, gf_ref)
    copies.finish()
    for store in stores:
        store.wait()


def bottleneck(backward, *operands):
    b16, f32 = jnp.bfloat16, jnp.float32
    vmem = pl.BlockSpec(memory_space=pltpu.VMEM)
    anywhere = pl.BlockSpec(memory_space=pl.ANY)
    padded_rows = SPOTS + 2 * ACROSS
    shape = jax.ShapeDtypeStruct
    out = shape((2, HALF, LANES), f32)
    pair = shape((2, HALF, PART), b16)
    if backward:
        grad = shape((9 * INNER // 2, PART // 2), f32)
        in_specs = [anywhere] * 5 + [vmem] * 7
        out_shape = [
            out, grad, grad, shape((HALF, PART), b16), shape((9, INNER), f32), pair,
            shape((2, 9 * INNER // 2, PART), b16),
        ]
        out_specs = [vmem] * 7
    else:
        in_specs = [vmem] * 4 + [anywhere] * 2
        out_shape = [
            out,
            shape((SPOTS, INNER), f32),
            shape((padded_rows, WIDE_ROWS), b16),
            shape((SPOTS, LANES), b16),
            shape((LANES, 9 * INNER), b16),
            shape((9 * INNER, LANES), b16),
            shape((9 * INNER // 2, 2 * PART), b16),
            shape((HALF, PART), b16),
            shape((HALF, PART), f32),
            shape((4 * HALF, 9 * INNER), b16),
            pair,
        ]
        out_specs = [vmem] + [anywhere] * 6 + [vmem] * 4
    scratch = [
        pltpu.VMEM((SPOTS, LANES), b16),
        pltpu.VMEM((LANES, 9 * INNER), b16),
        pltpu.VMEM((9 * INNER, LANES), b16),
        pltpu.VMEM((padded_rows, WIDE_ROWS), f32),
        pltpu.VMEM((SPOTS, INNER), f32),
        pltpu.VMEM((SPOTS, INNER), f32),
        pltpu.VMEM((padded_rows, WIDE_ROWS), b16),
        pltpu.VMEM((4 * PIECE, LANES), b16),
        pltpu.VMEM((4 * PIECE, 9 * INNER), b16),
        *[pltpu.VMEM((4, PIECE, LANES), b16) for _ in range(6)],
        pltpu.VMEM((4, 4, PIECE, LANES), f32),
        pltpu.VMEM((2, HALF, LANES), b16),
        pltpu.VMEM((PIECE, LANES), b16),
        pltpu.VMEM((PIECE, LANES), b16),
        pltpu.VMEM((2, HALF, LANES), b16),
        pltpu.VMEM((PIECE, LANES), b16),
        pltpu.VMEM((PIECE, LANES), b16),
        pltpu.VMEM((HALF, LANES), b16),
        pltpu.VMEM((HALF, LANES), b16),
        pltpu.VMEM((2, HALF, LANES), b16),
        pltpu.SemaphoreType.DMA((60,)),
        pltpu.SemaphoreType.DMA((60,)),
        pltpu.SemaphoreType.DMA((6,)),
    ]
    if backward:
        scratch += [
            pltpu.VMEM((SPOTS, INNER), f32),
            pltpu.VMEM((padded_rows, WIDE_ROWS), b16),
            pltpu.VMEM((SPOTS, LANES), b16),
            pltpu.VMEM((9 * INNER, LANES), f32),
            pltpu.VMEM((2, 2, 576, PART), b16),
            pltpu.VMEM((2, 576, LANES), b16),
            pltpu.VMEM((2, 2, 288, 256), b16),
            *[pltpu.VMEM((2, 576, 256), b16) for _ in range(4)],
            pltpu.VMEM((2, 2, 576, LANES), b16),
        ]
    else:
        scratch += [
            pltpu.VMEM((9, INNER, 2 * PART), b16),
            pltpu.VMEM((9, INNER, 2 * PART), b16),
            pltpu.VMEM((LANES, 9 * INNER), b16),
            pltpu.VMEM((9 * INNER, LANES), b16),
            pltpu.VMEM((2, 2 * ACROSS, INNER), b16),
            pltpu.VMEM((4, 6 * ACROSS, INNER), b16),
            pltpu.VMEM((9 * INNER // 2, 2 * PART), b16),
            pltpu.VMEM((12 * ACROSS, INNER), f32),
        ]
    return pl.pallas_call(
        functools.partial(phase_kernel, backward),
        out_shape=out_shape,
        in_specs=in_specs,
        out_specs=out_specs,
        scratch_shapes=scratch,
        compiler_params=pltpu.CompilerParams(
            collective_id=2 if backward else 1,
            has_side_effects=True,
            vmem_limit_bytes=60 * 1024 * 1024,
        ),
        name="backward_phase" if backward else "forward_phase",
    )(*operands)


SUM_ROWS = 1280


def sum_kernel(stacked_ref, coarse_ref, upward_grad_ref, bottom_grad_ref, inner_ref, joint_ref,
               reduce_ref, expand_ref, down_weight_ref, hidden_pre_ref, taps_ref, class_ref, down_out, up_out, conv_out, class_out, total, give, pair_in, a_out, a_in,
               b_out, b_in, z_out, z_in, result, conv_ref, send_sems, recv_sems):
    core, first, second = place()
    depth = lax.axis_index("samp")
    me = block_of(core, first, second)
    partner = {"wide": me * 2 + 1 - core}
    first_peers = [
        {"wide": block_of(core, (first + d) % 4, second) * 2 + core} for d in range(4)
    ]
    second_peers = [
        {"wide": block_of(core, first, (second + d) % 4) * 2 + core} for d in range(4)
    ]
    depth_peers = [{"samp": (depth + d) % 4} for d in range(4)]
    copies = Copies(send_sems, recv_sems)
    barrier = pltpu.get_barrier_semaphore()
    for device in [partner, *first_peers[1:], *second_peers[1:], *depth_peers[1:]]:
        pl.semaphore_signal(
            barrier, inc=1, device_id=device, device_id_type=pl.DeviceIdType.MESH
        )

    def own_lanes(half, width):
        return pl.ds(pl.multiple_of(half * width, 128), width)

    down_back = contract_last(bottom_grad_ref[0], down_weight_ref[:, 0:PART]) + contract_last(
        bottom_grad_ref[1], down_weight_ref[:, PART:]
    )
    down_back = down_back + jnp.concatenate([inner_ref[0], inner_ref[1]], axis=1)
    hidden_grad = (down_back + upward_grad_ref[...].astype(jnp.float32)) * silu_slope(
        hidden_pre_ref[...]
    )
    conv_ref[...] = contract_first(taps_ref[...], stacked_up(hidden_grad.astype(jnp.bfloat16)))

    def pack(half, to, kind):
        lanes = own_lanes(half, PART)
        to[0:512, :] = (
            contract_first(stacked_ref[...], bottom_grad_ref[half])
            + contract_first(joint_ref[1], expand_ref[:, lanes])
        ).astype(kind)
        to[512:1024, :] = (
            contract_first(coarse_ref[half], upward_grad_ref[...])
            + contract_first(reduce_ref[:, lanes], joint_ref[0])
        ).astype(kind)
        to[1168:1184, :] = jnp.zeros((16, PART), kind)
        to[1168:1177, 0:INNER] = class_ref[...].astype(kind)
        for piece in range(4):
            rows = pl.ds(pl.multiple_of((half * 4 + piece) * 144, 16), 144)
            to[1024:1168, piece * 128 : (piece + 1) * 128] = conv_ref[rows, :].astype(kind)
        to[1184:, :] = jnp.zeros((SUM_ROWS - 1184, PART), kind)

    def spot(at_first, at_second):
        base = (at_first % 4) * 320 + (at_second % 4) * 80
        return pl.ds(pl.multiple_of(base, 16), 80)

    order = (2, 1, 3, 0)
    pack(1 - core, give, jnp.bfloat16)
    pl.semaphore_wait(barrier, 10)
    for i, ds in enumerate(order):
        for df in range(4):
            part = spot(second + df, first + ds)
            copies.start(i * 4 + df, give.at[part, :], pair_in.at[part, :], partner)
    pack(core, total, jnp.float32)
    for i, ds in enumerate(order):
        for df in range(1, 4):
            part = spot(first + df, second + ds)
            copies.arrived(i * 4 + df, pair_in.at[part, :], partner)
            a_out[df, i] = (total[part, :] + pair_in[part, :].astype(jnp.float32)).astype(
                jnp.bfloat16
            )
            copies.start(16 + i * 3 + df - 1, a_out.at[df, i], a_in.at[df, i], first_peers[df])

    def after_first(i):
        part = spot(first, second + order[i])
        copies.arrived(i * 4, pair_in.at[part, :], partner)
        value = total[part, :] + pair_in[part, :].astype(jnp.float32)
        for df in range(1, 4):
            copies.arrived(16 + i * 3 + df - 1, a_in.at[df, i], first_peers[df])
            value = value + a_in[df, i].astype(jnp.float32)
        return value

    for i in range(3):
        b_out[i] = after_first(i).astype(jnp.bfloat16)
        copies.start(28 + i, b_out.at[i], b_in.at[i], second_peers[order[i]])
    total[0:80, :] = after_first(3)
    for i in range(3):
        copies.arrived(28 + i, b_in.at[i], second_peers[order[i]])
        total[0:80, :] += b_in[i].astype(jnp.float32)
    for d in range(1, 4):
        z_out[d] = total[0:80, own_lanes((depth + d) % 4, 128)].astype(jnp.bfloat16)
        copies.start(30 + d, z_out.at[d], z_in.at[d], depth_peers[d])
    value = total[0:80, own_lanes(depth, 128)]
    for d in range(1, 4):
        copies.arrived(30 + d, z_in.at[d], depth_peers[d])
        value = value + z_in[d].astype(jnp.float32)

    def at_depth(d):
        return result.at[core, spot(first, second), own_lanes((depth + d) % 4, 128)]

    def at(df, ds, half):
        return result.at[half, spot(first + df, second + ds), :]

    def pass_on(df, ds):
        copies.start(52 + df * 4 + ds, at(df, ds, core), at(df, ds, core), partner)

    def along_first(ds):
        for df in range(1, 4):
            copies.start(40 + ds * 3 + df - 1, at(0, ds, core), at(0, ds, core), first_peers[df])

    at_depth(0)[...] = value.astype(jnp.bfloat16)
    for d in range(1, 4):
        copies.start(33 + d, at_depth(0), at_depth(0), depth_peers[d])
    for d in range(1, 4):
        copies.arrived(33 + d, at_depth(4 - d), depth_peers[d])
    for ds in range(1, 4):
        copies.start(36 + ds, at(0, 0, core), at(0, 0, core), second_peers[ds])
    along_first(0)
    pass_on(0, 0)
    for ds in (1, 3, 2):
        copies.arrived(36 + ds, at(0, 4 - ds, core), second_peers[ds])
        along_first(4 - ds)
        pass_on(0, 4 - ds)
    for ds in (0, 3, 1, 2):
        for df in (1, 3, 2):
            copies.arrived(40 + ds * 3 + df - 1, at(4 - df, ds, core), first_peers[df])
            pass_on(4 - df, ds)
    def unpack(half):
        down_out[:, own_lanes(half, PART)] = result[half, 0:512, :]
        up_out[pl.ds(pl.multiple_of(half * PART, PART), PART), :] = result[half, 512:1024, :]
        for piece in range(4):
            rows = pl.ds(pl.multiple_of((half * 4 + piece) * 144, 16), 144)
            conv_out[rows, :] = result[half, 1024:1168, piece * 128 : (piece + 1) * 128]

    unpack(core)
    for df in range(4):
        for ds in range(4):
            copies.arrived(52 + df * 4 + ds, at(df, ds, 1 - core), partner)
    unpack(1 - core)
    class_out[...] = result[0, 1168:1184, 0:INNER].astype(jnp.float32)[0:9, :]
    copies.finish()


def sum_everywhere(*operands):
    b16, f32 = jnp.bfloat16, jnp.float32
    vmem = pl.BlockSpec(memory_space=pltpu.VMEM)
    down, up, conv, small = pl.pallas_call(
        sum_kernel,
        out_shape=[
            jax.ShapeDtypeStruct((PART, 2 * PART), b16),
            jax.ShapeDtypeStruct((2 * PART, PART), b16),
            jax.ShapeDtypeStruct((9 * INNER, INNER), b16),
            jax.ShapeDtypeStruct((9, INNER), f32),
        ],
        in_specs=[vmem] * 12,
        out_specs=[vmem] * 4,
        scratch_shapes=[
            pltpu.VMEM((SUM_ROWS, PART), f32),
            pltpu.VMEM((SUM_ROWS, PART), b16),
            pltpu.VMEM((SUM_ROWS, PART), b16),
            pltpu.VMEM((4, 4, 80, PART), b16),
            pltpu.VMEM((4, 4, 80, PART), b16),
            pltpu.VMEM((3, 80, PART), b16),
            pltpu.VMEM((3, 80, PART), b16),
            pltpu.VMEM((4, 80, 128), b16),
            pltpu.VMEM((4, 80, 128), b16),
            pltpu.VMEM((2, SUM_ROWS, PART), b16),
            pltpu.VMEM((9 * INNER, INNER), f32),
            pltpu.SemaphoreType.DMA((68,)),
            pltpu.SemaphoreType.DMA((68,)),
        ],
        compiler_params=pltpu.CompilerParams(
            collective_id=3, has_side_effects=True, vmem_limit_bytes=60 * 1024 * 1024
        ),
        name="sum_everywhere",
    )(*operands)
    conv = conv.astype(f32).reshape(3, 3, INNER, INNER)
    return conv, down.astype(f32), up.astype(f32), small.T


def local(
    features,
    labels,
    conv_weight,
    down_weight,
    expand_weight,
    reduce_weight,
    up_weight,
    class_weight,
):
    expand = jnp.transpose(expand_weight, (0, 1, 3, 2)).reshape(9, INNER // 2, 2 * PART)
    reduce = reduce_weight.reshape(9, INNER // 2, 2 * PART)
    (
        inner, pre, expanded, gathered, wa_back, wb_back, expand_tall, stacked, hidden_pre, taps,
        coarse,
    ) = bottleneck(
        False, features[0], conv_weight.reshape(9 * INNER, INNER), down_weight, up_weight, expand,
        reduce,
    )
    inner_back, reduce_grad, expand_grad, upward_grad, class_grad, bottom_grad, joint = bottleneck(
        True, wa_back, wb_back, pre, expanded, gathered, coarse, inner, stacked, labels[0], up_weight,
        down_weight, class_weight.T,
    )
    conv_grad, down_grad, up_grad, class_grad = sum_everywhere(
        stacked, coarse, upward_grad, bottom_grad, inner_back, joint,
        reduce.reshape(9 * INNER // 2, 2 * PART), expand_tall, down_weight, hidden_pre, taps,
        class_grad,
    )
    reduce_grad = reduce_grad.reshape(3, 3, INNER // 2, -1)
    expand_grad = jnp.transpose(expand_grad.reshape(9, INNER // 2, -1)[::-1], (0, 2, 1))
    expand_grad = expand_grad.reshape(3, 3, -1, INNER // 2)
    return (conv_grad, down_grad, expand_grad, reduce_grad, up_grad, class_grad)


def solution(mesh):
    return jax.shard_map(
        local,
        mesh=mesh,
        in_specs=(
            P("samp", "wide", None, None),
            P("samp", "wide", None),
            P(),
            P(),
            P(None, None, None, "wide"),
            P(None, None, "wide", None),
            P(),
            P(),
        ),
        out_specs=(
            P(),
            P(),
            P(None, None, "samp", "wide"),
            P(None, None, "wide", "samp"),
            P(),
            P(),
        ),
        check_vma=False,
    )
```

```python
import functools
import math

import jax
import jax.numpy as jnp
from jax import lax
from jax.experimental import pallas as pl
from jax.experimental.pallas import tpu as pltpu
from jax.sharding import PartitionSpec as P


def silu_slope(value):
    logistic = jax.nn.sigmoid(value)
    return logistic * (1.0 + value * (1.0 - logistic))


ROWS = 64
ACROSS = 48
SPOTS = ROWS * ACROSS
PIECE = 192
HALF = 96
PART = 512
LANES = 256
INNER = 128
WIDE_ROWS = 3 * INNER


def place():
    wide = lax.axis_index("wide")
    core = wide % 2
    x = (wide // 2) % 4
    y = wide // 8
    first = x + core * (y - x)
    second = y + core * (x - y)
    return core, first % 4, second % 4


def block_of(core, first, second):
    x = first + core * (second - first)
    y = second + core * (first - second)
    return y * 4 + x


def rows_of(block, length=PIECE):
    return pl.ds(pl.multiple_of(block * PIECE, 64), length)


def edge_masks(length):
    column = lax.broadcasted_iota(jnp.int32, (length, INNER), 0) % ACROSS
    return column == 0, column == ACROSS - 1


def from_left(values, at_left):
    return jnp.where(at_left, 0.0, pltpu.roll(values, 1, axis=0))


def from_right(values, at_right):
    return jnp.where(at_right, 0.0, pltpu.roll(values, values.shape[0] - 1, axis=0))


class Copies:
    def __init__(self, send_sems, recv_sems):
        self.send_sems = send_sems
        self.recv_sems = recv_sems
        self.sent = []

    def remote(self, index, source, target, device):
        copy = pltpu.make_async_remote_copy(
            src_ref=source,
            dst_ref=target,
            send_sem=self.send_sems.at[index],
            recv_sem=self.recv_sems.at[index],
            device_id=device if isinstance(device, dict) else {"wide": device},
            device_id_type=pl.DeviceIdType.MESH,
        )
        return copy

    def start(self, index, source, target, device):
        copy = self.remote(index, source, target, device)
        copy.start()
        self.sent.append(copy)

    def arrived(self, index, target, device):
        self.remote(index, target, target, device).wait_recv()

    def finish(self):
        for copy in self.sent:
            copy.wait_send()


def contract_first(left, right):
    return lax.dot_general(left, right, (((0,), (0,)), ((), ())), preferred_element_type=jnp.float32)


def contract_last(left, right):
    return lax.dot_general(left, right, (((1,), (1,)), ((), ())), preferred_element_type=jnp.float32)


def multiply(left, right):
    return jnp.dot(left, right, preferred_element_type=jnp.float32)


def side_by_side(tall):
    return jnp.concatenate([tall[i * HALF : (i + 1) * HALF] for i in range(4)], axis=1)


def stacked_up(flat):
    return jnp.concatenate([flat[:, i * INNER : (i + 1) * INNER] for i in range(4)], axis=0)


def first_layers(wide, copies, after, before, feature_ref, halo, columns, conv_weight_ref,
                 taps_ref, hidden_pre_ref, stacked_ref, x_ref, spread_rows):
    at_left, at_right = edge_masks(ACROSS)

    def row_columns(row, values):
        spread_rows[pl.ds(row * 2 * ACROSS, 2 * ACROSS), :] = values
        even = spread_rows[pl.ds(row * 2 * ACROSS, ACROSS, stride=2), :]
        odd = spread_rows[pl.ds(row * 2 * ACROSS + 1, ACROSS, stride=2), :]
        to = pl.ds(row * ACROSS, ACROSS)
        columns[0, to, :] = from_left(odd, at_left).astype(jnp.bfloat16)
        columns[1, to, :] = even.astype(jnp.bfloat16)
        columns[2, to, :] = odd.astype(jnp.bfloat16)
        columns[3, to, :] = from_right(even, at_right).astype(jnp.bfloat16)

    for row in range(4):
        row_columns(row + 1, feature_ref[row].astype(jnp.float32))
    copies.arrived(56, halo.at[0], after)
    copies.arrived(57, halo.at[1], before)
    row_columns(0, halo[0].astype(jnp.float32) * jnp.where(wide > 0, 1.0, 0.0))
    row_columns(5, halo[1].astype(jnp.float32) * jnp.where(wide < 31, 1.0, 0.0))
    for a in range(2):
        for b in range(2):
            for i in range(2):
                for p in range(3):
                    for q in range(3):
                        low = (a * 2 + b) * HALF + i * ACROSS
                        source = (a + p + 2 * i) * ACROSS
                        tap = (p * 3 + q) * INNER
                        taps_ref[low : low + ACROSS, tap : tap + INNER] = columns[
                            b + q, source : source + ACROSS, :
                        ]
    hidden_pre = multiply(taps_ref[...], conv_weight_ref[...])
    hidden_pre = side_by_side(hidden_pre)
    hidden_pre_ref[...] = hidden_pre
    stacked = jax.nn.silu(hidden_pre).astype(jnp.bfloat16)
    stacked_ref[...] = stacked
    for half in range(2):
        x_ref[half] = stacked[:, half * LANES : (half + 1) * LANES]


def label_column(labels):
    values = labels.astype(jnp.float32).astype(jnp.bfloat16)
    to = lax.broadcasted_iota(jnp.int32, (ACROSS, HALF), 0)
    source = lax.broadcasted_iota(jnp.int32, (ACROSS, HALF), 1)
    pieces = []
    picked = [
        contract_last((source == 2 * to + b).astype(jnp.float32).astype(jnp.bfloat16), values)
        for b in range(2)
    ]
    for a in range(2):
        for b in range(2):
            for i in range(2):
                row = a + 2 * i
                pieces.append(picked[b][:, row : row + 1])
    return jnp.concatenate(pieces, axis=0)


def middle(coarse_ref, inner_ref, stacked_ref, label_ref, up_weight_ref, class_ref,
           x_ref, upward_grad_ref, class_grad_ref):
    loss_scale = 8.0 / math.sqrt(49152)
    upward = multiply(coarse_ref[0], up_weight_ref[0:PART, :]) + multiply(
        coarse_ref[1], up_weight_ref[PART:, :]
    )
    upward = upward + jnp.concatenate([inner_ref[0], inner_ref[1]], axis=1)
    joined_pre = stacked_up(upward + stacked_ref[...].astype(jnp.float32))
    joined = jax.nn.silu(joined_pre).astype(jnp.bfloat16)
    logits = contract_last(joined, class_ref[...])
    classes = lax.broadcasted_iota(jnp.int32, logits.shape, 1)
    exp_logits = jnp.exp(logits)
    probability = exp_logits / jnp.sum(exp_logits, axis=1, keepdims=True)
    onehot = (label_column(label_ref[...]) == classes.astype(jnp.float32)).astype(jnp.float32)
    logit_grad = ((probability - onehot) * loss_scale).astype(jnp.bfloat16)
    joined_grad = multiply(logit_grad, class_ref[...])
    upward_grad = side_by_side((joined_grad * silu_slope(joined_pre)).astype(jnp.bfloat16))
    upward_grad_ref[...] = upward_grad
    for half in range(2):
        x_ref[half] = upward_grad[:, half * LANES : (half + 1) * LANES]
    class_grad_ref[...] = contract_first(logit_grad, joined)


def phase_kernel(backward, *refs):
    if backward:
        (
            wa_hbm, wb_hbm, pre_hbm, ef_hbm, xf_hbm, coarse_ref, inner_ref, stacked_ref, label_ref,
            up_weight_ref, class_ref,
            out_ref, ge_ref, upward_grad_ref, class_grad_ref, bottom_grad_ref, joint_ref,
        ) = refs[:17]
        scratch = refs[17:]
    else:
        (
            feature_ref, conv_weight_ref, down_weight_ref, up_weight_ref, expand_hbm, reduce_hbm,
            out_ref, pre_hbm, ef_hbm, xf_hbm, wa_hbm, wb_hbm, expand_tall_hbm, stacked_ref,
            hidden_pre_ref, taps_ref, coarse_ref,
        ) = refs[:17]
        scratch = refs[17:]
    (
        xall, wa, wb, total, pre, other, padded, chunk, window,
        far_out, up_out, down_out, far_in, up_in, down_in, reduced,
        far2_out, up2_out, down2_out, far2_in, up2_in, down2_in, swap_out, swap_in,
        x_ref, send_sems, recv_sems, local_sems,
    ) = scratch[:28]
    core, first, second = place()
    me = block_of(core, first, second)
    partner = me * 2 + 1 - core
    f_up = block_of(core, (first + 1) % 4, second) * 2 + core
    f_down = block_of(core, (first + 3) % 4, second) * 2 + core
    s_up = block_of(core, first, (second + 1) % 4) * 2 + core
    s_down = block_of(core, first, (second + 3) % 4) * 2 + core
    copies = Copies(send_sems, recv_sems)

    if backward:
        loads = [
            pltpu.make_async_copy(wa_hbm, wa, local_sems.at[0]),
            pltpu.make_async_copy(wb_hbm, wb, local_sems.at[1]),
        ]
        pre_f, ef, xf, grad, full, give, zfar_in, zup_out, zdown_out, zup_in, zdown_in, joint = scratch[28:]
        loads += [
            pltpu.make_async_copy(pre_hbm, pre_f, local_sems.at[2]),
            pltpu.make_async_copy(ef_hbm, ef, local_sems.at[3]),
            pltpu.make_async_copy(xf_hbm, xf, local_sems.at[4]),
        ]
    else:
        expand_both, reduce_both, wa_back, wb_back, halo, columns, expand_tall, spread_rows = scratch[28:]
        lanes = pl.ds(pl.multiple_of(core * LANES, LANES), LANES)
        own_rows = pl.ds(pl.multiple_of(core * 64, 64), 64)
        loads = [
            pltpu.make_async_copy(
                expand_hbm, expand_both.at[:, own_rows, :], local_sems.at[0]
            ),
            pltpu.make_async_copy(
                reduce_hbm, reduce_both.at[:, own_rows, :], local_sems.at[1]
            ),
        ]
    for load in loads:
        load.start()

    peers = [{"wide": device} for device in (partner, f_up, f_down, s_up, s_down)]
    if backward:
        depth = lax.axis_index("samp")
        z_up = {"samp": (depth + 1) % 4}
        z_down = {"samp": (depth + 3) % 4}
        peers += [z_up, z_down]
    else:
        wide = lax.axis_index("wide")
        after = {"wide": (wide + 1) % 32}
        before = {"wide": (wide + 31) % 32}
        peers += [after, before]
    barrier = pltpu.get_barrier_semaphore()
    for device in peers:
        pl.semaphore_signal(
            barrier, inc=1, device_id=device, device_id_type=pl.DeviceIdType.MESH
        )
    if backward:
        middle(
            coarse_ref, inner_ref, stacked_ref, label_ref, up_weight_ref, class_ref,
            x_ref, upward_grad_ref, class_grad_ref,
        )
    pl.semaphore_wait(barrier, len(peers))
    if not backward:
        copies.start(56, feature_ref.at[3], halo.at[0], after)
        copies.start(57, feature_ref.at[0], halo.at[1], before)
        copies.start(58, expand_hbm, expand_both.at[:, own_rows, :], partner)
        copies.start(59, reduce_hbm, reduce_both.at[:, own_rows, :], partner)
        first_layers(
            wide, copies, after, before, feature_ref, halo, columns, conv_weight_ref,
            taps_ref, hidden_pre_ref, stacked_ref, x_ref, spread_rows,
        )

    mine = pl.ds(pl.multiple_of(me * PIECE + core * HALF, 32), HALF)
    theirs = pl.ds(pl.multiple_of(me * PIECE + (1 - core) * HALF, 32), HALF)
    copies.start(0, x_ref.at[1 - core], xall.at[mine, :], partner)
    xall[mine, :] = x_ref[core]
    copies.arrived(0, xall.at[theirs, :], partner)

    def piece(first_at, second_at, low=0, length=PIECE):
        block = block_of(core, first_at % 4, second_at % 4)
        return xall.at[pl.ds(pl.multiple_of(block * PIECE + low, 32), length), :]

    def send_second(order, first_at):
        copies.start(5 + order, piece(first_at, second), piece(first_at, second), s_up)
        copies.start(9 + order, piece(first_at, second), piece(first_at, second), s_down)

    own = piece(first, second)
    copies.start(1, own, own, f_up)
    copies.start(2, own, own, f_down)
    send_second(0, first)

    def clear(step, carry):
        total[pl.ds(pl.multiple_of(step * 96, 32), 96), :] = jnp.zeros((96, WIDE_ROWS), jnp.float32)
        return carry

    def clear_grad(step, carry):
        grad[pl.ds(pl.multiple_of(step * INNER, 128), INNER), :] = jnp.zeros((INNER, LANES), jnp.float32)
        return carry

    def add_gradient():
        grad[...] += lax.dot_general(
            window[...], chunk[...], (((0,), (0,)), ((), ())), preferred_element_type=jnp.float32
        )

    def fill_window(source, row):
        for position in range(4):
            block = block_of(core, position, row)
            for p in range(3):
                window[
                    position * PIECE : (position + 1) * PIECE, p * WIDE_ROWS : (p + 1) * WIDE_ROWS
                ] = source[pl.ds(pl.multiple_of(block * PIECE + p * ACROSS, 16), PIECE), :]

    def fill_chunk(source, row):
        for position in range(4):
            block = block_of(core, position, row)
            chunk[position * PIECE : (position + 1) * PIECE, :] = source[rows_of(block), :]

    def hand_over(which):
        def pack(tap, carry):
            to = pl.ds(pl.multiple_of(tap * 64, 64), 64)
            own_rows = pl.ds(pl.multiple_of(tap * INNER + core * 64, 64), 64)
            other_rows = pl.ds(pl.multiple_of(tap * INNER + (1 - core) * 64, 64), 64)
            joint[which, core, to, :] = grad[own_rows, :].astype(jnp.bfloat16)
            give[which, to, :] = grad[other_rows, :].astype(jnp.bfloat16)
            return carry

        lax.fori_loop(0, 9, pack, 0)
        copies.start(38 + which, give.at[which], joint.at[which, core], partner)

    def take_over(which):
        copies.arrived(38 + which, joint.at[which, 1 - core], partner)
        both = jnp.concatenate([joint[which, 0], joint[which, 1]], axis=1)
        joint_ref[which] = both
        return both

    def share(which, at, low, length):
        at = at % 4
        lanes = pl.ds(pl.multiple_of((at % 2) * 256, 256), 256)
        return full.at[which, at // 2, pl.ds(low, length), lanes]

    def depth_far(which):
        both = take_over(which)
        for half in range(2):
            part = slice(half * PART, (half + 1) * PART)
            full[which, half] = narrow(contract_last(both, up_weight_ref[part, :]))
        copies.start(40 + which, share(which, depth + 2, 0, 288), zfar_in.at[which, 0], z_up)
        copies.start(42 + which, share(which, depth + 2, 288, 288), zfar_in.at[which, 1], z_down)

    def depth_near(which):
        near = share(which, depth + 1, 288, 288)[...]
        zup_out[which, 288:576, :] = near
        near = share(which, depth + 3, 0, 288)[...]
        zdown_out[which, 0:288, :] = near
        copies.arrived(40 + which, zfar_in.at[which, 0], z_up)
        near = share(which, depth + 1, 0, 288)[...].astype(jnp.float32)
        zup_out[which, 0:288, :] = narrow(near + zfar_in[which, 0].astype(jnp.float32))
        copies.start(44 + which, zup_out.at[which], zup_in.at[which], z_up)
        copies.arrived(42 + which, zfar_in.at[which, 1], z_down)
        near = share(which, depth + 3, 288, 288)[...].astype(jnp.float32)
        zdown_out[which, 288:576, :] = narrow(near + zfar_in[which, 1].astype(jnp.float32))
        copies.start(46 + which, zdown_out.at[which], zdown_in.at[which], z_down)

    def depth_own(which, out):
        copies.arrived(44 + which, zup_in.at[which], z_up)
        copies.arrived(46 + which, zdown_in.at[which], z_down)
        out[...] = (
            share(which, depth, 0, 576)[...].astype(jnp.float32)
            + zup_in[which].astype(jnp.float32)
            + zdown_in[which].astype(jnp.float32)
        )

    def narrow(values):
        return values.astype(jnp.bfloat16)

    lax.fori_loop(0, 33, clear, 0)
    if backward:
        lax.fori_loop(0, 9, clear_grad, 0)
    padded[0:ACROSS, :] = jnp.zeros((ACROSS, WIDE_ROWS), jnp.bfloat16)
    padded[SPOTS + ACROSS :, :] = jnp.zeros((ACROSS, WIDE_ROWS), jnp.bfloat16)

    offsets = (0, 3, 1, 2)

    def relay(order):
        first_at = first + offsets[order]
        here = piece(first_at, second + 3)
        copies.arrived(5 + order, here, s_up)
        low = piece(first_at, second + 3, 0, HALF)
        copies.start(13 + order, low, low, s_up)
        here = piece(first_at, second + 1)
        copies.arrived(9 + order, here, s_down)
        high = piece(first_at, second + 1, HALF, HALF)
        copies.start(48 + order, high, high, s_down)

    for load in loads:
        load.wait()
    if not backward:
        partner_rows = pl.ds(pl.multiple_of((1 - core) * 64, 64), 64)
        copies.arrived(58, expand_both.at[:, partner_rows, :], partner)
        copies.arrived(59, reduce_both.at[:, partner_rows, :], partner)
        share_rows = down_weight_ref[pl.ds(pl.multiple_of(core * LANES, LANES), LANES), :]
        joined_weight = narrow(
            contract_last(expand_both[...].reshape(9 * INNER, 2 * PART), share_rows)
        )
        for tap in range(9):
            block = joined_weight[tap * INNER : (tap + 1) * INNER, :]
            wa[:, tap * INNER : (tap + 1) * INNER] = block.T
            wb_back[(8 - tap) * INNER : (9 - tap) * INNER, :] = block
            expand_tall[(8 - tap) * 64 : (9 - tap) * 64, :] = expand_both[tap, own_rows, :]

    left = piece(first + 3, second)
    right = piece(first + 1, second)
    copies.arrived(1, left, f_up)
    low = piece(first + 3, second, 0, HALF)
    copies.start(3, low, low, f_up)
    send_second(1, first + 3)
    copies.arrived(2, right, f_down)
    high = piece(first + 1, second, HALF, HALF)
    copies.start(4, high, high, f_down)
    send_second(2, first + 1)
    relay(0)
    copies.arrived(3, piece(first + 2, second, 0, HALF), f_up)
    copies.arrived(4, piece(first + 2, second, HALF, HALF), f_down)
    send_second(3, first + 2)
    if not backward:
        wb[...] = narrow(
            multiply(
                reduce_both[...].reshape(9 * INNER, 2 * PART), up_weight_ref[:, lanes]
            )
        )
        for tap in range(9):
            here = slice(tap * INNER, (tap + 1) * INNER)
            back = slice((8 - tap) * INNER, (9 - tap) * INNER)
            wa_back[:, back] = wb[here, :].T
        for half in range(2):
            coarse_ref[half] = narrow(
                multiply(stacked_ref[...], down_weight_ref[:, half * PART : (half + 1) * PART])
            )
        stores = [
            pltpu.make_async_copy(wa_back, wa_hbm, local_sems.at[0]),
            pltpu.make_async_copy(wb_back, wb_hbm, local_sems.at[1]),
            pltpu.make_async_copy(expand_tall, expand_tall_hbm, local_sems.at[5]),
        ]
        for store in stores:
            store.start()
    else:
        stores = []
        for half in range(2):
            bottom_grad_ref[half] = narrow(
                contract_last(
                    upward_grad_ref[...], up_weight_ref[half * PART : (half + 1) * PART, :]
                )
            )

    def product(step, carry):
        turn = (3 * step + (step // 2) * (7 - 2 * step)) % 4

        @pl.when(step == 1)
        def _():
            for order in (1, 2, 3):
                first_at = first + offsets[order]
                copies.arrived(5 + order, piece(first_at, second + 3), s_up)
                low = piece(first_at, second + 3, 0, HALF)
                copies.remote(13 + order, low, low, s_up).start()
                copies.arrived(9 + order, piece(first_at, second + 1), s_down)
                high = piece(first_at, second + 1, HALF, HALF)
                copies.remote(48 + order, high, high, s_down).start()

        @pl.when(step == 3)
        def _():
            for order in range(4):
                first_at = first + offsets[order]
                copies.arrived(13 + order, piece(first_at, second + 2, 0, HALF), s_up)
                copies.arrived(48 + order, piece(first_at, second + 2, HALF, HALF), s_down)

        row = (second + turn) % 4
        fill_chunk(xall, row)
        result = jnp.dot(chunk[...], wa[...], preferred_element_type=jnp.float32)
        for position in range(4):
            block = block_of(core, position, row)
            for p in range(3):
                where = pl.ds(pl.multiple_of(block * PIECE + (2 - p) * ACROSS, 16), PIECE)
                total[where, :] += result[
                    position * PIECE : (position + 1) * PIECE, p * WIDE_ROWS : (p + 1) * WIDE_ROWS
                ]

        if backward:

            @pl.when(step < 3)
            def _():
                fill_window(ef, row)
                add_gradient()

        return carry

    lax.fori_loop(0, 4, product, 0)
    for order in (1, 2, 3):
        here = piece(first, second, 0, HALF)
        copies.sent.append(copies.remote(13 + order, here, here, s_up))
        copies.sent.append(copies.remote(48 + order, here, here, s_down))

    at_left, at_right = edge_masks(PIECE)

    def fold(step, carry):
        rows = rows_of(step)
        padded_rows = pl.ds(pl.multiple_of(step * PIECE + ACROSS, 16), PIECE)
        pre[rows, :] = (
            total[padded_rows, INNER : 2 * INNER]
            + from_left(total[padded_rows, 0:INNER], at_left)
            + from_right(total[padded_rows, 2 * INNER :], at_right)
        )
        return carry

    for quarter in range(4):
        lax.fori_loop(quarter * 4, quarter * 4 + 4, fold, 0)
        rows = pl.ds(quarter * 768, 768)
        copies.start(17 + quarter, pre.at[rows, :], other.at[rows, :], partner)

    if backward:
        fill_window(ef, (second + 2) % 4)
        add_gradient()
        hand_over(0)
        lax.fori_loop(0, 9, clear_grad, 0)

    def shape(step, carry):
        rows = rows_of(step)
        padded_rows = pl.ds(pl.multiple_of(step * PIECE + ACROSS, 16), PIECE)
        value = pre[rows, :] + other[rows, :]
        if backward:
            value = value * silu_slope(pre_f[rows, :])
        else:
            other[rows, :] = value
            value = jax.nn.silu(value)
        value = value.astype(jnp.bfloat16).astype(jnp.float32)
        padded[padded_rows, 0:INNER] = from_left(value, at_left).astype(jnp.bfloat16)
        padded[padded_rows, INNER : 2 * INNER] = value.astype(jnp.bfloat16)
        padded[padded_rows, 2 * INNER :] = from_right(value, at_right).astype(jnp.bfloat16)
        return carry

    for quarter in range(4):
        copies.arrived(17 + quarter, other.at[pl.ds(quarter * 768, 768), :], partner)
        lax.fori_loop(quarter * 4, quarter * 4 + 4, shape, 0)

    if not backward:
        more = [
            pltpu.make_async_copy(other, pre_hbm, local_sems.at[2]),
            pltpu.make_async_copy(padded, ef_hbm, local_sems.at[3]),
            pltpu.make_async_copy(xall, xf_hbm, local_sems.at[4]),
        ]
        for store in more:
            store.start()
        stores += more

    if backward:
        depth_far(0)

    def place_of(order):
        return (first + (2, 1, 3, 0)[order]) % 4

    def spread(step, carry):
        turn = (2 - step + (step // 2) * (7 - 2 * step)) % 4
        row = (second + turn) % 4
        fill_window(padded, row)
        result = jnp.dot(window[...], wb[...], preferred_element_type=jnp.float32)
        for position in range(4):
            reduced[step, position] = result[position * PIECE : (position + 1) * PIECE, :]

        @pl.when(step == 0)
        def _():
            for order in range(4):
                far_out[order] = narrow(reduced[0, place_of(order)])
                low = pl.ds(0, HALF)
                copies.remote(
                    21 + order, far_out.at[order, low, :], far_in.at[order, low, :], s_up
                ).start()
                high = pl.ds(HALF, HALF)
                copies.remote(
                    33 + order, far_out.at[order, high, :], far_in.at[order, high, :], s_down
                ).start()

        @pl.when(step == 2)
        def _():
            for order in range(4):
                at = place_of(order)
                low = pl.ds(0, HALF)
                high = pl.ds(HALF, HALF)
                up_out[order, high, :] = narrow(reduced[1, at, high, :])
                down_out[order, low, :] = narrow(reduced[2, at, low, :])
                copies.arrived(21 + order, far_in.at[order, low, :], s_up)
                up_out[order, low, :] = narrow(
                    reduced[1, at, low, :] + far_in[order, low, :].astype(jnp.float32)
                )
                copies.remote(25 + order, up_out.at[order], up_in.at[order], s_up).start()
                copies.arrived(33 + order, far_in.at[order, high, :], s_down)
                down_out[order, high, :] = narrow(
                    reduced[2, at, high, :] + far_in[order, high, :].astype(jnp.float32)
                )
                copies.remote(29 + order, down_out.at[order], down_in.at[order], s_down).start()

        if backward:

            @pl.when(step >= 2)
            def _():
                fill_chunk(xf, row)
                add_gradient()

            @pl.when(step == 3)
            def _():
                for turn in (2, 1):
                    fill_window(padded, (second + turn) % 4)
                    fill_chunk(xf, (second + turn) % 4)
                    add_gradient()

        return carry

    lax.fori_loop(0, 4, spread, 0)
    for order in range(4):
        low = pl.ds(0, HALF)
        half = far_out.at[order, low, :]
        copies.sent.append(copies.remote(21 + order, half, half, s_up))
        copies.sent.append(copies.remote(33 + order, half, half, s_down))
        copies.sent.append(copies.remote(25 + order, up_out.at[order], up_in.at[order], s_up))
        copies.sent.append(copies.remote(29 + order, down_out.at[order], down_in.at[order], s_down))
    if backward:
        hand_over(1)
        depth_near(0)

    def arrive_second(order):
        copies.arrived(25 + order, up_in.at[order], s_up)
        copies.arrived(29 + order, down_in.at[order], s_down)

    def gathered(order, low, length):
        rows = pl.ds(low, length)
        return (
            reduced[3, place_of(order), rows, :]
            + up_in[order, rows, :].astype(jnp.float32)
            + down_in[order, rows, :].astype(jnp.float32)
        )

    arrive_second(0)
    far2_out[0] = narrow(gathered(0, 0, HALF))
    copies.start(52, far2_out.at[0], far2_in.at[0], f_up)
    far2_out[1] = narrow(gathered(0, HALF, HALF))
    copies.start(53, far2_out.at[1], far2_in.at[1], f_down)
    arrive_second(1)
    up2_out[HALF:, :] = narrow(gathered(1, HALF, HALF))
    copies.arrived(52, far2_in.at[0], f_up)
    up2_out[:HALF, :] = narrow(gathered(1, 0, HALF) + far2_in[0].astype(jnp.float32))
    copies.start(54, up2_out, up2_in, f_up)
    arrive_second(2)
    down2_out[:HALF, :] = narrow(gathered(2, 0, HALF))
    copies.arrived(53, far2_in.at[1], f_down)
    down2_out[HALF:, :] = narrow(gathered(2, HALF, HALF) + far2_in[1].astype(jnp.float32))
    copies.start(55, down2_out, down2_in, f_down)
    if backward:
        take_over(1)
    arrive_second(3)
    copies.arrived(54, up2_in, f_up)
    copies.arrived(55, down2_in, f_down)

    def settled(which):
        rows = pl.ds(pl.multiple_of(which * HALF, 32), HALF)
        return (
            reduced[3, first, rows, :]
            + up_in[3, rows, :].astype(jnp.float32)
            + down_in[3, rows, :].astype(jnp.float32)
            + up2_in[rows, :].astype(jnp.float32)
            + down2_in[rows, :].astype(jnp.float32)
        )

    swap_out[...] = narrow(settled(1 - core))
    copies.start(37, swap_out, swap_in, partner)
    out_ref[core] = settled(core)
    copies.arrived(37, swap_in, partner)
    out_ref[1 - core] = swap_in[...].astype(jnp.float32)
    if backward:
        depth_own(0, ge_ref)
    copies.finish()
    for store in stores:
        store.wait()


def bottleneck(backward, *operands):
    b16, f32 = jnp.bfloat16, jnp.float32
    vmem = pl.BlockSpec(memory_space=pltpu.VMEM)
    anywhere = pl.BlockSpec(memory_space=pl.ANY)
    padded_rows = SPOTS + 2 * ACROSS
    shape = jax.ShapeDtypeStruct
    out = shape((2, HALF, LANES), f32)
    pair = shape((2, HALF, PART), b16)
    if backward:
        grad = shape((9 * INNER // 2, PART // 2), f32)
        in_specs = [anywhere] * 5 + [vmem] * 6
        out_shape = [
            out, grad, shape((HALF, PART), b16), shape((9, INNER), f32), pair,
            shape((2, 9 * INNER // 2, PART), b16),
        ]
        out_specs = [vmem] * 6
    else:
        in_specs = [vmem] * 4 + [anywhere] * 2
        out_shape = [
            out,
            shape((SPOTS, INNER), f32),
            shape((padded_rows, WIDE_ROWS), b16),
            shape((SPOTS, LANES), b16),
            shape((LANES, 9 * INNER), b16),
            shape((9 * INNER, LANES), b16),
            shape((9 * INNER // 2, 2 * PART), b16),
            shape((HALF, PART), b16),
            shape((HALF, PART), f32),
            shape((4 * HALF, 9 * INNER), b16),
            pair,
        ]
        out_specs = [vmem] + [anywhere] * 6 + [vmem] * 4
    scratch = [
        pltpu.VMEM((SPOTS, LANES), b16),
        pltpu.VMEM((LANES, 9 * INNER), b16),
        pltpu.VMEM((9 * INNER, LANES), b16),
        pltpu.VMEM((padded_rows, WIDE_ROWS), f32),
        pltpu.VMEM((SPOTS, INNER), f32),
        pltpu.VMEM((SPOTS, INNER), f32),
        pltpu.VMEM((padded_rows, WIDE_ROWS), b16),
        pltpu.VMEM((4 * PIECE, LANES), b16),
        pltpu.VMEM((4 * PIECE, 9 * INNER), b16),
        *[pltpu.VMEM((4, PIECE, LANES), b16) for _ in range(6)],
        pltpu.VMEM((4, 4, PIECE, LANES), f32),
        pltpu.VMEM((2, HALF, LANES), b16),
        pltpu.VMEM((PIECE, LANES), b16),
        pltpu.VMEM((PIECE, LANES), b16),
        pltpu.VMEM((2, HALF, LANES), b16),
        pltpu.VMEM((PIECE, LANES), b16),
        pltpu.VMEM((PIECE, LANES), b16),
        pltpu.VMEM((HALF, LANES), b16),
        pltpu.VMEM((HALF, LANES), b16),
        pltpu.VMEM((2, HALF, LANES), b16),
        pltpu.SemaphoreType.DMA((60,)),
        pltpu.SemaphoreType.DMA((60,)),
        pltpu.SemaphoreType.DMA((6,)),
    ]
    if backward:
        scratch += [
            pltpu.VMEM((SPOTS, INNER), f32),
            pltpu.VMEM((padded_rows, WIDE_ROWS), b16),
            pltpu.VMEM((SPOTS, LANES), b16),
            pltpu.VMEM((9 * INNER, LANES), f32),
            pltpu.VMEM((2, 2, 576, PART), b16),
            pltpu.VMEM((2, 576, LANES), b16),
            pltpu.VMEM((2, 2, 288, 256), b16),
            *[pltpu.VMEM((2, 576, 256), b16) for _ in range(4)],
            pltpu.VMEM((2, 2, 576, LANES), b16),
        ]
    else:
        scratch += [
            pltpu.VMEM((9, INNER, 2 * PART), b16),
            pltpu.VMEM((9, INNER, 2 * PART), b16),
            pltpu.VMEM((LANES, 9 * INNER), b16),
            pltpu.VMEM((9 * INNER, LANES), b16),
            pltpu.VMEM((2, 2 * ACROSS, INNER), b16),
            pltpu.VMEM((4, 6 * ACROSS, INNER), b16),
            pltpu.VMEM((9 * INNER // 2, 2 * PART), b16),
            pltpu.VMEM((12 * ACROSS, INNER), f32),
        ]
    return pl.pallas_call(
        functools.partial(phase_kernel, backward),
        out_shape=out_shape,
        in_specs=in_specs,
        out_specs=out_specs,
        scratch_shapes=scratch,
        compiler_params=pltpu.CompilerParams(
            collective_id=2 if backward else 1,
            has_side_effects=True,
            vmem_limit_bytes=60 * 1024 * 1024,
        ),
        name="backward_phase" if backward else "forward_phase",
    )(*operands)


SUM_ROWS = 1280


def sum_kernel(stacked_ref, coarse_ref, upward_grad_ref, bottom_grad_ref, inner_ref, joint_ref,
               reduce_ref, expand_ref, down_weight_ref, hidden_pre_ref, taps_ref, class_ref, down_out, up_out, conv_out, class_out, expand_out, total, give, pair_in, a_out, a_in,
               b_out, b_in, z_out, z_in, result, conv_ref, full, zfar_in, zup_out, zdown_out,
               zup_in, zdown_in, send_sems, recv_sems):
    core, first, second = place()
    depth = lax.axis_index("samp")
    me = block_of(core, first, second)
    partner = {"wide": me * 2 + 1 - core}
    first_peers = [
        {"wide": block_of(core, (first + d) % 4, second) * 2 + core} for d in range(4)
    ]
    second_peers = [
        {"wide": block_of(core, first, (second + d) % 4) * 2 + core} for d in range(4)
    ]
    depth_peers = [{"samp": (depth + d) % 4} for d in range(4)]
    copies = Copies(send_sems, recv_sems)
    barrier = pltpu.get_barrier_semaphore()
    for device in [partner, *first_peers[1:], *second_peers[1:], *depth_peers[1:]]:
        pl.semaphore_signal(
            barrier, inc=1, device_id=device, device_id_type=pl.DeviceIdType.MESH
        )

    def own_lanes(half, width):
        return pl.ds(pl.multiple_of(half * width, 128), width)

    down_back = contract_last(bottom_grad_ref[0], down_weight_ref[:, 0:PART]) + contract_last(
        bottom_grad_ref[1], down_weight_ref[:, PART:]
    )
    down_back = down_back + jnp.concatenate([inner_ref[0], inner_ref[1]], axis=1)
    hidden_grad = (down_back + upward_grad_ref[...].astype(jnp.float32)) * silu_slope(
        hidden_pre_ref[...]
    )
    conv_ref[...] = contract_first(taps_ref[...], stacked_up(hidden_grad.astype(jnp.bfloat16)))

    def pack(half, to, kind):
        lanes = own_lanes(half, PART)
        to[0:512, :] = (
            contract_first(stacked_ref[...], bottom_grad_ref[half])
            + contract_first(joint_ref[1], expand_ref[:, lanes])
        ).astype(kind)
        to[512:1024, :] = (
            contract_first(coarse_ref[half], upward_grad_ref[...])
            + contract_first(reduce_ref[:, lanes], joint_ref[0])
        ).astype(kind)
        to[1168:1184, :] = jnp.zeros((16, PART), kind)
        to[1168:1177, 0:INNER] = class_ref[...].astype(kind)
        for piece in range(4):
            rows = pl.ds(pl.multiple_of((half * 4 + piece) * 144, 16), 144)
            to[1024:1168, piece * 128 : (piece + 1) * 128] = conv_ref[rows, :].astype(kind)
        to[1184:, :] = jnp.zeros((SUM_ROWS - 1184, PART), kind)

    def spot(at_first, at_second):
        base = (at_first % 4) * 320 + (at_second % 4) * 80
        return pl.ds(pl.multiple_of(base, 16), 80)

    order = (2, 1, 3, 0)
    pack(1 - core, give, jnp.bfloat16)
    pl.semaphore_wait(barrier, 10)
    for i, ds in enumerate(order):
        for df in range(4):
            part = spot(second + df, first + ds)
            copies.start(i * 4 + df, give.at[part, :], pair_in.at[part, :], partner)
    pack(core, total, jnp.float32)
    for i, ds in enumerate(order):
        for df in range(1, 4):
            part = spot(first + df, second + ds)
            copies.arrived(i * 4 + df, pair_in.at[part, :], partner)
            a_out[df, i] = (total[part, :] + pair_in[part, :].astype(jnp.float32)).astype(
                jnp.bfloat16
            )
            copies.start(16 + i * 3 + df - 1, a_out.at[df, i], a_in.at[df, i], first_peers[df])

    z_up, z_down = depth_peers[1], depth_peers[3]

    def share(at, low, length):
        at = at % 4
        return full.at[at // 2, pl.ds(low, length), own_lanes(at % 2, 256)]

    def plus(left, right):
        return left.astype(jnp.float32) + right.astype(jnp.float32)

    for half in range(2):
        part = slice(half * PART, (half + 1) * PART)
        full[half] = multiply(joint_ref[1], down_weight_ref[:, part]).astype(jnp.bfloat16)
    copies.start(68, share(depth + 2, 0, 288), zfar_in.at[0], z_up)
    copies.start(69, share(depth + 2, 288, 288), zfar_in.at[1], z_down)

    def after_first(i):
        part = spot(first, second + order[i])
        copies.arrived(i * 4, pair_in.at[part, :], partner)
        value = total[part, :] + pair_in[part, :].astype(jnp.float32)
        for df in range(1, 4):
            copies.arrived(16 + i * 3 + df - 1, a_in.at[df, i], first_peers[df])
            value = value + a_in[df, i].astype(jnp.float32)
        return value

    for i in range(3):
        b_out[i] = after_first(i).astype(jnp.bfloat16)
        copies.start(28 + i, b_out.at[i], b_in.at[i], second_peers[order[i]])
    total[0:80, :] = after_first(3)
    zup_out[288:576, :] = share(depth + 1, 288, 288)[...]
    zdown_out[0:288, :] = share(depth + 3, 0, 288)[...]
    copies.arrived(68, zfar_in.at[0], z_up)
    zup_out[0:288, :] = plus(share(depth + 1, 0, 288)[...], zfar_in[0]).astype(jnp.bfloat16)
    copies.arrived(69, zfar_in.at[1], z_down)
    zdown_out[288:576, :] = plus(share(depth + 3, 288, 288)[...], zfar_in[1]).astype(jnp.bfloat16)
    for i in range(3):
        copies.arrived(28 + i, b_in.at[i], second_peers[order[i]])
        total[0:80, :] += b_in[i].astype(jnp.float32)
    for d in range(1, 4):
        z_out[d] = total[0:80, own_lanes((depth + d) % 4, 128)].astype(jnp.bfloat16)
        copies.start(30 + d, z_out.at[d], z_in.at[d], depth_peers[d])
    value = total[0:80, own_lanes(depth, 128)]
    for d in range(1, 4):
        copies.arrived(30 + d, z_in.at[d], depth_peers[d])
        value = value + z_in[d].astype(jnp.float32)

    def at_depth(d):
        return result.at[core, spot(first, second), own_lanes((depth + d) % 4, 128)]

    def at(df, ds, half):
        return result.at[half, spot(first + df, second + ds), :]

    def pass_on(df, ds):
        copies.start(52 + df * 4 + ds, at(df, ds, core), at(df, ds, core), partner)

    def along_first(ds):
        for df in range(1, 4):
            copies.start(40 + ds * 3 + df - 1, at(0, ds, core), at(0, ds, core), first_peers[df])

    at_depth(0)[...] = value.astype(jnp.bfloat16)
    for d in range(1, 4):
        copies.start(33 + d, at_depth(0), at_depth(0), depth_peers[d])
    for d in range(1, 4):
        copies.arrived(33 + d, at_depth(4 - d), depth_peers[d])
    copies.start(70, zup_out, zup_in, z_up)
    copies.start(71, zdown_out, zdown_in, z_down)
    for ds in range(1, 4):
        copies.start(36 + ds, at(0, 0, core), at(0, 0, core), second_peers[ds])
    along_first(0)
    pass_on(0, 0)
    for ds in (1, 3, 2):
        copies.arrived(36 + ds, at(0, 4 - ds, core), second_peers[ds])
        along_first(4 - ds)
        pass_on(0, 4 - ds)
    for ds in (0, 3, 1, 2):
        for df in (1, 3, 2):
            copies.arrived(40 + ds * 3 + df - 1, at(4 - df, ds, core), first_peers[df])
            pass_on(4 - df, ds)
    copies.arrived(70, zup_in, z_up)
    copies.arrived(71, zdown_in, z_down)
    expand_out[...] = plus(share(depth, 0, 576)[...], zup_in[...]) + zdown_in[...].astype(
        jnp.float32
    )

    def unpack(half):
        down_out[:, own_lanes(half, PART)] = result[half, 0:512, :]
        up_out[pl.ds(pl.multiple_of(half * PART, PART), PART), :] = result[half, 512:1024, :]
        for piece in range(4):
            rows = pl.ds(pl.multiple_of((half * 4 + piece) * 144, 16), 144)
            conv_out[rows, :] = result[half, 1024:1168, piece * 128 : (piece + 1) * 128]

    unpack(core)
    for df in range(4):
        for ds in range(4):
            copies.arrived(52 + df * 4 + ds, at(df, ds, 1 - core), partner)
    unpack(1 - core)
    class_out[...] = result[0, 1168:1184, 0:INNER].astype(jnp.float32)[0:9, :]
    copies.finish()


def sum_everywhere(*operands):
    b16, f32 = jnp.bfloat16, jnp.float32
    vmem = pl.BlockSpec(memory_space=pltpu.VMEM)
    down, up, conv, small, expand = pl.pallas_call(
        sum_kernel,
        out_shape=[
            jax.ShapeDtypeStruct((PART, 2 * PART), b16),
            jax.ShapeDtypeStruct((2 * PART, PART), b16),
            jax.ShapeDtypeStruct((9 * INNER, INNER), b16),
            jax.ShapeDtypeStruct((9, INNER), f32),
            jax.ShapeDtypeStruct((9 * INNER // 2, PART // 2), f32),
        ],
        in_specs=[vmem] * 12,
        out_specs=[vmem] * 5,
        scratch_shapes=[
            pltpu.VMEM((SUM_ROWS, PART), f32),
            pltpu.VMEM((SUM_ROWS, PART), b16),
            pltpu.VMEM((SUM_ROWS, PART), b16),
            pltpu.VMEM((4, 4, 80, PART), b16),
            pltpu.VMEM((4, 4, 80, PART), b16),
            pltpu.VMEM((3, 80, PART), b16),
            pltpu.VMEM((3, 80, PART), b16),
            pltpu.VMEM((4, 80, 128), b16),
            pltpu.VMEM((4, 80, 128), b16),
            pltpu.VMEM((2, SUM_ROWS, PART), b16),
            pltpu.VMEM((9 * INNER, INNER), f32),
            pltpu.VMEM((2, 576, PART), b16),
            pltpu.VMEM((2, 288, 256), b16),
            *[pltpu.VMEM((576, 256), b16) for _ in range(4)],
            pltpu.SemaphoreType.DMA((72,)),
            pltpu.SemaphoreType.DMA((72,)),
        ],
        compiler_params=pltpu.CompilerParams(
            collective_id=3, has_side_effects=True, vmem_limit_bytes=60 * 1024 * 1024
        ),
        name="sum_everywhere",
    )(*operands)
    conv = conv.astype(f32).reshape(3, 3, INNER, INNER)
    return conv, down.astype(f32), up.astype(f32), small.T, expand


def local(
    features,
    labels,
    conv_weight,
    down_weight,
    expand_weight,
    reduce_weight,
    up_weight,
    class_weight,
):
    expand = jnp.transpose(expand_weight, (0, 1, 3, 2)).reshape(9, INNER // 2, 2 * PART)
    reduce = reduce_weight.reshape(9, INNER // 2, 2 * PART)
    (
        inner, pre, expanded, gathered, wa_back, wb_back, expand_tall, stacked, hidden_pre, taps,
        coarse,
    ) = bottleneck(
        False, features[0], conv_weight.reshape(9 * INNER, INNER), down_weight, up_weight, expand,
        reduce,
    )
    inner_back, reduce_grad, upward_grad, class_grad, bottom_grad, joint = bottleneck(
        True, wa_back, wb_back, pre, expanded, gathered, coarse, inner, stacked, labels[0], up_weight,
        class_weight.T,
    )
    conv_grad, down_grad, up_grad, class_grad, expand_grad = sum_everywhere(
        stacked, coarse, upward_grad, bottom_grad, inner_back, joint,
        reduce.reshape(9 * INNER // 2, 2 * PART), expand_tall, down_weight, hidden_pre, taps,
        class_grad,
    )
    reduce_grad = reduce_grad.reshape(3, 3, INNER // 2, -1)
    expand_grad = jnp.transpose(expand_grad.reshape(9, INNER // 2, -1)[::-1], (0, 2, 1))
    expand_grad = expand_grad.reshape(3, 3, -1, INNER // 2)
    return (conv_grad, down_grad, expand_grad, reduce_grad, up_grad, class_grad)


def solution(mesh):
    return jax.shard_map(
        local,
        mesh=mesh,
        in_specs=(
            P("samp", "wide", None, None),
            P("samp", "wide", None),
            P(),
            P(),
            P(None, None, None, "wide"),
            P(None, None, "wide", None),
            P(),
            P(),
        ),
        out_specs=(
            P(),
            P(),
            P(None, None, "samp", "wide"),
            P(None, None, "wide", "samp"),
            P(),
            P(),
        ),
        check_vma=False,
    )
```

```python
import functools
import math

import jax
import jax.numpy as jnp
from jax import lax
from jax.experimental import pallas as pl
from jax.experimental.pallas import tpu as pltpu
from jax.sharding import PartitionSpec as P


def silu_slope(value):
    logistic = jax.nn.sigmoid(value)
    return logistic * (1.0 + value * (1.0 - logistic))


ROWS = 64
ACROSS = 48
SPOTS = ROWS * ACROSS
PIECE = 192
HALF = 96
PART = 512
LANES = 256
INNER = 128
WIDE_ROWS = 3 * INNER


def place():
    wide = lax.axis_index("wide")
    core = wide % 2
    x = (wide // 2) % 4
    y = wide // 8
    first = x + core * (y - x)
    second = y + core * (x - y)
    return core, first % 4, second % 4


def block_of(core, first, second):
    x = first + core * (second - first)
    y = second + core * (first - second)
    return y * 4 + x


def rows_of(block, length=PIECE):
    return pl.ds(pl.multiple_of(block * PIECE, 64), length)


def edge_masks(length):
    column = lax.broadcasted_iota(jnp.int32, (length, INNER), 0) % ACROSS
    return column == 0, column == ACROSS - 1


def from_left(values, at_left):
    return jnp.where(at_left, 0.0, pltpu.roll(values, 1, axis=0))


def from_right(values, at_right):
    return jnp.where(at_right, 0.0, pltpu.roll(values, values.shape[0] - 1, axis=0))


class Copies:
    def __init__(self, send_sems, recv_sems):
        self.send_sems = send_sems
        self.recv_sems = recv_sems
        self.sent = []

    def remote(self, index, source, target, device):
        copy = pltpu.make_async_remote_copy(
            src_ref=source,
            dst_ref=target,
            send_sem=self.send_sems.at[index],
            recv_sem=self.recv_sems.at[index],
            device_id=device if isinstance(device, dict) else {"wide": device},
            device_id_type=pl.DeviceIdType.MESH,
        )
        return copy

    def start(self, index, source, target, device):
        copy = self.remote(index, source, target, device)
        copy.start()
        self.sent.append(copy)

    def arrived(self, index, target, device):
        self.remote(index, target, target, device).wait_recv()

    def finish(self):
        for copy in self.sent:
            copy.wait_send()


def contract_first(left, right):
    return lax.dot_general(left, right, (((0,), (0,)), ((), ())), preferred_element_type=jnp.float32)


def contract_last(left, right):
    return lax.dot_general(left, right, (((1,), (1,)), ((), ())), preferred_element_type=jnp.float32)


def multiply(left, right):
    return jnp.dot(left, right, preferred_element_type=jnp.float32)


def side_by_side(tall):
    return jnp.concatenate([tall[i * HALF : (i + 1) * HALF] for i in range(4)], axis=1)


def stacked_up(flat):
    return jnp.concatenate([flat[:, i * INNER : (i + 1) * INNER] for i in range(4)], axis=0)


def first_layers(wide, copies, after, before, feature_ref, halo, columns, conv_weight_ref,
                 taps_ref, hidden_pre_ref, stacked_ref, x_ref, spread_rows):
    at_left, at_right = edge_masks(ACROSS)

    def row_columns(row, values):
        spread_rows[pl.ds(row * 2 * ACROSS, 2 * ACROSS), :] = values
        even = spread_rows[pl.ds(row * 2 * ACROSS, ACROSS, stride=2), :]
        odd = spread_rows[pl.ds(row * 2 * ACROSS + 1, ACROSS, stride=2), :]
        to = pl.ds(row * ACROSS, ACROSS)
        columns[0, to, :] = from_left(odd, at_left).astype(jnp.bfloat16)
        columns[1, to, :] = even.astype(jnp.bfloat16)
        columns[2, to, :] = odd.astype(jnp.bfloat16)
        columns[3, to, :] = from_right(even, at_right).astype(jnp.bfloat16)

    for row in range(4):
        row_columns(row + 1, feature_ref[row].astype(jnp.float32))
    copies.arrived(56, halo.at[0], after)
    copies.arrived(57, halo.at[1], before)
    row_columns(0, halo[0].astype(jnp.float32) * jnp.where(wide > 0, 1.0, 0.0))
    row_columns(5, halo[1].astype(jnp.float32) * jnp.where(wide < 31, 1.0, 0.0))
    for a in range(2):
        for b in range(2):
            for i in range(2):
                for p in range(3):
                    for q in range(3):
                        low = (a * 2 + b) * HALF + i * ACROSS
                        source = (a + p + 2 * i) * ACROSS
                        tap = (p * 3 + q) * INNER
                        taps_ref[low : low + ACROSS, tap : tap + INNER] = columns[
                            b + q, source : source + ACROSS, :
                        ]
    hidden_pre = multiply(taps_ref[...], conv_weight_ref[...])
    hidden_pre = side_by_side(hidden_pre)
    hidden_pre_ref[...] = hidden_pre
    stacked = jax.nn.silu(hidden_pre).astype(jnp.bfloat16)
    stacked_ref[...] = stacked
    for half in range(2):
        x_ref[half] = stacked[:, half * LANES : (half + 1) * LANES]


def label_column(labels):
    values = labels.astype(jnp.float32).astype(jnp.bfloat16)
    to = lax.broadcasted_iota(jnp.int32, (ACROSS, HALF), 0)
    source = lax.broadcasted_iota(jnp.int32, (ACROSS, HALF), 1)
    pieces = []
    picked = [
        contract_last((source == 2 * to + b).astype(jnp.float32).astype(jnp.bfloat16), values)
        for b in range(2)
    ]
    for a in range(2):
        for b in range(2):
            for i in range(2):
                row = a + 2 * i
                pieces.append(picked[b][:, row : row + 1])
    return jnp.concatenate(pieces, axis=0)


def middle(coarse_ref, inner_ref, stacked_ref, label_ref, up_weight_ref, class_ref,
           x_ref, upward_grad_ref, class_grad_ref):
    loss_scale = 8.0 / math.sqrt(49152)
    upward = multiply(coarse_ref[0], up_weight_ref[0:PART, :]) + multiply(
        coarse_ref[1], up_weight_ref[PART:, :]
    )
    upward = upward + jnp.concatenate([inner_ref[0], inner_ref[1]], axis=1)
    joined_pre = stacked_up(upward + stacked_ref[...].astype(jnp.float32))
    joined = jax.nn.silu(joined_pre).astype(jnp.bfloat16)
    logits = contract_last(joined, class_ref[...])
    classes = lax.broadcasted_iota(jnp.int32, logits.shape, 1)
    exp_logits = jnp.exp(logits)
    probability = exp_logits / jnp.sum(exp_logits, axis=1, keepdims=True)
    onehot = (label_column(label_ref[...]) == classes.astype(jnp.float32)).astype(jnp.float32)
    logit_grad = ((probability - onehot) * loss_scale).astype(jnp.bfloat16)
    joined_grad = multiply(logit_grad, class_ref[...])
    upward_grad = side_by_side((joined_grad * silu_slope(joined_pre)).astype(jnp.bfloat16))
    upward_grad_ref[...] = upward_grad
    for half in range(2):
        x_ref[half] = upward_grad[:, half * LANES : (half + 1) * LANES]
    class_grad_ref[...] = contract_first(logit_grad, joined)


def phase_kernel(backward, *refs):
    if backward:
        (
            wa_hbm, wb_hbm, pre_hbm, ef_hbm, xf_hbm, coarse_ref, inner_ref, stacked_ref, label_ref,
            up_weight_ref, class_ref,
            out_ref, ge_ref, upward_grad_ref, class_grad_ref, bottom_grad_ref, joint_ref,
        ) = refs[:17]
        scratch = refs[17:]
    else:
        (
            feature_ref, conv_weight_ref, down_weight_ref, up_weight_ref, expand_hbm, reduce_hbm,
            out_ref, pre_hbm, ef_hbm, xf_hbm, wa_hbm, wb_hbm, expand_tall_hbm, stacked_ref,
            hidden_pre_ref, taps_ref, coarse_ref,
        ) = refs[:17]
        scratch = refs[17:]
    (
        xall, wa, wb, total, pre, other, padded, chunk, window,
        far_out, up_out, down_out, far_in, up_in, down_in, reduced,
        far2_out, up2_out, down2_out, far2_in, up2_in, down2_in, swap_out, swap_in,
        x_ref, send_sems, recv_sems, local_sems,
    ) = scratch[:28]
    core, first, second = place()
    me = block_of(core, first, second)
    partner = me * 2 + 1 - core
    f_up = block_of(core, (first + 1) % 4, second) * 2 + core
    f_down = block_of(core, (first + 3) % 4, second) * 2 + core
    s_up = block_of(core, first, (second + 1) % 4) * 2 + core
    s_down = block_of(core, first, (second + 3) % 4) * 2 + core
    copies = Copies(send_sems, recv_sems)

    if backward:
        loads = [
            pltpu.make_async_copy(wa_hbm, wa, local_sems.at[0]),
            pltpu.make_async_copy(wb_hbm, wb, local_sems.at[1]),
        ]
        pre_f, ef, xf, grad, full, give, zfar_in, zup_out, zdown_out, zup_in, zdown_in, joint = scratch[28:]
        loads += [
            pltpu.make_async_copy(pre_hbm, pre_f, local_sems.at[2]),
            pltpu.make_async_copy(ef_hbm, ef, local_sems.at[3]),
            pltpu.make_async_copy(xf_hbm, xf, local_sems.at[4]),
        ]
    else:
        expand_both, reduce_both, wa_back, wb_back, halo, columns, expand_tall, spread_rows = scratch[28:]
        lanes = pl.ds(pl.multiple_of(core * LANES, LANES), LANES)
        own_rows = pl.ds(pl.multiple_of(core * 64, 64), 64)
        loads = [
            pltpu.make_async_copy(
                expand_hbm, expand_both.at[:, own_rows, :], local_sems.at[0]
            ),
            pltpu.make_async_copy(
                reduce_hbm, reduce_both.at[:, own_rows, :], local_sems.at[1]
            ),
        ]
    for load in loads:
        load.start()

    peers = [{"wide": device} for device in (partner, f_up, f_down, s_up, s_down)]
    if backward:
        depth = lax.axis_index("samp")
        z_up = {"samp": (depth + 1) % 4}
        z_down = {"samp": (depth + 3) % 4}
        peers += [z_up, z_down]
    else:
        wide = lax.axis_index("wide")
        after = {"wide": (wide + 1) % 32}
        before = {"wide": (wide + 31) % 32}
        peers += [after, before]
    barrier = pltpu.get_barrier_semaphore()
    for device in peers:
        pl.semaphore_signal(
            barrier, inc=1, device_id=device, device_id_type=pl.DeviceIdType.MESH
        )
    if backward:
        middle(
            coarse_ref, inner_ref, stacked_ref, label_ref, up_weight_ref, class_ref,
            x_ref, upward_grad_ref, class_grad_ref,
        )
    pl.semaphore_wait(barrier, len(peers))
    if not backward:
        copies.start(56, feature_ref.at[3], halo.at[0], after)
        copies.start(57, feature_ref.at[0], halo.at[1], before)
        copies.start(58, expand_hbm, expand_both.at[:, own_rows, :], partner)
        copies.start(59, reduce_hbm, reduce_both.at[:, own_rows, :], partner)
        first_layers(
            wide, copies, after, before, feature_ref, halo, columns, conv_weight_ref,
            taps_ref, hidden_pre_ref, stacked_ref, x_ref, spread_rows,
        )

    mine = pl.ds(pl.multiple_of(me * PIECE + core * HALF, 32), HALF)
    theirs = pl.ds(pl.multiple_of(me * PIECE + (1 - core) * HALF, 32), HALF)
    copies.start(0, x_ref.at[1 - core], xall.at[mine, :], partner)
    xall[mine, :] = x_ref[core]
    copies.arrived(0, xall.at[theirs, :], partner)

    def piece(first_at, second_at, low=0, length=PIECE):
        block = block_of(core, first_at % 4, second_at % 4)
        return xall.at[pl.ds(pl.multiple_of(block * PIECE + low, 32), length), :]

    def send_second(order, first_at):
        copies.start(5 + order, piece(first_at, second), piece(first_at, second), s_up)
        copies.start(9 + order, piece(first_at, second), piece(first_at, second), s_down)

    own = piece(first, second)
    copies.start(1, own, own, f_up)
    copies.start(2, own, own, f_down)
    send_second(0, first)

    def clear(step, carry):
        total[pl.ds(pl.multiple_of(step * 96, 32), 96), :] = jnp.zeros((96, WIDE_ROWS), jnp.float32)
        return carry

    def clear_grad(step, carry):
        grad[pl.ds(pl.multiple_of(step * INNER, 128), INNER), :] = jnp.zeros((INNER, LANES), jnp.float32)
        return carry

    def add_gradient():
        grad[...] += lax.dot_general(
            window[...], chunk[...], (((0,), (0,)), ((), ())), preferred_element_type=jnp.float32
        )

    def fill_window(source, row):
        for position in range(4):
            block = block_of(core, position, row)
            for p in range(3):
                window[
                    position * PIECE : (position + 1) * PIECE, p * WIDE_ROWS : (p + 1) * WIDE_ROWS
                ] = source[pl.ds(pl.multiple_of(block * PIECE + p * ACROSS, 16), PIECE), :]

    def fill_chunk(source, row):
        for position in range(4):
            block = block_of(core, position, row)
            chunk[position * PIECE : (position + 1) * PIECE, :] = source[rows_of(block), :]

    def hand_over(which):
        def pack(tap, carry):
            to = pl.ds(pl.multiple_of(tap * 64, 64), 64)
            own_rows = pl.ds(pl.multiple_of(tap * INNER + core * 64, 64), 64)
            other_rows = pl.ds(pl.multiple_of(tap * INNER + (1 - core) * 64, 64), 64)
            joint[which, core, to, :] = grad[own_rows, :].astype(jnp.bfloat16)
            give[which, to, :] = grad[other_rows, :].astype(jnp.bfloat16)
            return carry

        lax.fori_loop(0, 9, pack, 0)
        copies.start(38 + which, give.at[which], joint.at[which, core], partner)

    def take_over(which):
        copies.arrived(38 + which, joint.at[which, 1 - core], partner)
        both = jnp.concatenate([joint[which, 0], joint[which, 1]], axis=1)
        joint_ref[which] = both
        return both

    def share(which, at, low, length):
        at = at % 4
        lanes = pl.ds(pl.multiple_of((at % 2) * 256, 256), 256)
        return full.at[which, at // 2, pl.ds(low, length), lanes]

    def depth_far(which):
        both = take_over(which)
        for half in range(2):
            part = slice(half * PART, (half + 1) * PART)
            full[which, half] = narrow(contract_last(both, up_weight_ref[part, :]))
        copies.start(40 + which, share(which, depth + 2, 0, 288), zfar_in.at[which, 0], z_up)
        copies.start(42 + which, share(which, depth + 2, 288, 288), zfar_in.at[which, 1], z_down)

    def depth_near(which):
        near = share(which, depth + 1, 288, 288)[...]
        zup_out[which, 288:576, :] = near
        near = share(which, depth + 3, 0, 288)[...]
        zdown_out[which, 0:288, :] = near
        copies.arrived(40 + which, zfar_in.at[which, 0], z_up)
        near = share(which, depth + 1, 0, 288)[...].astype(jnp.float32)
        zup_out[which, 0:288, :] = narrow(near + zfar_in[which, 0].astype(jnp.float32))
        copies.start(44 + which, zup_out.at[which], zup_in.at[which], z_up)
        copies.arrived(42 + which, zfar_in.at[which, 1], z_down)
        near = share(which, depth + 3, 288, 288)[...].astype(jnp.float32)
        zdown_out[which, 288:576, :] = narrow(near + zfar_in[which, 1].astype(jnp.float32))
        copies.start(46 + which, zdown_out.at[which], zdown_in.at[which], z_down)

    def depth_own(which, out):
        copies.arrived(44 + which, zup_in.at[which], z_up)
        copies.arrived(46 + which, zdown_in.at[which], z_down)
        out[...] = (
            share(which, depth, 0, 576)[...].astype(jnp.float32)
            + zup_in[which].astype(jnp.float32)
            + zdown_in[which].astype(jnp.float32)
        )

    def narrow(values):
        return values.astype(jnp.bfloat16)

    lax.fori_loop(0, 33, clear, 0)
    if backward:
        lax.fori_loop(0, 9, clear_grad, 0)
    padded[0:ACROSS, :] = jnp.zeros((ACROSS, WIDE_ROWS), jnp.bfloat16)
    padded[SPOTS + ACROSS :, :] = jnp.zeros((ACROSS, WIDE_ROWS), jnp.bfloat16)

    offsets = (0, 3, 1, 2)

    def relay(order):
        first_at = first + offsets[order]
        here = piece(first_at, second + 3)
        copies.arrived(5 + order, here, s_up)
        low = piece(first_at, second + 3, 0, HALF)
        copies.start(13 + order, low, low, s_up)
        here = piece(first_at, second + 1)
        copies.arrived(9 + order, here, s_down)
        high = piece(first_at, second + 1, HALF, HALF)
        copies.start(48 + order, high, high, s_down)

    for load in loads:
        load.wait()
    if not backward:
        partner_rows = pl.ds(pl.multiple_of((1 - core) * 64, 64), 64)
        copies.arrived(58, expand_both.at[:, partner_rows, :], partner)
        copies.arrived(59, reduce_both.at[:, partner_rows, :], partner)
        share_rows = down_weight_ref[pl.ds(pl.multiple_of(core * LANES, LANES), LANES), :]
        joined_weight = narrow(
            contract_last(expand_both[...].reshape(9 * INNER, 2 * PART), share_rows)
        )
        for tap in range(9):
            block = joined_weight[tap * INNER : (tap + 1) * INNER, :]
            wa[:, tap * INNER : (tap + 1) * INNER] = block.T
            wb_back[(8 - tap) * INNER : (9 - tap) * INNER, :] = block
            expand_tall[(8 - tap) * 64 : (9 - tap) * 64, :] = expand_both[tap, own_rows, :]

    left = piece(first + 3, second)
    right = piece(first + 1, second)
    copies.arrived(1, left, f_up)
    low = piece(first + 3, second, 0, HALF)
    copies.start(3, low, low, f_up)
    send_second(1, first + 3)
    copies.arrived(2, right, f_down)
    high = piece(first + 1, second, HALF, HALF)
    copies.start(4, high, high, f_down)
    send_second(2, first + 1)
    relay(0)
    copies.arrived(3, piece(first + 2, second, 0, HALF), f_up)
    copies.arrived(4, piece(first + 2, second, HALF, HALF), f_down)
    send_second(3, first + 2)
    if not backward:
        wb[...] = narrow(
            multiply(
                reduce_both[...].reshape(9 * INNER, 2 * PART), up_weight_ref[:, lanes]
            )
        )
        for tap in range(9):
            here = slice(tap * INNER, (tap + 1) * INNER)
            back = slice((8 - tap) * INNER, (9 - tap) * INNER)
            wa_back[:, back] = wb[here, :].T
        for half in range(2):
            coarse_ref[half] = narrow(
                multiply(stacked_ref[...], down_weight_ref[:, half * PART : (half + 1) * PART])
            )
        stores = [
            pltpu.make_async_copy(wa_back, wa_hbm, local_sems.at[0]),
            pltpu.make_async_copy(wb_back, wb_hbm, local_sems.at[1]),
            pltpu.make_async_copy(expand_tall, expand_tall_hbm, local_sems.at[5]),
        ]
        for store in stores:
            store.start()
    else:
        stores = []
        for half in range(2):
            bottom_grad_ref[half] = narrow(
                contract_last(
                    upward_grad_ref[...], up_weight_ref[half * PART : (half + 1) * PART, :]
                )
            )

    def product(step, carry):
        turn = (3 * step + (step // 2) * (7 - 2 * step)) % 4

        @pl.when(step == 1)
        def _():
            for order in (1, 2, 3):
                first_at = first + offsets[order]
                copies.arrived(5 + order, piece(first_at, second + 3), s_up)
                low = piece(first_at, second + 3, 0, HALF)
                copies.remote(13 + order, low, low, s_up).start()
                copies.arrived(9 + order, piece(first_at, second + 1), s_down)
                high = piece(first_at, second + 1, HALF, HALF)
                copies.remote(48 + order, high, high, s_down).start()

        @pl.when(step == 3)
        def _():
            for order in range(4):
                first_at = first + offsets[order]
                copies.arrived(13 + order, piece(first_at, second + 2, 0, HALF), s_up)
                copies.arrived(48 + order, piece(first_at, second + 2, HALF, HALF), s_down)

        row = (second + turn) % 4
        fill_chunk(xall, row)
        result = jnp.dot(chunk[...], wa[...], preferred_element_type=jnp.float32)
        for position in range(4):
            block = block_of(core, position, row)
            for p in range(3):
                where = pl.ds(pl.multiple_of(block * PIECE + (2 - p) * ACROSS, 16), PIECE)
                total[where, :] += result[
                    position * PIECE : (position + 1) * PIECE, p * WIDE_ROWS : (p + 1) * WIDE_ROWS
                ]

        if backward:

            @pl.when(step < 3)
            def _():
                fill_window(ef, row)
                add_gradient()

        return carry

    lax.fori_loop(0, 4, product, 0)
    for order in (1, 2, 3):
        here = piece(first, second, 0, HALF)
        copies.sent.append(copies.remote(13 + order, here, here, s_up))
        copies.sent.append(copies.remote(48 + order, here, here, s_down))

    at_left, at_right = edge_masks(PIECE)

    def fold(step, carry):
        rows = rows_of(step)
        padded_rows = pl.ds(pl.multiple_of(step * PIECE + ACROSS, 16), PIECE)
        pre[rows, :] = (
            total[padded_rows, INNER : 2 * INNER]
            + from_left(total[padded_rows, 0:INNER], at_left)
            + from_right(total[padded_rows, 2 * INNER :], at_right)
        )
        return carry

    for quarter in range(4):
        lax.fori_loop(quarter * 4, quarter * 4 + 4, fold, 0)
        rows = pl.ds(quarter * 768, 768)
        copies.start(17 + quarter, pre.at[rows, :], other.at[rows, :], partner)

    if backward:
        fill_window(ef, (second + 2) % 4)
        add_gradient()
        hand_over(0)
        lax.fori_loop(0, 9, clear_grad, 0)

    def shape(step, carry):
        rows = rows_of(step)
        padded_rows = pl.ds(pl.multiple_of(step * PIECE + ACROSS, 16), PIECE)
        value = pre[rows, :] + other[rows, :]
        if backward:
            value = value * silu_slope(pre_f[rows, :])
        else:
            other[rows, :] = value
            value = jax.nn.silu(value)
        value = value.astype(jnp.bfloat16).astype(jnp.float32)
        padded[padded_rows, 0:INNER] = from_left(value, at_left).astype(jnp.bfloat16)
        padded[padded_rows, INNER : 2 * INNER] = value.astype(jnp.bfloat16)
        padded[padded_rows, 2 * INNER :] = from_right(value, at_right).astype(jnp.bfloat16)
        return carry

    for quarter in range(4):
        copies.arrived(17 + quarter, other.at[pl.ds(quarter * 768, 768), :], partner)
        lax.fori_loop(quarter * 4, quarter * 4 + 4, shape, 0)

    if not backward:
        more = [
            pltpu.make_async_copy(other, pre_hbm, local_sems.at[2]),
            pltpu.make_async_copy(padded, ef_hbm, local_sems.at[3]),
            pltpu.make_async_copy(xall, xf_hbm, local_sems.at[4]),
        ]
        for store in more:
            store.start()
        stores += more

    if backward:
        depth_far(0)

    def place_of(order):
        return (first + (2, 1, 3, 0)[order]) % 4

    def spread(step, carry):
        turn = (2 - step + (step // 2) * (7 - 2 * step)) % 4
        row = (second + turn) % 4
        fill_window(padded, row)
        result = jnp.dot(window[...], wb[...], preferred_element_type=jnp.float32)
        for position in range(4):
            reduced[step, position] = result[position * PIECE : (position + 1) * PIECE, :]

        @pl.when(step == 0)
        def _():
            for order in range(4):
                far_out[order] = narrow(reduced[0, place_of(order)])
                low = pl.ds(0, HALF)
                copies.remote(
                    21 + order, far_out.at[order, low, :], far_in.at[order, low, :], s_up
                ).start()
                high = pl.ds(HALF, HALF)
                copies.remote(
                    33 + order, far_out.at[order, high, :], far_in.at[order, high, :], s_down
                ).start()

        @pl.when(step == 2)
        def _():
            for order in range(4):
                at = place_of(order)
                low = pl.ds(0, HALF)
                high = pl.ds(HALF, HALF)
                up_out[order, high, :] = narrow(reduced[1, at, high, :])
                down_out[order, low, :] = narrow(reduced[2, at, low, :])
                copies.arrived(21 + order, far_in.at[order, low, :], s_up)
                up_out[order, low, :] = narrow(
                    reduced[1, at, low, :] + far_in[order, low, :].astype(jnp.float32)
                )
                copies.remote(25 + order, up_out.at[order], up_in.at[order], s_up).start()
                copies.arrived(33 + order, far_in.at[order, high, :], s_down)
                down_out[order, high, :] = narrow(
                    reduced[2, at, high, :] + far_in[order, high, :].astype(jnp.float32)
                )
                copies.remote(29 + order, down_out.at[order], down_in.at[order], s_down).start()

        if backward:

            @pl.when(step >= 2)
            def _():
                fill_chunk(xf, row)
                add_gradient()

            @pl.when(step == 3)
            def _():
                for turn in (2, 1):
                    fill_window(padded, (second + turn) % 4)
                    fill_chunk(xf, (second + turn) % 4)
                    add_gradient()

        return carry

    lax.fori_loop(0, 4, spread, 0)
    for order in range(4):
        low = pl.ds(0, HALF)
        half = far_out.at[order, low, :]
        copies.sent.append(copies.remote(21 + order, half, half, s_up))
        copies.sent.append(copies.remote(33 + order, half, half, s_down))
        copies.sent.append(copies.remote(25 + order, up_out.at[order], up_in.at[order], s_up))
        copies.sent.append(copies.remote(29 + order, down_out.at[order], down_in.at[order], s_down))
    if backward:
        hand_over(1)
        depth_near(0)

    def arrive_second(order):
        copies.arrived(25 + order, up_in.at[order], s_up)
        copies.arrived(29 + order, down_in.at[order], s_down)

    def gathered(order, low, length):
        rows = pl.ds(low, length)
        return (
            reduced[3, place_of(order), rows, :]
            + up_in[order, rows, :].astype(jnp.float32)
            + down_in[order, rows, :].astype(jnp.float32)
        )

    arrive_second(0)
    far2_out[0] = narrow(gathered(0, 0, HALF))
    copies.start(52, far2_out.at[0], far2_in.at[0], f_up)
    far2_out[1] = narrow(gathered(0, HALF, HALF))
    copies.start(53, far2_out.at[1], far2_in.at[1], f_down)
    arrive_second(1)
    up2_out[HALF:, :] = narrow(gathered(1, HALF, HALF))
    copies.arrived(52, far2_in.at[0], f_up)
    up2_out[:HALF, :] = narrow(gathered(1, 0, HALF) + far2_in[0].astype(jnp.float32))
    copies.start(54, up2_out, up2_in, f_up)
    arrive_second(2)
    down2_out[:HALF, :] = narrow(gathered(2, 0, HALF))
    copies.arrived(53, far2_in.at[1], f_down)
    down2_out[HALF:, :] = narrow(gathered(2, HALF, HALF) + far2_in[1].astype(jnp.float32))
    copies.start(55, down2_out, down2_in, f_down)
    if backward:
        take_over(1)
    arrive_second(3)
    copies.arrived(54, up2_in, f_up)
    copies.arrived(55, down2_in, f_down)

    def settled(which):
        rows = pl.ds(pl.multiple_of(which * HALF, 32), HALF)
        return (
            reduced[3, first, rows, :]
            + up_in[3, rows, :].astype(jnp.float32)
            + down_in[3, rows, :].astype(jnp.float32)
            + up2_in[rows, :].astype(jnp.float32)
            + down2_in[rows, :].astype(jnp.float32)
        )

    swap_out[...] = narrow(settled(1 - core))
    copies.start(37, swap_out, swap_in, partner)
    out_ref[core] = settled(core)
    copies.arrived(37, swap_in, partner)
    out_ref[1 - core] = swap_in[...].astype(jnp.float32)
    if backward:
        depth_own(0, ge_ref)
    copies.finish()
    for store in stores:
        store.wait()


def bottleneck(backward, *operands):
    b16, f32 = jnp.bfloat16, jnp.float32
    vmem = pl.BlockSpec(memory_space=pltpu.VMEM)
    anywhere = pl.BlockSpec(memory_space=pl.ANY)
    padded_rows = SPOTS + 2 * ACROSS
    shape = jax.ShapeDtypeStruct
    out = shape((2, HALF, LANES), f32)
    pair = shape((2, HALF, PART), b16)
    if backward:
        grad = shape((9 * INNER // 2, PART // 2), f32)
        in_specs = [anywhere] * 5 + [vmem] * 6
        out_shape = [
            out, grad, shape((HALF, PART), b16), shape((9, INNER), f32), pair,
            shape((2, 9 * INNER // 2, PART), b16),
        ]
        out_specs = [vmem] * 6
    else:
        in_specs = [vmem] * 4 + [anywhere] * 2
        out_shape = [
            out,
            shape((SPOTS, INNER), f32),
            shape((padded_rows, WIDE_ROWS), b16),
            shape((SPOTS, LANES), b16),
            shape((LANES, 9 * INNER), b16),
            shape((9 * INNER, LANES), b16),
            shape((9 * INNER // 2, 2 * PART), b16),
            shape((HALF, PART), b16),
            shape((HALF, PART), f32),
            shape((4 * HALF, 9 * INNER), b16),
            pair,
        ]
        out_specs = [vmem] + [anywhere] * 6 + [vmem] * 4
    scratch = [
        pltpu.VMEM((SPOTS, LANES), b16),
        pltpu.VMEM((LANES, 9 * INNER), b16),
        pltpu.VMEM((9 * INNER, LANES), b16),
        pltpu.VMEM((padded_rows, WIDE_ROWS), f32),
        pltpu.VMEM((SPOTS, INNER), f32),
        pltpu.VMEM((SPOTS, INNER), f32),
        pltpu.VMEM((padded_rows, WIDE_ROWS), b16),
        pltpu.VMEM((4 * PIECE, LANES), b16),
        pltpu.VMEM((4 * PIECE, 9 * INNER), b16),
        *[pltpu.VMEM((4, PIECE, LANES), b16) for _ in range(6)],
        pltpu.VMEM((4, 4, PIECE, LANES), f32),
        pltpu.VMEM((2, HALF, LANES), b16),
        pltpu.VMEM((PIECE, LANES), b16),
        pltpu.VMEM((PIECE, LANES), b16),
        pltpu.VMEM((2, HALF, LANES), b16),
        pltpu.VMEM((PIECE, LANES), b16),
        pltpu.VMEM((PIECE, LANES), b16),
        pltpu.VMEM((HALF, LANES), b16),
        pltpu.VMEM((HALF, LANES), b16),
        pltpu.VMEM((2, HALF, LANES), b16),
        pltpu.SemaphoreType.DMA((60,)),
        pltpu.SemaphoreType.DMA((60,)),
        pltpu.SemaphoreType.DMA((6,)),
    ]
    if backward:
        scratch += [
            pltpu.VMEM((SPOTS, INNER), f32),
            pltpu.VMEM((padded_rows, WIDE_ROWS), b16),
            pltpu.VMEM((SPOTS, LANES), b16),
            pltpu.VMEM((9 * INNER, LANES), f32),
            pltpu.VMEM((2, 2, 576, PART), b16),
            pltpu.VMEM((2, 576, LANES), b16),
            pltpu.VMEM((2, 2, 288, 256), b16),
            *[pltpu.VMEM((2, 576, 256), b16) for _ in range(4)],
            pltpu.VMEM((2, 2, 576, LANES), b16),
        ]
    else:
        scratch += [
            pltpu.VMEM((9, INNER, 2 * PART), b16),
            pltpu.VMEM((9, INNER, 2 * PART), b16),
            pltpu.VMEM((LANES, 9 * INNER), b16),
            pltpu.VMEM((9 * INNER, LANES), b16),
            pltpu.VMEM((2, 2 * ACROSS, INNER), b16),
            pltpu.VMEM((4, 6 * ACROSS, INNER), b16),
            pltpu.VMEM((9 * INNER // 2, 2 * PART), b16),
            pltpu.VMEM((12 * ACROSS, INNER), f32),
        ]
    return pl.pallas_call(
        functools.partial(phase_kernel, backward),
        out_shape=out_shape,
        in_specs=in_specs,
        out_specs=out_specs,
        scratch_shapes=scratch,
        compiler_params=pltpu.CompilerParams(
            collective_id=2 if backward else 1,
            has_side_effects=True,
            vmem_limit_bytes=60 * 1024 * 1024,
        ),
        name="backward_phase" if backward else "forward_phase",
    )(*operands)


SUM_ROWS = 1280


def sum_kernel(stacked_ref, coarse_ref, upward_grad_ref, bottom_grad_ref, inner_ref, joint_ref,
               reduce_ref, expand_ref, down_weight_ref, hidden_pre_ref, taps_ref, class_ref, down_out, up_out, conv_out, class_out, expand_out, total, give, pair_in, a_out, a_in,
               b_out, b_in, z_out, z_in, result, conv_ref, full, zfar_in, zup_out, zdown_out,
               zup_in, zdown_in, send_sems, recv_sems):
    core, first, second = place()
    depth = lax.axis_index("samp")
    me = block_of(core, first, second)
    partner = {"wide": me * 2 + 1 - core}
    first_peers = [
        {"wide": block_of(core, (first + d) % 4, second) * 2 + core} for d in range(4)
    ]
    second_peers = [
        {"wide": block_of(core, first, (second + d) % 4) * 2 + core} for d in range(4)
    ]
    depth_peers = [{"samp": (depth + d) % 4} for d in range(4)]
    copies = Copies(send_sems, recv_sems)
    barrier = pltpu.get_barrier_semaphore()
    for device in [partner, *first_peers[1:], *second_peers[1:], *depth_peers[1:]]:
        pl.semaphore_signal(
            barrier, inc=1, device_id=device, device_id_type=pl.DeviceIdType.MESH
        )

    def own_lanes(half, width):
        return pl.ds(pl.multiple_of(half * width, 128), width)

    down_back = contract_last(bottom_grad_ref[0], down_weight_ref[:, 0:PART]) + contract_last(
        bottom_grad_ref[1], down_weight_ref[:, PART:]
    )
    down_back = down_back + jnp.concatenate([inner_ref[0], inner_ref[1]], axis=1)
    hidden_grad = (down_back + upward_grad_ref[...].astype(jnp.float32)) * silu_slope(
        hidden_pre_ref[...]
    )
    conv_ref[...] = contract_first(taps_ref[...], stacked_up(hidden_grad.astype(jnp.bfloat16)))

    def pack(half, to, kind):
        lanes = own_lanes(half, PART)
        to[0:512, :] = (
            contract_first(stacked_ref[...], bottom_grad_ref[half])
            + contract_first(joint_ref[1], expand_ref[:, lanes])
        ).astype(kind)
        to[512:1024, :] = (
            contract_first(coarse_ref[half], upward_grad_ref[...])
            + contract_first(reduce_ref[:, lanes], joint_ref[0])
        ).astype(kind)
        to[1168:1184, :] = jnp.zeros((16, PART), kind)
        to[1168:1177, 0:INNER] = class_ref[...].astype(kind)
        for piece in range(4):
            rows = pl.ds(pl.multiple_of((half * 4 + piece) * 144, 16), 144)
            to[1024:1168, piece * 128 : (piece + 1) * 128] = conv_ref[rows, :].astype(kind)
        to[1184:, :] = jnp.zeros((SUM_ROWS - 1184, PART), kind)

    def spot(at_first, at_second):
        base = (at_first % 4) * 320 + (at_second % 4) * 80
        return pl.ds(pl.multiple_of(base, 16), 80)

    order = (2, 1, 3, 0)
    pack(1 - core, give, jnp.bfloat16)
    pl.semaphore_wait(barrier, 10)
    for i, ds in enumerate(order):
        for df in (2, 1, 3, 0):
            part = spot(second + df, first + ds)
            copies.start(i * 4 + df, give.at[part, :], pair_in.at[part, :], partner)
    pack(core, total, jnp.float32)
    for i, ds in enumerate(order):
        for df in (2, 1, 3):
            part = spot(first + df, second + ds)
            copies.arrived(i * 4 + df, pair_in.at[part, :], partner)
            a_out[df, i] = (total[part, :] + pair_in[part, :].astype(jnp.float32)).astype(
                jnp.bfloat16
            )
            copies.start(16 + i * 3 + df - 1, a_out.at[df, i], a_in.at[df, i], first_peers[df])

    z_up, z_down = depth_peers[1], depth_peers[3]

    def share(at, low, length):
        at = at % 4
        return full.at[at // 2, pl.ds(low, length), own_lanes(at % 2, 256)]

    def plus(left, right):
        return left.astype(jnp.float32) + right.astype(jnp.float32)

    for half in range(2):
        part = slice(half * PART, (half + 1) * PART)
        full[half] = multiply(joint_ref[1], down_weight_ref[:, part]).astype(jnp.bfloat16)
    copies.start(68, share(depth + 2, 0, 288), zfar_in.at[0], z_up)
    copies.start(69, share(depth + 2, 288, 288), zfar_in.at[1], z_down)

    def after_first(i):
        part = spot(first, second + order[i])
        copies.arrived(i * 4, pair_in.at[part, :], partner)
        value = total[part, :] + pair_in[part, :].astype(jnp.float32)
        for df in range(1, 4):
            copies.arrived(16 + i * 3 + df - 1, a_in.at[df, i], first_peers[df])
            value = value + a_in[df, i].astype(jnp.float32)
        return value

    for i in range(3):
        b_out[i] = after_first(i).astype(jnp.bfloat16)
        copies.start(28 + i, b_out.at[i], b_in.at[i], second_peers[order[i]])
    total[0:80, :] = after_first(3)
    zup_out[288:576, :] = share(depth + 1, 288, 288)[...]
    zdown_out[0:288, :] = share(depth + 3, 0, 288)[...]
    copies.arrived(68, zfar_in.at[0], z_up)
    zup_out[0:288, :] = plus(share(depth + 1, 0, 288)[...], zfar_in[0]).astype(jnp.bfloat16)
    copies.arrived(69, zfar_in.at[1], z_down)
    zdown_out[288:576, :] = plus(share(depth + 3, 288, 288)[...], zfar_in[1]).astype(jnp.bfloat16)
    for i in range(3):
        copies.arrived(28 + i, b_in.at[i], second_peers[order[i]])
        total[0:80, :] += b_in[i].astype(jnp.float32)
    for d in range(1, 4):
        z_out[d] = total[0:80, own_lanes((depth + d) % 4, 128)].astype(jnp.bfloat16)
        copies.start(30 + d, z_out.at[d], z_in.at[d], depth_peers[d])
    value = total[0:80, own_lanes(depth, 128)]
    for d in range(1, 4):
        copies.arrived(30 + d, z_in.at[d], depth_peers[d])
        value = value + z_in[d].astype(jnp.float32)

    def at_depth(d):
        return result.at[core, spot(first, second), own_lanes((depth + d) % 4, 128)]

    def at(df, ds, half):
        return result.at[half, spot(first + df, second + ds), :]

    def pass_on(df, ds):
        copies.start(52 + df * 4 + ds, at(df, ds, core), at(df, ds, core), partner)

    def along_first(ds):
        for df in (2, 1, 3):
            copies.start(40 + ds * 3 + df - 1, at(0, ds, core), at(0, ds, core), first_peers[df])

    at_depth(0)[...] = value.astype(jnp.bfloat16)
    for d in range(1, 4):
        copies.start(33 + d, at_depth(0), at_depth(0), depth_peers[d])
    for d in range(1, 4):
        copies.arrived(33 + d, at_depth(4 - d), depth_peers[d])
    copies.start(70, zup_out, zup_in, z_up)
    copies.start(71, zdown_out, zdown_in, z_down)
    for ds in range(1, 4):
        copies.start(36 + ds, at(0, 0, core), at(0, 0, core), second_peers[ds])
    along_first(0)
    pass_on(0, 0)
    for ds in (1, 3, 2):
        copies.arrived(36 + ds, at(0, 4 - ds, core), second_peers[ds])
        along_first(4 - ds)
        pass_on(0, 4 - ds)
    for ds in (0, 3, 1, 2):
        for df in (1, 3, 2):
            copies.arrived(40 + ds * 3 + df - 1, at(4 - df, ds, core), first_peers[df])
            pass_on(4 - df, ds)
    copies.arrived(70, zup_in, z_up)
    copies.arrived(71, zdown_in, z_down)
    expand_out[...] = plus(share(depth, 0, 576)[...], zup_in[...]) + zdown_in[...].astype(
        jnp.float32
    )

    def unpack(half):
        down_out[:, own_lanes(half, PART)] = result[half, 0:512, :]
        up_out[pl.ds(pl.multiple_of(half * PART, PART), PART), :] = result[half, 512:1024, :]
        for piece in range(4):
            rows = pl.ds(pl.multiple_of((half * 4 + piece) * 144, 16), 144)
            conv_out[rows, :] = result[half, 1024:1168, piece * 128 : (piece + 1) * 128]

    unpack(core)
    for df in range(4):
        for ds in range(4):
            copies.arrived(52 + df * 4 + ds, at(df, ds, 1 - core), partner)
    unpack(1 - core)
    class_out[...] = result[0, 1168:1184, 0:INNER].astype(jnp.float32)[0:9, :]
    copies.finish()


def sum_everywhere(*operands):
    b16, f32 = jnp.bfloat16, jnp.float32
    vmem = pl.BlockSpec(memory_space=pltpu.VMEM)
    down, up, conv, small, expand = pl.pallas_call(
        sum_kernel,
        out_shape=[
            jax.ShapeDtypeStruct((PART, 2 * PART), b16),
            jax.ShapeDtypeStruct((2 * PART, PART), b16),
            jax.ShapeDtypeStruct((9 * INNER, INNER), b16),
            jax.ShapeDtypeStruct((9, INNER), f32),
            jax.ShapeDtypeStruct((9 * INNER // 2, PART // 2), f32),
        ],
        in_specs=[vmem] * 12,
        out_specs=[vmem] * 5,
        scratch_shapes=[
            pltpu.VMEM((SUM_ROWS, PART), f32),
            pltpu.VMEM((SUM_ROWS, PART), b16),
            pltpu.VMEM((SUM_ROWS, PART), b16),
            pltpu.VMEM((4, 4, 80, PART), b16),
            pltpu.VMEM((4, 4, 80, PART), b16),
            pltpu.VMEM((3, 80, PART), b16),
            pltpu.VMEM((3, 80, PART), b16),
            pltpu.VMEM((4, 80, 128), b16),
            pltpu.VMEM((4, 80, 128), b16),
            pltpu.VMEM((2, SUM_ROWS, PART), b16),
            pltpu.VMEM((9 * INNER, INNER), f32),
            pltpu.VMEM((2, 576, PART), b16),
            pltpu.VMEM((2, 288, 256), b16),
            *[pltpu.VMEM((576, 256), b16) for _ in range(4)],
            pltpu.SemaphoreType.DMA((72,)),
            pltpu.SemaphoreType.DMA((72,)),
        ],
        compiler_params=pltpu.CompilerParams(
            collective_id=3, has_side_effects=True, vmem_limit_bytes=60 * 1024 * 1024
        ),
        name="sum_everywhere",
    )(*operands)
    conv = conv.astype(f32).reshape(3, 3, INNER, INNER)
    return conv, down.astype(f32), up.astype(f32), small.T, expand


def local(
    features,
    labels,
    conv_weight,
    down_weight,
    expand_weight,
    reduce_weight,
    up_weight,
    class_weight,
):
    expand = jnp.transpose(expand_weight, (0, 1, 3, 2)).reshape(9, INNER // 2, 2 * PART)
    reduce = reduce_weight.reshape(9, INNER // 2, 2 * PART)
    (
        inner, pre, expanded, gathered, wa_back, wb_back, expand_tall, stacked, hidden_pre, taps,
        coarse,
    ) = bottleneck(
        False, features[0], conv_weight.reshape(9 * INNER, INNER), down_weight, up_weight, expand,
        reduce,
    )
    inner_back, reduce_grad, upward_grad, class_grad, bottom_grad, joint = bottleneck(
        True, wa_back, wb_back, pre, expanded, gathered, coarse, inner, stacked, labels[0], up_weight,
        class_weight.T,
    )
    conv_grad, down_grad, up_grad, class_grad, expand_grad = sum_everywhere(
        stacked, coarse, upward_grad, bottom_grad, inner_back, joint,
        reduce.reshape(9 * INNER // 2, 2 * PART), expand_tall, down_weight, hidden_pre, taps,
        class_grad,
    )
    reduce_grad = reduce_grad.reshape(3, 3, INNER // 2, -1)
    expand_grad = jnp.transpose(expand_grad.reshape(9, INNER // 2, -1)[::-1], (0, 2, 1))
    expand_grad = expand_grad.reshape(3, 3, -1, INNER // 2)
    return (conv_grad, down_grad, expand_grad, reduce_grad, up_grad, class_grad)


def solution(mesh):
    return jax.shard_map(
        local,
        mesh=mesh,
        in_specs=(
            P("samp", "wide", None, None),
            P("samp", "wide", None),
            P(),
            P(),
            P(None, None, None, "wide"),
            P(None, None, "wide", None),
            P(),
            P(),
        ),
        out_specs=(
            P(),
            P(),
            P(None, None, "samp", "wide"),
            P(None, None, "wide", "samp"),
            P(),
            P(),
        ),
        check_vma=False,
    )
```
